32 devices in a mesh: section: 2 (over y), wide: 16 (over z, x, core).
Axes of the slice: x: 2, y: 2, z: 4, core: 2. Of those that a mesh axis runs over, the one named last changes fastest.
Arguments:
- features: bfloat16 [32, 512, 256], P('wide')
- masked: int32 [32, 512], P('wide'), may hold values 0 or 1
- valid: int32 [32, 512], P('wide'), may hold values from 0 to 1, as said below
- kinds: int32 [32], P('wide'), may hold values from 0 to 1, as said below
- embed_weight: bfloat16 [2, 256, 768], replicated, may hold values from -0.375 to 0.375
- embed_vectors: float32 [3, 768], replicated, may hold values from -3 to 3
- pos_embed: float32 [512, 768], replicated, may hold values from -3 to 3
- norm_gains: float32 [2, 2, 768], P('section'), may hold values from 0.5 to 1.5
- vectors: float32 [2, 6, 768], P('section'), may hold values from -2 to 2
- qkv_weight: bfloat16 [2, 768, 2304], P('section'), may hold values from -0.21875 to 0.21875
- out_weight: bfloat16 [2, 768, 768], P('section'), may hold values from -1.75 to 1.75
- up_weight: bfloat16 [2, 768, 3072], P('section'), may hold values from -0.21875 to 0.21875
- up_bias: float32 [2, 3072], P('section'), may hold values from -2 to 2
- down_weight: bfloat16 [2, 3072, 768], P('section'), may hold values from -0.109375 to 0.109375
- cotangent: bfloat16 [32, 512, 768], P('wide'), may hold values from -6 to 6
Outputs:
- output: bfloat16 [32, 512, 768], P('wide', None, 'section')
- feature_grad: bfloat16 [32, 512, 256], P('wide', None, 'section')
- embed_weight_grad: float32 [2, 256, 768], replicated
- embed_vectors_grad: float32 [3, 768], replicated
- pos_grad: float32 [512, 768], replicated
- norm_gains_grad: float32 [2, 2, 768], P('section')
- vectors_grad: float32 [2, 6, 768], P('section')
- qkv_grad: float32 [2, 768, 2304], P('section')
- out_grad: float32 [2, 768, 768], P('section')
- up_grad: float32 [2, 768, 3072], P('section')
- up_bias_grad: float32 [2, 3072], P('section')
- down_grad: float32 [2, 3072, 768], P('section')
- rms: float32 [2, 3], P('section')
The draws below stay inside these ranges and needn't reach their ends.
Inputs may be any that keep to these rules, and one draw needn't show every extreme that they name: In each clip the valid tokens are its first ones, at least 256 of them and never all. `kinds`: exactly half of the clips are of each kind.
All inputs are finite; a program needn't handle non-finite values. No bound on the sum of `masked` on one device may be relied on, other than what follows from the above.
Results may differ from the reference program's by a relative error of at most 0.015.
Values may be sent and summed in bfloat16 or wider, within the bound.
A program may use at most 320 MiB of HBM per device.

```python
import jax
import jax.numpy as jnp
from jax import lax

D = 768
H = 12
HD = 64
FF = 3072
FEAT = 256
LEN = 512
CLIPS = 32


def draw_features(key, part):
    key = jax.random.fold_in(key, 11)
    keys = jax.random.split(key, 3)
    ladder = jnp.arange(CLIPS, dtype=jnp.float32) / max(CLIPS - 1, 1)
    base = jax.random.normal(keys[0], (CLIPS, LEN, FEAT), jnp.float32)
    ladder = jnp.exp(ladder * jnp.log(3.0))
    row_scale = jnp.exp(jax.random.uniform(keys[1], (CLIPS, LEN, 1), jnp.float32, -1.05, 1.05))
    column_scale = jnp.exp(jax.random.uniform(keys[2], (1, 1, FEAT), jnp.float32, -0.7, 0.7))
    values = base * ladder[:, None, None] * row_scale * column_scale
    return values.astype(jnp.bfloat16)


def draw_valid(key, part):
    key = jax.random.fold_in(key, 12)
    lengths = jax.random.randint(key, (CLIPS, 1), LEN // 2, LEN)
    return (jnp.arange(LEN, dtype=jnp.int32)[None, :] < lengths).astype(jnp.int32)


def draw_kinds(key, part):
    key = jax.random.fold_in(key, 13)
    return (jax.random.permutation(key, CLIPS) % 2).astype(jnp.int32)


def touch_ends(entries, key, low, largest):
    spot = [jax.random.randint(jax.random.fold_in(key, axis), (), 0, length) for axis, length in enumerate(entries.shape)]
    main_axis = entries.shape.index(max(entries.shape))
    beside = spot[:main_axis] + [(spot[main_axis] + 1) % entries.shape[main_axis]] + spot[main_axis + 1:]
    return entries.at[tuple(spot)].set(low).at[tuple(beside)].set(largest)


def shard_levels(stream_key, dims, pieces, smallest, largest):
    loudness, own = 1.0, jax.random.fold_in(stream_key, 6)
    for axis_at, blocks in pieces:
        steps = jnp.exp(jax.random.uniform(jax.random.fold_in(own, axis_at), (blocks,), jnp.float32, smallest / len(pieces), largest / len(pieces)))
        loudness = loudness * jnp.repeat(steps, dims[axis_at] // blocks).reshape([-1 if axis == axis_at else 1 for axis in range(len(dims))])
    return loudness


def centred(stream_key, shape, deviation, most, cuts=(), kind=jnp.bfloat16):
    array = deviation * jax.random.normal(stream_key, shape, jnp.float32)
    if cuts:
        array = array * shard_levels(stream_key, shape, cuts, -0.22, 0.18)
    return jnp.clip(array, -most, most).astype(kind)


def setup_inputs(seed: int = 0) -> dict:
    arg_keys = jax.random.split(jax.random.key(seed), 16)
    return {
        "features": draw_features(jax.random.fold_in(arg_keys[15], 71), 0),
        "masked": touch_ends((jax.random.randint(arg_keys[1], (CLIPS, LEN), 0, 4) < 1).astype(jnp.int32), jax.random.fold_in(arg_keys[1], 1), 0, 1),
        "valid": draw_valid(jax.random.fold_in(arg_keys[15], 71), 0),
        "kinds": draw_kinds(jax.random.fold_in(arg_keys[15], 71), 0),
        "embed_weight": centred(arg_keys[4], (2, FEAT, D), FEAT ** -0.5, 0.375),
        "embed_vectors": centred(arg_keys[5], (3, D), 0.5, 3.0, (), jnp.float32),
        "pos_embed": centred(arg_keys[6], (LEN, D), 0.5, 3.0, (), jnp.float32),
        "norm_gains": jnp.clip(1.0 + 0.1 * jax.random.normal(arg_keys[7], (2, 2, D), jnp.float32), 0.5, 1.5),
        "vectors": centred(arg_keys[8], (2, 6, D), 0.3, 2.0, ((0, 2),), jnp.float32),
        "qkv_weight": centred(arg_keys[9], (2, D, 3 * D), D ** -0.5, 0.21875, ((0, 2),)),
        "out_weight": centred(arg_keys[10], (2, D, D), (D * 8 // LEN) ** -0.5, 1.75, ((0, 2),)),
        "up_weight": centred(arg_keys[11], (2, D, FF), D ** -0.5, 0.21875, ((0, 2),)),
        "up_bias": centred(arg_keys[12], (2, FF), 0.3, 2.0, ((0, 2),), jnp.float32),
        "down_weight": centred(arg_keys[13], (2, FF, D), FF ** -0.5, 0.109375, ((0, 2),)),
        "cotangent": centred(arg_keys[14], (CLIPS, LEN, D), 1.0, 6.0, ((0, 16),)),
    }


@jax.custom_vjp
def low(v):
    return lax.optimization_barrier(v.astype(jnp.bfloat16)).astype(jnp.float32)

@jax.custom_vjp
def low_back(v):
    return v

def low_keep(v):
    return (low(v), None)

def low_pass(kept, grad):
    return (grad,)

def back_keep(v):
    return (v, None)

def back_low(kept, grad):
    return (low(grad),)
low.defvjp(low_keep, low_pass)
low_back.defvjp(back_keep, back_low)
EPS = 1e-06
NEG = -1000000000.0
HIGH = lax.Precision.HIGHEST
GROUP_CLIPS = 4

def layer_norm(values, gain, shift):
    center = lax.optimization_barrier(jnp.mean(values, axis=-1, keepdims=True))
    offset = values - center
    spread = lax.optimization_barrier(jnp.mean(offset * offset, axis=-1, keepdims=True))
    return offset * lax.rsqrt(spread + EPS) * gain + shift

def matmul_rows(left, right):
    return jnp.einsum('gtd,de->gte', left, right, precision=HIGH)

@jax.checkpoint
def attend(queries, keys_in, values_in, live_keys):
    scores = low_back(jnp.einsum('gqhe,gkhe->ghqk', queries, keys_in, precision=HIGH) * HD ** (-0.5))
    scores = jnp.where(live_keys[:, None, None, :] > 0, scores, NEG)
    row_top = lax.optimization_barrier(jnp.max(scores, axis=-1, keepdims=True))
    exp_scores = jnp.exp(scores - row_top)
    soft_low = low(exp_scores / lax.optimization_barrier(jnp.sum(exp_scores, axis=-1, keepdims=True)))
    return jnp.einsum('ghqk,gkhe->gqhe', soft_low, values_in, precision=HIGH)

def encoder_layer(layer_in, live_keys, gain_rows, vector_rows, attend_weight, project_weight, up_matrix, up_offset, down_matrix):
    groups, length, model_width = layer_in.shape
    normed = low(layer_norm(layer_in, gain_rows[0], vector_rows[0]))
    in_offset = jnp.concatenate([vector_rows[1], jnp.zeros((model_width,), jnp.float32), vector_rows[2]])
    packed = low(low_back(matmul_rows(normed, attend_weight) + in_offset))
    packed = packed.reshape(groups, length, 3, H, HD)
    context = attend(packed[:, :, 0], packed[:, :, 1], packed[:, :, 2], live_keys)
    context = low(low_back(context.reshape(groups, length, model_width)))
    branch = low_back(matmul_rows(context, project_weight) + vector_rows[3])
    middle = layer_in + branch
    hidden_in = low(layer_norm(middle, gain_rows[1], vector_rows[4]))
    hidden = low_back(matmul_rows(hidden_in, up_matrix) + up_offset)
    active = low(jax.nn.gelu(hidden, approximate=False))
    mixer = low_back(matmul_rows(active, down_matrix) + vector_rows[5])
    return (middle + mixer, branch, mixer)

def forward_group(feature_rows, embed_weight, embed_vectors, pos_embed, norm_gains, vectors, qkv_weight, out_weight, up_weight, up_bias, down_weight, mask_rows, live_keys, kind_rows):
    kind_onehot = (kind_rows[:, None] == jnp.arange(2, dtype=jnp.int32)[None, :]).astype(jnp.float32)
    chosen = jnp.einsum('gk,kfd->gfd', kind_onehot, embed_weight, precision=HIGH)
    kind_offset = jnp.dot(kind_onehot, embed_vectors[:2], precision=HIGH)
    lifted = jnp.einsum('gtf,gfd->gtd', feature_rows, chosen, precision=HIGH) + kind_offset[:, None, :]
    start = low_back(jnp.where(mask_rows[:, :, None] > 0, embed_vectors[2], lifted) + pos_embed)
    first_out, first_branch, first_mixer = encoder_layer(start, live_keys, norm_gains[0], vectors[0], qkv_weight[0], out_weight[0], up_weight[0], up_bias[0], down_weight[0])
    second_in = low(low_back(first_out))
    second_out, second_branch, second_mixer = encoder_layer(second_in, live_keys, norm_gains[1], vectors[1], qkv_weight[1], out_weight[1], up_weight[1], up_bias[1], down_weight[1])
    token_flags = live_keys[:, :, None]
    square_sums = jnp.stack([jnp.stack([jnp.sum(token_flags * first_out * first_out), jnp.sum(token_flags * first_branch * first_branch), jnp.sum(token_flags * first_mixer * first_mixer)]), jnp.stack([jnp.sum(token_flags * second_out * second_out), jnp.sum(token_flags * second_branch * second_branch), jnp.sum(token_flags * second_mixer * second_mixer)])])
    return (second_out, square_sums)

def reference(features, masked, valid, kinds, embed_weight, embed_vectors, pos_embed, norm_gains, vectors, qkv_weight, out_weight, up_weight, up_bias, down_weight, cotangent):
    params = tuple((item.astype(jnp.float32) for item in (embed_weight, embed_vectors, pos_embed, norm_gains, vectors, qkv_weight, out_weight, up_weight, up_bias, down_weight)))
    group_total = CLIPS // GROUP_CLIPS

    def split_groups(source):
        return source.reshape((group_total, GROUP_CLIPS) + source.shape[1:])
    group_inputs = (split_groups(features), split_groups(masked), split_groups(valid), split_groups(kinds), split_groups(cotangent))

    def group_step(group_carry, group_item):
        totals, square_sums, valid_count = group_carry
        feature_rows, mask_rows, valid_rows, kind_rows, cot_rows = group_item
        live_keys = valid_rows.astype(jnp.float32)

        def forward_fn(feature_in, *weights):
            return forward_group(feature_in, *weights, mask_rows, live_keys, kind_rows)
        group_out, pullback, part_sums = jax.vjp(forward_fn, feature_rows.astype(jnp.float32), *params, has_aux=True)
        group_grads = pullback(cot_rows.astype(jnp.float32))
        totals = tuple((total + grad for total, grad in zip(totals, group_grads[1:])))
        new_carry = (totals, square_sums + part_sums, valid_count + jnp.sum(live_keys))
        return (new_carry, (group_out.astype(jnp.bfloat16), group_grads[0].astype(jnp.bfloat16)))
    start_carry = (tuple((jnp.zeros_like(item) for item in params)), jnp.zeros((2, 3), jnp.float32), jnp.zeros((), jnp.float32))
    final_carry, stacked = lax.scan(group_step, start_carry, group_inputs)
    totals, square_sums, valid_count = final_carry
    output = stacked[0].reshape(CLIPS, LEN, D)
    feature_grad = stacked[1].reshape(CLIPS, LEN, FEAT)
    rms = jnp.sqrt(square_sums / (valid_count * D))
    return (output, feature_grad, totals[0], totals[1], totals[2], totals[3], totals[4], totals[5], totals[6], totals[7], totals[8], totals[9], rms)
```

```python
import functools

import jax
import jax.numpy as jnp
from jax import lax
from jax.experimental import pallas as pl
from jax.experimental.pallas import tpu as pltpu
from jax.sharding import PartitionSpec as P

H = 12
HD = 64
MB = 2


EPS = 1e-06
NEG = -1000000000.0


MESH = pl.DeviceIdType.MESH
SMALL = 16


def ring_kernel(n, rows, tail, g_ref, o_ref, e_ref, own, part, ring, sems):
    (own_sem, part_send, part_recv, ring_send, ring_recv, gather_send, gather_recv,
     pair_send, pair_recv, keep_sem, cross_send, cross_recv) = sems
    columns = g_ref.shape[2] // 2
    me = lax.axis_index("wide")
    section = lax.axis_index("section")
    chip, core = me // 2, me % 2
    place = jnp.where(chip % 2 == 0, chip // 2, n - 1 - chip // 2)

    def member(position):
        position = lax.rem(position + 2 * n, n)
        return jnp.where(2 * position < n, 2 * position, 2 * (n - 1 - position) + 1) * 2 + core

    right, left = member(place + 1), member(place - 1)
    other = chip * 2 + 1 - core
    target = (right, left)

    barrier = pltpu.get_barrier_semaphore()
    for peer in (right, left, other):
        pl.semaphore_signal(barrier, inc=1, device_id={"wide": peer}, device_id_type=MESH)
    pl.semaphore_signal(barrier, inc=1, device_id={"section": 1 - section}, device_id_type=MESH)
    pl.semaphore_wait(barrier, 4)

    half = -(-rows // 32) * 16
    spans = ((0, half), (half, rows - half))
    streams = [(q, d) for q in range(2) for d in range(2)]

    def turn(position):
        return lax.rem(position + 2 * n, n)

    def reduce_at(d, step):
        return turn(place - step) if d == 0 else turn(place + step)

    def gather_at(d, index):
        return turn(place + 1 - index) if d == 0 else turn(place - 1 + index)

    def span(q):
        return pl.ds(*spans[q])

    def cols(d):
        return pl.ds(d * columns, columns)

    def remote(src, dst, send, recv, device):
        return pltpu.make_async_remote_copy(
            src_ref=src, dst_ref=dst, send_sem=send, recv_sem=recv,
            device_id=device, device_id_type=MESH)

    def own_copy(q, d, s):
        return pltpu.make_async_copy(
            g_ref.at[reduce_at(d, s) * 2 + core, span(q), cols(d)],
            own.at[d, s, span(q)], own_sem.at[d, q, s])

    def part_copy(q, d, s):
        return remote(
            g_ref.at[reduce_at(d, s) * 2 + 1 - core, span(q), cols(d)],
            part.at[d, s, span(q)], part_send.at[d, q, s], part_recv.at[d, q, s],
            {"wide": other})

    def ring_copy(q, d, s):
        return remote(
            own.at[d, s, span(q)], ring.at[d, s, span(q)],
            ring_send.at[d, q, s], ring_recv.at[d, q, s], {"wide": target[d]})

    def spot(q, d, index, which):
        return o_ref.at[gather_at(d, index) * 2 + which, span(q), cols(d)]

    def source(q, d, index):
        return own.at[d, n - 1, span(q)] if index == 0 else spot(q, d, index, core)

    def gather_copy(q, d, index):
        return remote(
            source(q, d, index), spot(q, d, index, core),
            gather_send.at[d, q, index], gather_recv.at[d, q, index], {"wide": target[d]})

    def gather_landed(q, d, index):
        return remote(
            source(q, d, 0), spot(q, d, index + 1, core),
            gather_send.at[d, q, index], gather_recv.at[d, q, index], {"wide": target[d]})

    def pair_copy(q, d, index):
        return remote(
            source(q, d, index), spot(q, d, index, core),
            pair_send.at[d, q, index], pair_recv.at[d, q, index], {"wide": other})

    def pair_landed(q, d, index):
        return remote(
            source(q, d, 0), spot(q, d, index, 1 - core),
            pair_send.at[d, q, index], pair_recv.at[d, q, index], {"wide": other})

    def keep_copy(q, d):
        return pltpu.make_async_copy(
            own.at[d, n - 1, span(q)], spot(q, d, 0, core), keep_sem.at[d, q])

    def cross_copy(d, index, mine):
        which = core if mine else 1 - core
        at = gather_at(d, index) * 2 + which
        if mine and index == 0:
            src = own.at[d, n - 1, pl.ds(rows - tail, tail)]
        else:
            src = o_ref.at[at, pl.ds(rows - tail, tail), cols(d)]
        lane = 0 if mine else 1
        return remote(
            src, e_ref.at[at, :, cols(d)],
            cross_send.at[d, lane, index], cross_recv.at[d, lane, index],
            {"section": 1 - section})

    for s in range(n):
        for q, d in streams:
            own_copy(q, d, s).start()
            part_copy(q, d, s).start()

    for s in range(n):
        for q, d in streams:
            own_copy(q, d, s).wait()
            part_copy(q, d, s).wait_recv()
            if s:
                ring_copy(q, d, s - 1).wait_recv()

            def add(tile, carry, q=q, d=d, s=s):
                at = pl.ds(pl.multiple_of(spans[q][0] + tile * 16, 16), 16)
                total = own[d, s, at].astype(jnp.float32) + part[d, s, at].astype(jnp.float32)
                if s:
                    total = total + ring[d, s - 1, at].astype(jnp.float32)
                own[d, s, at] = total.astype(own.dtype)
                return carry

            lax.fori_loop(0, spans[q][1] // 16, add, 0)
            if s < n - 1:
                ring_copy(q, d, s).start()
            else:
                gather_copy(q, d, 0).start()
                pair_copy(q, d, 0).start()
                keep_copy(q, d).start()
                if q == 1:
                    cross_copy(d, 0, True).start()

    for t in range(n - 1):
        for q, d in streams:
            gather_landed(q, d, t).wait_recv()
            if t < n - 2:
                gather_copy(q, d, t + 1).start()
            pair_copy(q, d, t + 1).start()
            if q == 1:
                cross_copy(d, t + 1, True).start()
        for q, d in streams:
            pair_landed(q, d, t).wait_recv()
            if q == 1:
                cross_copy(d, t, False).start()
    for q, d in streams:
        pair_landed(q, d, n - 1).wait_recv()
        if q == 1:
            cross_copy(d, n - 1, False).start()

    for q, d in streams:
        keep_copy(q, d).wait()
        for s in range(n):
            part_copy(q, d, s).wait_send()
            pair_copy(q, d, s).wait_send()
            if s < n - 1:
                ring_copy(q, d, s).wait_send()
                gather_copy(q, d, s).wait_send()
            if q == 1:
                for mine in (True, False):
                    cross_copy(d, s, mine).wait()


def ring_sum(stacked, tail):
    members, rows, width = stacked.shape
    n = members // 2
    dma = pltpu.SemaphoreType.DMA
    half = width // 2
    sems = [dma((2, 2, n)) for _ in range(9)] + [dma((2, 2)), dma((2, 2, n)), dma((2, 2, n))]
    return pl.pallas_call(
        functools.partial(ring_kernel, n, rows, tail),
        out_shape=(
            jax.ShapeDtypeStruct((members, rows, width), jnp.bfloat16),
            jax.ShapeDtypeStruct((members, tail, width), jnp.bfloat16),
        ),
        in_specs=[pl.BlockSpec(memory_space=pl.ANY)],
        out_specs=(pl.BlockSpec(memory_space=pl.ANY), pl.BlockSpec(memory_space=pl.ANY)),
        scratch_shapes=[
            pltpu.VMEM((2, n, rows, half), jnp.bfloat16),
            pltpu.VMEM((2, n, rows, half), jnp.bfloat16),
            pltpu.VMEM((2, n - 1, rows, half), jnp.bfloat16),
            sems,
        ],
        compiler_params=pltpu.CompilerParams(
            collective_id=0, has_side_effects=True, vmem_limit_bytes=48 * 2**20
        ),
    )(stacked)


def from_partner(block, axis, apart):
    count = lax.axis_size(axis)
    route = []
    for low in range(count):
        high = low | 1 << apart
        if high != low and high < count:
            route += [(low, high), (high, low)]
    return lax.ppermute(block, axis, route)


def layer_norm(values, gain, shift):
    center = jnp.mean(values, axis=-1, keepdims=True)
    offset = values - center
    spread = jnp.mean(offset * offset, axis=-1, keepdims=True)
    return offset * lax.rsqrt(spread + EPS) * gain + shift


def matmul_plain(left, right):
    return jnp.dot(left, right, preferred_element_type=jnp.float32)


def matmul_left_t(left, right):
    return lax.dot_general(
        left, right, (((0,), (0,)), ((), ())), preferred_element_type=jnp.float32
    )


def matmul_right_t(left, right):
    return lax.dot_general(
        left, right, (((1,), (1,)), ((), ())), preferred_element_type=jnp.float32
    )


def gelu_exact(values):
    return jax.nn.gelu(values, approximate=False)


def head_scores(packed, live_keys):
    length = packed.shape[0]
    heads_view = packed.reshape(length, 3, H, HD)
    scores = jnp.einsum(
        "qhe,khe->hqk", heads_view[:, 0], heads_view[:, 1], preferred_element_type=jnp.float32
    ) * HD ** (-0.5)
    return (heads_view, jnp.where(live_keys[None, None, :] > 0, scores, NEG))


def attend_clip(clip_item):
    packed, live_keys = clip_item
    heads_view, scores = head_scores(packed, live_keys)
    row_top = jnp.max(scores, axis=-1, keepdims=True)
    exp_scores = jnp.exp(scores - row_top)
    row_total = jnp.sum(exp_scores, axis=-1, keepdims=True)
    soft_low = (exp_scores / row_total).astype(jnp.bfloat16)
    context = jnp.einsum(
        "hqk,khe->qhe", soft_low, heads_view[:, 2], preferred_element_type=jnp.float32
    )
    return (context.reshape(packed.shape[0], H * HD), (row_top + jnp.log(row_total))[:, :, 0])


def attend_back_clip(clip_item):
    packed, live_keys, log_total, context_grad = clip_item
    length = packed.shape[0]
    heads_view, scores = head_scores(packed, live_keys)
    soft_weights = jnp.exp(scores - log_total[:, :, None])
    grad_view = context_grad.reshape(length, H, HD)
    weight_grad = jnp.einsum(
        "qhe,khe->hqk", grad_view, heads_view[:, 2], preferred_element_type=jnp.float32
    )
    value_grad = jnp.einsum(
        "hqk,qhe->khe",
        soft_weights.astype(jnp.bfloat16),
        grad_view,
        preferred_element_type=jnp.float32,
    )
    row_delta = jnp.sum(weight_grad * soft_weights, axis=-1, keepdims=True)
    score_grad = (soft_weights * (weight_grad - row_delta)).astype(jnp.bfloat16)
    query_grad = jnp.einsum(
        "hqk,khe->qhe", score_grad, heads_view[:, 1], preferred_element_type=jnp.float32
    ) * HD ** (-0.5)
    key_grad = jnp.einsum(
        "hqk,qhe->khe", score_grad, heads_view[:, 0], preferred_element_type=jnp.float32
    ) * HD ** (-0.5)
    return jnp.concatenate(
        [
            query_grad.reshape(length, H * HD),
            key_grad.reshape(length, H * HD),
            value_grad.reshape(length, H * HD),
        ],
        axis=1,
    )


def layer_forward(layer_in, live_keys, weights):
    gain_rows, vector_rows, attend_weight, project_weight, up_matrix, up_offset, down_matrix = (
        weights
    )
    block_clips, length, model_width = layer_in.shape
    flat_rows = layer_in.reshape(block_clips * length, model_width)
    normed = layer_norm(flat_rows, gain_rows[0], vector_rows[0]).astype(jnp.bfloat16)
    in_offset = jnp.concatenate(
        [vector_rows[1], jnp.zeros((model_width,), jnp.float32), vector_rows[2]]
    )
    packed = (matmul_plain(normed, attend_weight) + in_offset).astype(jnp.bfloat16)
    context, log_total = lax.map(
        attend_clip, (packed.reshape(block_clips, length, 3 * model_width), live_keys)
    )
    context = context.reshape(block_clips * length, model_width).astype(jnp.bfloat16)
    branch = matmul_plain(context, project_weight) + vector_rows[3]
    middle = flat_rows + branch
    hidden_in = layer_norm(middle, gain_rows[1], vector_rows[4]).astype(jnp.bfloat16)
    hidden = matmul_plain(hidden_in, up_matrix) + up_offset
    active = gelu_exact(hidden).astype(jnp.bfloat16)
    mixer = matmul_plain(active, down_matrix) + vector_rows[5]
    layer_out = middle + mixer
    kept_state = (
        flat_rows,
        normed,
        packed,
        log_total,
        context,
        middle,
        hidden_in,
        hidden,
        active,
        live_keys,
    )
    return (layer_out, branch, mixer, kept_state)


def ffn_back(out_grad_rows, kept_state, weights):
    gain_rows, vector_rows, attend_weight, project_weight, up_matrix, up_offset, down_matrix = (
        weights
    )
    flat_rows, normed, packed, log_total, context, middle, hidden_in, hidden, active, live_keys = (
        kept_state
    )
    mix_grad = out_grad_rows.astype(jnp.bfloat16)
    down_part = matmul_left_t(active, mix_grad)
    down_offset_part = jnp.sum(mix_grad.astype(jnp.float32), axis=0)
    active_grad = matmul_right_t(mix_grad, down_matrix)
    gelu_value, gelu_pull = jax.vjp(gelu_exact, hidden)
    hidden_grad = gelu_pull(active_grad)[0].astype(jnp.bfloat16)
    up_part = matmul_left_t(hidden_in, hidden_grad)
    up_offset_part = jnp.sum(hidden_grad.astype(jnp.float32), axis=0)
    hidden_in_grad = matmul_right_t(hidden_grad, up_matrix)
    norm_value, norm_pull = jax.vjp(layer_norm, middle, gain_rows[1], vector_rows[4])
    middle_part, gain_part, shift_part = norm_pull(hidden_in_grad)
    middle_grad = out_grad_rows + middle_part
    return (
        middle_grad,
        (gain_part, jnp.stack([shift_part, down_offset_part]), up_part, up_offset_part, down_part),
    )


def attn_back(middle_grad, kept_state, weights):
    gain_rows, vector_rows, attend_weight, project_weight, up_matrix, up_offset, down_matrix = (
        weights
    )
    flat_rows, normed, packed, log_total, context, middle, hidden_in, hidden, active, live_keys = (
        kept_state
    )
    block_clips = live_keys.shape[0]
    length = live_keys.shape[1]
    model_width = flat_rows.shape[1]
    branch_grad = middle_grad.astype(jnp.bfloat16)
    project_part = matmul_left_t(context, branch_grad)
    project_offset_part = jnp.sum(branch_grad.astype(jnp.float32), axis=0)
    context_grad = matmul_right_t(branch_grad, project_weight).astype(jnp.bfloat16)
    packed_grad = lax.map(
        attend_back_clip,
        (
            packed.reshape(block_clips, length, 3 * model_width),
            live_keys,
            log_total,
            context_grad.reshape(block_clips, length, model_width),
        ),
    )
    packed_grad = packed_grad.reshape(block_clips * length, 3 * model_width).astype(jnp.bfloat16)
    attend_part = matmul_left_t(normed, packed_grad)
    column_sums = jnp.sum(packed_grad.astype(jnp.float32), axis=0)
    normed_grad = matmul_right_t(packed_grad, attend_weight)
    norm_value, norm_pull = jax.vjp(layer_norm, flat_rows, gain_rows[0], vector_rows[0])
    row_part, gain_part, shift_part = norm_pull(normed_grad)
    input_grad = middle_grad + row_part
    vector_part = jnp.stack(
        [shift_part, column_sums[:model_width], column_sums[2 * model_width :], project_offset_part]
    )
    return (input_grad, (gain_part, vector_part, attend_part, project_part))


def embed_forward(feature_rows, mask_rows, kind_rows, embed_weight, embed_vectors, pos_embed):
    chosen = jnp.where(kind_rows[:, None, None] == 0, embed_weight[0], embed_weight[1])
    kind_offset = jnp.where(kind_rows[:, None] == 0, embed_vectors[0], embed_vectors[1])
    lifted = (
        jnp.einsum("ctf,cfd->ctd", feature_rows, chosen, preferred_element_type=jnp.float32)
        + kind_offset[:, None, :]
    )
    start = jnp.where(mask_rows[:, :, None] > 0, embed_vectors[2], lifted) + pos_embed
    return (start, chosen)


def embed_feature_grad(grad_low, mask_rows, chosen):
    lifted_grad = jnp.where(mask_rows[:, :, None] > 0, jnp.zeros_like(grad_low), grad_low)
    return jnp.einsum(
        "ctd,cfd->ctf", lifted_grad, chosen, preferred_element_type=jnp.float32
    ).astype(jnp.bfloat16)


def embed_parts(grad_low, feature_rows, mask_rows, kind_rows, position_keep):
    kept_grad = grad_low.astype(jnp.float32) * position_keep[None, :, None]
    lifted_grad = jnp.where(mask_rows[:, :, None] > 0, 0.0, kept_grad).astype(jnp.bfloat16)
    chosen_grad = jnp.einsum(
        "ctf,ctd->cfd", feature_rows, lifted_grad, preferred_element_type=jnp.float32
    )
    offset_grad = jnp.sum(lifted_grad.astype(jnp.float32), axis=1)
    kind_zero = kind_rows == 0
    weight_part = jnp.stack(
        [
            jnp.sum(jnp.where(kind_zero[:, None, None], chosen_grad, 0.0), axis=0),
            jnp.sum(jnp.where(kind_zero[:, None, None], 0.0, chosen_grad), axis=0),
        ]
    )
    mask_part = jnp.sum(jnp.where(mask_rows[:, :, None] > 0, kept_grad, 0.0), axis=(0, 1))
    vector_part = jnp.stack(
        [
            jnp.sum(jnp.where(kind_zero[:, None], offset_grad, 0.0), axis=0),
            jnp.sum(jnp.where(kind_zero[:, None], 0.0, offset_grad), axis=0),
            mask_part,
        ]
    )
    pos_part = jnp.sum(kept_grad, axis=0)
    return (weight_part, vector_part, pos_part)


def local(
    features,
    masked,
    valid,
    kinds,
    embed_weight,
    embed_vectors,
    pos_embed,
    norm_gains,
    vectors,
    qkv_weight,
    out_weight,
    up_weight,
    up_bias,
    down_weight,
    cotangent,
):
    section_index = lax.axis_index("section")
    is_first = section_index == 0
    clip_total, length, feat_width = features.shape
    model_width = pos_embed.shape[1]
    half_width = model_width // 2
    half_feat = feat_width // 2
    block_clips = clip_total // MB
    weights = (
        norm_gains[0],
        vectors[0],
        qkv_weight[0],
        out_weight[0],
        up_weight[0],
        up_bias[0],
        down_weight[0],
    )
    live_all = valid.astype(jnp.float32)
    position_keep = (jnp.arange(length, dtype=jnp.int32) // (length // 2) == section_index).astype(
        jnp.float32
    )

    def block_rows(source, block_index):
        return lax.dynamic_slice_in_dim(source, block_index * block_clips, block_clips, 0)

    received = jnp.zeros((block_clips, length, model_width), jnp.bfloat16)
    kept_ticks = []
    output_blocks = []
    square_sums = jnp.zeros((3,), jnp.float32)
    for forward_tick in range(MB + 1):
        offset_tick = forward_tick - section_index
        block_index = jnp.clip(offset_tick, 0, MB - 1)
        tick_flag = ((offset_tick >= 0) & (offset_tick < MB)).astype(jnp.float32)
        feature_rows = block_rows(features, block_index)
        mask_rows = block_rows(masked, block_index)
        kind_rows = block_rows(kinds, block_index)
        live_keys = block_rows(live_all, block_index)
        start, chosen = embed_forward(
            feature_rows, mask_rows, kind_rows, embed_weight, embed_vectors, pos_embed
        )
        layer_in = jnp.where(is_first, start, received.astype(jnp.float32))
        layer_out, branch, mixer, kept_state = layer_forward(layer_in, live_keys, weights)
        token_flags = live_keys.reshape(-1, 1) * tick_flag
        square_sums = square_sums + jnp.stack(
            [
                jnp.sum(token_flags * layer_out * layer_out),
                jnp.sum(token_flags * branch * branch),
                jnp.sum(token_flags * mixer * mixer),
            ]
        )
        sent_rows = layer_out.astype(jnp.bfloat16).reshape(block_clips, length, model_width)
        received = from_partner(sent_rows, "section", 0)
        if forward_tick >= 1:
            full_out = jnp.where(is_first, received, sent_rows)
            output_blocks.append(
                lax.dynamic_slice_in_dim(full_out, section_index * half_width, half_width, 2)
            )
        kept_ticks.append((kept_state, mask_rows, chosen))
    valid_count = jnp.sum(live_all)
    ffn_accum = (
        jnp.zeros((model_width,), jnp.float32),
        jnp.zeros((2, model_width), jnp.float32),
        jnp.zeros(up_weight.shape[1:], jnp.float32),
        jnp.zeros(up_bias.shape[1:], jnp.float32),
        jnp.zeros(down_weight.shape[1:], jnp.float32),
    )
    attn_accum = (
        jnp.zeros((model_width,), jnp.float32),
        jnp.zeros((4, model_width), jnp.float32),
        jnp.zeros(qkv_weight.shape[1:], jnp.float32),
        jnp.zeros(out_weight.shape[1:], jnp.float32),
    )
    embed_accum = (
        jnp.zeros(embed_weight.shape, jnp.float32),
        jnp.zeros(embed_vectors.shape, jnp.float32),
        jnp.zeros(pos_embed.shape, jnp.float32),
    )
    back_in = jnp.zeros((block_clips, length, model_width), jnp.bfloat16)
    feature_blocks = []
    for back_tick in range(MB + 1):
        kept_state, mask_rows, chosen = kept_ticks[MB - back_tick]
        offset_tick = MB - back_tick - section_index
        block_index = jnp.clip(offset_tick, 0, MB - 1)
        tick_flag = ((offset_tick >= 0) & (offset_tick < MB)).astype(jnp.float32)
        cot_rows = block_rows(cotangent, block_index)
        out_grad_rows = jnp.where(
            is_first, back_in.astype(jnp.float32), cot_rows.astype(jnp.float32)
        ).reshape(block_clips * length, model_width)
        middle_grad, ffn_part = ffn_back(out_grad_rows, kept_state, weights)
        ffn_accum = tuple((accum + tick_flag * part for accum, part in zip(ffn_accum, ffn_part)))
        input_grad, attn_part = attn_back(middle_grad, kept_state, weights)
        attn_accum = tuple((accum + tick_flag * part for accum, part in zip(attn_accum, attn_part)))
        own_low = input_grad.astype(jnp.bfloat16).reshape(block_clips, length, model_width)
        feature_grad = embed_feature_grad(own_low, mask_rows, chosen)
        joined_send = jnp.concatenate([own_low, feature_grad[:, :, half_feat:]], axis=2)
        joined_back = from_partner(joined_send, "section", 0)
        back_in = joined_back[:, :, :model_width]
        if back_tick >= 1:
            feature_blocks.append(
                jnp.where(is_first, feature_grad[:, :, :half_feat], joined_back[:, :, model_width:])
            )
            part_index = MB - back_tick
            grad_low = jnp.where(is_first, own_low, back_in)
            embed_part = embed_parts(
                grad_low,
                block_rows(features, part_index),
                block_rows(masked, part_index),
                block_rows(kinds, part_index),
                position_keep,
            )
            embed_accum = tuple((accum + part for accum, part in zip(embed_accum, embed_part)))
    low = jnp.bfloat16
    members = lax.axis_size("wide")
    feed_width = up_weight.shape[2]
    blocks = feed_width // model_width

    def side_by_side(matrix):
        height, width = matrix.shape
        pieces = matrix.reshape(height, width // model_width, model_width)
        return pieces.transpose(1, 0, 2).reshape(-1, model_width)

    weight_rows = jnp.concatenate(
        [
            side_by_side(attn_accum[2].astype(low)),
            attn_accum[3].astype(low),
            side_by_side(ffn_accum[2].astype(low)),
            ffn_accum[4].astype(low),
        ]
    ).reshape(members, -1, model_width)
    embed_rows = jnp.concatenate(
        [embed_accum[0].reshape(-1, model_width), embed_accum[2]]
    ).astype(low).reshape(members, -1, model_width)
    stats = jnp.zeros((1, model_width), jnp.float32)
    stats = stats.at[0, 0:3].set(square_sums).at[0, 3].set(valid_count)
    small_rows = jnp.concatenate(
        [
            attn_accum[0][None],
            ffn_accum[0][None],
            attn_accum[1],
            ffn_accum[1],
            ffn_accum[3].reshape(blocks, model_width),
            embed_accum[1],
            stats,
        ]
    ).astype(low)
    small_rows = jnp.pad(small_rows, ((0, members * SMALL - small_rows.shape[0]), (0, 0)))
    stacked = jnp.concatenate(
        [weight_rows, embed_rows, small_rows.reshape(members, SMALL, model_width)], axis=1
    )
    weight_count, embed_count = weight_rows.shape[1], embed_rows.shape[1]
    total, cross = ring_sum(stacked, embed_count + SMALL)
    cross = cross.astype(jnp.float32)
    weight_total = total[:, :weight_count].reshape(-1, model_width).astype(jnp.float32)
    embed_total = (total[:, weight_count : weight_count + embed_count].astype(jnp.float32)
                   + cross[:, :embed_count]).reshape(-1, model_width)
    small_total = total[0, weight_count + embed_count :].astype(jnp.float32)
    small_cross = cross[0, embed_count:]
    width = model_width
    edges = [3 * width, 4 * width, 4 * width + blocks * width]

    def joined(rows, count):
        return rows.reshape(count, width, width).transpose(1, 0, 2).reshape(width, count * width)

    attend_total = joined(weight_total[: edges[0]], 3)
    project_total = weight_total[edges[0] : edges[1]]
    up_total = joined(weight_total[edges[1] : edges[2]], blocks)
    down_total = weight_total[edges[2] :]
    gains_out = small_total[None, 0:2]
    vectors_out = small_total[None, 2:8]
    up_offset_total = small_total[8 : 8 + blocks].reshape(-1)
    embed_vectors_total = (small_total + small_cross)[8 + blocks : 11 + blocks]
    stat_row = small_total[11 + blocks]
    output = jnp.concatenate(output_blocks, axis=0)
    feature_out = jnp.concatenate(feature_blocks[::-1], axis=0)
    rms_out = jnp.sqrt(stat_row[0:3] / (stat_row[3] * model_width))[None]
    embed_weight_rows = 2 * feat_width
    return (
        output,
        feature_out,
        embed_total[:embed_weight_rows].reshape(2, feat_width, width),
        embed_vectors_total,
        embed_total[embed_weight_rows:],
        gains_out,
        vectors_out,
        attend_total[None],
        project_total[None],
        up_total[None],
        up_offset_total[None],
        down_total[None],
        rms_out,
    )


def solution(mesh):
    return jax.shard_map(
        local,
        mesh=mesh,
        in_specs=(
            P("wide", None, None),
            P("wide", None),
            P("wide", None),
            P("wide"),
            P(),
            P(),
            P(),
            P("section", None, None),
            P("section", None, None),
            P("section", None, None),
            P("section", None, None),
            P("section", None, None),
            P("section", None),
            P("section", None, None),
            P("wide", None, None),
        ),
        out_specs=(
            P("wide", None, "section"),
            P("wide", None, "section"),
            P(),
            P(),
            P(),
            P("section", None, None),
            P("section", None, None),
            P("section", None, None),
            P("section", None, None),
            P("section", None, None),
            P("section", None),
            P("section", None, None),
            P("section", None),
        ),
        check_vma=False,
    )
```

```python
import functools
import math

import jax
import jax.numpy as jnp
from jax import lax
from jax.experimental import pallas as pl
from jax.experimental.pallas import tpu as pltpu
from jax.sharding import PartitionSpec as P

H = 12
HD = 64
EPS = 1e-06
NEG = -1000000000.0
MESH = pl.DeviceIdType.MESH
SMALL = 16


def ring_kernel(n, rows, tail, g_ref, f_ref, o_ref, e_ref, h_ref, own, part, ring, sems):
    (own_sem, part_send, part_recv, ring_send, ring_recv, gather_send, gather_recv,
     pair_send, pair_recv, keep_sem, cross_send, cross_recv, feat_sem) = sems
    columns = g_ref.shape[2] // 2
    me = lax.axis_index("wide")
    section = lax.axis_index("section")
    chip, core = me // 2, me % 2
    place = jnp.where(chip % 2 == 0, chip // 2, n - 1 - chip // 2)

    def member(position):
        position = lax.rem(position + 2 * n, n)
        return jnp.where(2 * position < n, 2 * position, 2 * (n - 1 - position) + 1) * 2 + core

    right, left = member(place + 1), member(place - 1)
    other = chip * 2 + 1 - core
    target = (right, left)

    barrier = pltpu.get_barrier_semaphore()
    for peer in (right, left, other):
        pl.semaphore_signal(barrier, inc=1, device_id={"wide": peer}, device_id_type=MESH)
    pl.semaphore_signal(barrier, inc=1, device_id={"section": 1 - section}, device_id_type=MESH)
    pl.semaphore_wait(barrier, 4)

    half = -(-rows // 32) * 16
    spans = ((0, half), (half, rows - half))
    streams = [(q, d) for q in range(2) for d in range(2)]

    def turn(position):
        return lax.rem(position + 2 * n, n)

    def reduce_at(d, step):
        return turn(place - step) if d == 0 else turn(place + step)

    def gather_at(d, index):
        return turn(place + 1 - index) if d == 0 else turn(place - 1 + index)

    def span(q):
        return pl.ds(*spans[q])

    def cols(d):
        return pl.ds(d * columns, columns)

    def remote(src, dst, send, recv, device):
        return pltpu.make_async_remote_copy(
            src_ref=src, dst_ref=dst, send_sem=send, recv_sem=recv,
            device_id=device, device_id_type=MESH)

    def own_copy(q, d, s):
        return pltpu.make_async_copy(
            g_ref.at[reduce_at(d, s) * 2 + core, span(q), cols(d)],
            own.at[d, s, span(q)], own_sem.at[d, q, s])

    def part_copy(q, d, s):
        return remote(
            g_ref.at[reduce_at(d, s) * 2 + 1 - core, span(q), cols(d)],
            part.at[d, s, span(q)], part_send.at[d, q, s], part_recv.at[d, q, s],
            {"wide": other})

    def ring_copy(q, d, s):
        return remote(
            own.at[d, s, span(q)], ring.at[d, s, span(q)],
            ring_send.at[d, q, s], ring_recv.at[d, q, s], {"wide": target[d]})

    def spot(q, d, index, which):
        return o_ref.at[gather_at(d, index) * 2 + which, span(q), cols(d)]

    def source(q, d, index):
        return own.at[d, n - 1, span(q)] if index == 0 else spot(q, d, index, core)

    def gather_copy(q, d, index):
        return remote(
            source(q, d, index), spot(q, d, index, core),
            gather_send.at[d, q, index], gather_recv.at[d, q, index], {"wide": target[d]})

    def gather_landed(q, d, index):
        return remote(
            source(q, d, 0), spot(q, d, index + 1, core),
            gather_send.at[d, q, index], gather_recv.at[d, q, index], {"wide": target[d]})

    def pair_copy(q, d, index):
        return remote(
            source(q, d, index), spot(q, d, index, core),
            pair_send.at[d, q, index], pair_recv.at[d, q, index], {"wide": other})

    def pair_landed(q, d, index):
        return remote(
            source(q, d, 0), spot(q, d, index, 1 - core),
            pair_send.at[d, q, index], pair_recv.at[d, q, index], {"wide": other})

    def keep_copy(q, d):
        return pltpu.make_async_copy(
            own.at[d, n - 1, span(q)], spot(q, d, 0, core), keep_sem.at[d, q])

    def cross_copy(d, index, mine):
        which = core if mine else 1 - core
        at = gather_at(d, index) * 2 + which
        if mine and index == 0:
            src = own.at[d, n - 1, pl.ds(rows - tail, tail)]
        else:
            src = o_ref.at[at, pl.ds(rows - tail, tail), cols(d)]
        lane = 0 if mine else 1
        return remote(
            src, e_ref.at[at, :, cols(d)],
            cross_send.at[d, lane, index], cross_recv.at[d, lane, index],
            {"section": 1 - section})

    feat_half = h_ref.shape[2]
    feat_keep = pltpu.make_async_copy(
        f_ref.at[:, :, pl.ds(0, feat_half)], h_ref, feat_sem.at[0])
    feat_send = remote(
        f_ref.at[:, :, pl.ds(feat_half, feat_half)], h_ref, feat_sem.at[1], feat_sem.at[2],
        {"section": 1 - section})

    @pl.when(section == 0)
    def _():
        feat_keep.start()
        feat_send.start()

    for s in range(n):
        for q, d in streams:
            own_copy(q, d, s).start()
            part_copy(q, d, s).start()

    for s in range(n):
        for q, d in streams:
            own_copy(q, d, s).wait()
            part_copy(q, d, s).wait_recv()
            if s:
                ring_copy(q, d, s - 1).wait_recv()

            def add(tile, carry, q=q, d=d, s=s):
                at = pl.ds(pl.multiple_of(spans[q][0] + tile * 16, 16), 16)
                total = own[d, s, at].astype(jnp.float32) + part[d, s, at].astype(jnp.float32)
                if s:
                    total = total + ring[d, s - 1, at].astype(jnp.float32)
                own[d, s, at] = total.astype(own.dtype)
                return carry

            lax.fori_loop(0, spans[q][1] // 16, add, 0)
            if s < n - 1:
                ring_copy(q, d, s).start()
            else:
                gather_copy(q, d, 0).start()
                pair_copy(q, d, 0).start()
                keep_copy(q, d).start()
                if q == 1:
                    cross_copy(d, 0, True).start()

    for t in range(n - 1):
        for q, d in streams:
            gather_landed(q, d, t).wait_recv()
            if t < n - 2:
                gather_copy(q, d, t + 1).start()
            pair_copy(q, d, t + 1).start()
            if q == 1:
                cross_copy(d, t + 1, True).start()
        for q, d in streams:
            pair_landed(q, d, t).wait_recv()
            if q == 1:
                cross_copy(d, t, False).start()
    for q, d in streams:
        pair_landed(q, d, n - 1).wait_recv()
        if q == 1:
            cross_copy(d, n - 1, False).start()

    @pl.when(section == 0)
    def _():
        feat_keep.wait()
        feat_send.wait_send()

    @pl.when(section == 1)
    def _():
        feat_send.wait_recv()

    for q, d in streams:
        keep_copy(q, d).wait()
        for s in range(n):
            part_copy(q, d, s).wait_send()
            pair_copy(q, d, s).wait_send()
            if s < n - 1:
                ring_copy(q, d, s).wait_send()
                gather_copy(q, d, s).wait_send()
            if q == 1:
                for mine in (True, False):
                    cross_copy(d, s, mine).wait()


def dot_nn(left, right):
    return jnp.dot(left, right, preferred_element_type=jnp.float32)


def dot_nt(left, right):
    return lax.dot_general(
        left, right, (((1,), (1,)), ((), ())), preferred_element_type=jnp.float32
    )


def tile_of(index, size):
    return pl.ds(pl.multiple_of(index * size, size), size)


def column_sum(values):
    return jnp.sum(values, axis=0, keepdims=True)


def row_mean(values):
    return jnp.mean(values, axis=-1, keepdims=True)


def gelu_pair(hidden):
    decay = jnp.exp(-0.5 * hidden * hidden)
    t = 1.0 / (1.0 + (0.3275911 * 0.5**0.5) * jnp.abs(hidden))
    poly = 1.061405429 * 0.5
    for term in (-1.453152027, 1.421413741, -0.284496736, 0.254829592):
        poly = poly * t + 0.5 * term
    upper = poly * t * decay
    cdf = jnp.where(hidden > 0.0, 1.0 - upper, upper)
    return hidden * cdf, cdf + hidden * decay * 0.3989422804014327


def fetch(pairs, sems):
    copies = [pltpu.make_async_copy(src, dst, sems.at[i]) for i, (src, dst) in enumerate(pairs)]
    for copy in copies:
        copy.start()
    return copies


def greet_partner():
    barrier = pltpu.get_barrier_semaphore()
    pl.semaphore_signal(
        barrier, inc=1, device_id={"section": 1 - lax.axis_index("section")}, device_id_type=MESH
    )
    pl.semaphore_wait(barrier, 1)


def to_partner(src, dst, send, recv):
    return pltpu.make_async_remote_copy(
        src_ref=src, dst_ref=dst, send_sem=send, recv_sem=recv,
        device_id={"section": 1 - lax.axis_index("section")}, device_id_type=MESH)


def forward_kernel(
    feat_h, chosen_h, pos_h, wqkv_h, wout_h, wup_h, wdown_h,
    cols, kind_offset, mask_row, bias_row, live_row, gains, vectors, up_bias,
    left_h, x_h, qkv_h, probs_h, middle_h, slope_h, out_h, stats,
    feat, chosen, pos, wqkv, wout, wup, wdown,
    x, normed, qkv, probs, context, middle, hidden_in, active, slope, y, landed,
    load_sem, save_sem, probs_sem, send_sem, recv_sem, back_send, back_recv, keep_sem,
):
    low = jnp.bfloat16
    section = lax.axis_index("section")
    clips, length, width = landed.shape
    half = length // 2
    feed = wup.shape[1]
    heads2 = width // 128
    blocks = feed // width
    greet_partner()
    loads = fetch(
        [(feat_h, feat), (chosen_h, chosen), (pos_h, pos), (wqkv_h, wqkv), (wout_h, wout),
         (wup_h, wup), (wdown_h, wdown)], load_sem)
    stats[...] = jnp.zeros_like(stats)
    low_lanes = lax.broadcasted_iota(jnp.int32, (1, 128), 1) < HD

    def save(index, src, dst):
        return pltpu.make_async_copy(src, dst, save_sem.at[index])

    def saves(c):
        rows = pl.ds(pl.multiple_of(c * length, length), length)
        pairs = [
            (x, x_h.at[c]), (normed, left_h.at[0, rows]), (qkv, qkv_h.at[c]),
            (context, left_h.at[1, rows]), (middle, middle_h.at[c]),
            (hidden_in, left_h.at[2, rows]), (slope, slope_h.at[c]),
        ] + [
            (active.at[:, pl.ds(b * width, width)], left_h.at[3 + b, rows]) for b in range(blocks)
        ]
        return [save(i, src, dst) for i, (src, dst) in enumerate(pairs)]

    def probs_save(c, pair):
        slot = lax.rem(pair, 2)
        return pltpu.make_async_copy(
            probs.at[slot], probs_h.at[c, pl.ds(pair * 2, 2)], probs_sem.at[slot])

    def send_half(c, h):
        rows = pl.ds(h * half, half)
        return to_partner(
            y.at[c, rows], landed.at[c, rows], send_sem.at[c, h], recv_sem.at[c, h])

    def back_half(c, h):
        rows = pl.ds(h * half, half)
        return to_partner(
            y.at[c, rows, pl.ds(0, width // 2)], out_h.at[c, rows],
            back_send.at[c, h], back_recv.at[c, h])

    def keep_half(c, h):
        rows = pl.ds(h * half, half)
        return pltpu.make_async_copy(
            y.at[c, rows, pl.ds(width // 2, width // 2)], out_h.at[c, rows], keep_sem.at[c, h])

    def clip(c, carry):
        def after_first(index):
            @pl.when(c > 0)
            def _():
                saves(c - 1)[index].wait()

        after_first(0)
        after_first(1)

        @pl.when(section == 0)
        def _():
            @pl.when(c == 0)
            def _():
                for copy in loads[:3]:
                    copy.wait()

            def tile(i, carry):
                rows = tile_of(i, 128)
                lifted = dot_nn(feat[c, rows, :], chosen[c]) + kind_offset[c]
                hidden = cols[c, rows, :][:, 0:1]
                x[rows, :] = jnp.where(hidden > 0.0, mask_row[...], lifted) + pos[rows, :]
                return carry

            lax.fori_loop(0, length // 128, tile, 0)

        @pl.when(section == 1)
        def _():
            @pl.when(c == 0)
            def _():
                for copy in loads[:3]:
                    copy.wait()

            for h in range(2):
                send_half(c, h).wait_recv()

            def tile(i, carry):
                rows = tile_of(i, 64)
                x[rows, :] = landed[c, rows, :].astype(jnp.float32)
                return carry

            lax.fori_loop(0, length // 64, tile, 0)

        own = saves(c)
        own[0].start()

        def norm_rows(source, target, which, shift, first, count):
            gain, offset = gains[which : which + 1, :], vectors[shift : shift + 1, :]

            def tile(i, carry):
                rows = tile_of(i, 64)
                values = source[rows, :]
                values = values - row_mean(values)
                scale = lax.rsqrt(row_mean(values * values) + EPS)
                target[rows, :] = (values * scale * gain + offset).astype(low)
                return carry

            lax.fori_loop(first, first + count, tile, 0)

        norm_rows(x, normed, 0, 0, 0, length // 64)
        own[1].start()
        after_first(2)

        @pl.when(c == 0)
        def _():
            loads[3].wait()

        def qkv_tile(j, carry):
            at = tile_of(j, 256)
            qkv[:, at] = (dot_nn(normed[...], wqkv[:, at]) + bias_row[:, at]).astype(low)
            return carry

        lax.fori_loop(0, 3 * width // 256, qkv_tile, 0)
        own[2].start()
        after_first(3)

        def attend(pair, carry):
            @pl.when((pair > 1) | (c > 0))
            def _():
                probs_save(c, pair).wait()

            at = tile_of(pair, 128)
            queries = qkv[:, at]
            keys_in = qkv[:, tile_of(pair + heads2, 128)]
            values_in = qkv[:, tile_of(pair + 2 * heads2, 128)]
            outs = []
            for h in range(2):
                pick = jnp.where(low_lanes == (h == 0), HD**-0.5, 0.0).astype(low)
                scores = dot_nt(queries * pick, keys_in) + live_row[c]
                top = jnp.max(scores, axis=-1, keepdims=True)
                scores = jnp.exp(scores - top)
                total = jnp.sum(scores, axis=-1, keepdims=True)
                soft = (scores * (1.0 / total)).astype(low)
                probs[lax.rem(pair, 2), h] = soft
                outs.append(dot_nn(soft, values_in))
            context[:, at] = jnp.where(low_lanes, outs[0], outs[1]).astype(low)
            probs_save(c, pair).start()
            return carry

        lax.fori_loop(0, heads2, attend, 0)
        own[3].start()
        after_first(4)

        @pl.when(c == 0)
        def _():
            loads[4].wait()

        live = cols[c][:, 1:2]

        def out_tile(j, carry):
            at = tile_of(j, 256)
            branch = dot_nn(context[...], wout[:, at]) + vectors[3:4, at]
            middle[:, at] = x[:, at] + branch
            stats[1:2, at] += column_sum(branch * branch * live)
            return carry

        lax.fori_loop(0, width // 256, out_tile, 0)
        own[4].start()
        for index in range(5, 7 + blocks):
            after_first(index)

        @pl.when(c == 0)
        def _():
            loads[5].wait()
            loads[6].wait()

        for h in range(2):
            rows = pl.ds(h * half, half)
            norm_rows(middle, hidden_in, 1, 4, h * (half // 64), half // 64)
            if h == 1:
                own[5].start()

            def up_tile(j, carry):
                at = tile_of(j, 256)
                hidden = dot_nn(hidden_in[rows, :], wup[:, at]) + up_bias[:, at]
                value, steep = gelu_pair(hidden)
                active[rows, at] = value.astype(low)
                slope[rows, at] = steep.astype(low)
                return carry

            lax.fori_loop(0, feed // 256, up_tile, 0)
            if h == 1:
                for copy in own[6:]:
                    copy.start()

            def down_tile(j, carry):
                at = tile_of(j, 256)
                mixer = dot_nn(active[rows, :], wdown[:, at]) + vectors[5:6, at]
                total = middle[rows, at] + mixer
                flags = cols[c, rows, :][:, 1:2]
                stats[0:1, at] += column_sum(total * total * flags)
                stats[2:3, at] += column_sum(mixer * mixer * flags)
                y[c, rows, at] = total.astype(low)
                return carry

            lax.fori_loop(0, width // 256, down_tile, 0)

            @pl.when(section == 0)
            def _():
                send_half(c, h).start()

            @pl.when(section == 1)
            def _():
                back_half(c, h).start()
                keep_half(c, h).start()
        return carry

    lax.fori_loop(0, clips, clip, 0)
    for pair in (heads2 - 2, heads2 - 1):
        probs_save(clips - 1, pair).wait()
    for copy in saves(clips - 1):
        copy.wait()
    for c in range(clips):
        for h in range(2):
            @pl.when(section == 0)
            def _():
                send_half(c, h).wait_send()
                back_half(c, h).wait_recv()

            @pl.when(section == 1)
            def _():
                back_half(c, h).wait_send()
                keep_half(c, h).wait()


def backward_kernel(
    cot_h, wqkv_h, wout_h, wup_h, wdown_h, x_h, qkv_h, probs_h, middle_h, slope_h, gains,
    right_h, dx_h, small, up_sums,
    wqkv, wout, wup, wdown, x, qkv, probs, middle, slope, g,
    d_hidden, wide_grad, d_middle, d_branch, d_context, d_qkv, d_low,
    load_sem, state_sem, probs_sem, save_sem, dx_sem, send_sem, recv_sem,
):
    low = jnp.bfloat16
    f32 = jnp.float32
    section = lax.axis_index("section")
    clips, length, width = g.shape
    half = length // 2
    feed = wup.shape[1]
    heads2 = width // 128
    blocks = feed // width
    greet_partner()

    def cot_load(c):
        return pltpu.make_async_copy(cot_h.at[c], g.at[c], state_sem.at[c, 0])

    def state_loads(c):
        pairs = [(slope_h, slope), (middle_h, middle), (qkv_h, qkv), (x_h, x)]
        return [
            pltpu.make_async_copy(src.at[c], dst.at[c], state_sem.at[c, 1 + i])
            for i, (src, dst) in enumerate(pairs)
        ]

    @pl.when(section == 1)
    def _():
        cot_load(0).start()

    loads = fetch([(wdown_h, wdown), (wup_h, wup), (wout_h, wout), (wqkv_h, wqkv)], load_sem)
    for c in range(clips):
        for copy in state_loads(c):
            copy.start()

    @pl.when(section == 1)
    def _():
        for c in range(1, clips):
            cot_load(c).start()

    small[...] = jnp.zeros_like(small)
    up_sums[...] = jnp.zeros_like(up_sums)
    low_lanes = lax.broadcasted_iota(jnp.int32, (1, 128), 1) < HD
    slots = probs.shape[0]
    pairs_total = clips * heads2

    def probs_load(step):
        slot = lax.rem(step, slots)
        return pltpu.make_async_copy(
            probs_h.at[step // heads2, pl.ds(lax.rem(step, heads2) * 2, 2)],
            probs.at[slot], probs_sem.at[slot])

    for step in range(slots):
        probs_load(step).start()

    def saves(c):
        rows = pl.ds(pl.multiple_of(c * length, length), length)
        pairs = [(d_qkv.at[:, pl.ds(b * width, width)], right_h.at[b, rows]) for b in range(3)]
        pairs += [(d_branch, right_h.at[3, rows])]
        pairs += [
            (d_hidden.at[:, pl.ds(b * width, width)], right_h.at[4 + b, rows])
            for b in range(blocks)
        ]
        pairs += [(g.at[c], right_h.at[4 + blocks, rows])]
        return [pltpu.make_async_copy(s, d, save_sem.at[i]) for i, (s, d) in enumerate(pairs)]

    def send_half(c, h):
        rows = pl.ds(h * half, half)
        return to_partner(
            d_low.at[c, rows], g.at[c, rows], send_sem.at[c, h], recv_sem.at[c, h])

    def dx_save(c):
        return pltpu.make_async_copy(d_low.at[c], dx_h.at[c], dx_sem.at[c])

    def norm_back(source, carried, which, shift_row, rows, take):
        gain = gains[which : which + 1, :]
        values = source[rows, :]
        values = values - row_mean(values)
        scale = lax.rsqrt(row_mean(values * values) + EPS)
        values = values * scale
        grad = wide_grad[rows, :]
        small[which : which + 1, :] += column_sum(grad * values)
        small[shift_row : shift_row + 1, :] += column_sum(grad)
        grad = grad * gain
        return carried + scale * (grad - row_mean(grad) - values * row_mean(grad * values))

    def clip(c, carry):
        def after_first(lo, hi):
            @pl.when(c > 0)
            def _():
                for copy in saves(c - 1)[lo:hi]:
                    copy.wait()

        after_first(4, 5 + blocks)

        @pl.when(section == 1)
        def _():
            cot_load(c).wait()

        state = state_loads(c)
        own = saves(c)

        @pl.when(c == 0)
        def _():
            loads[0].wait()
            loads[1].wait()

        state[0].wait()
        state[1].wait()
        for h in range(2):
            rows = pl.ds(h * half, half)

            @pl.when(section == 0)
            def _():
                send_half(c, h).wait_recv()

            if h == 1:
                own[-1].start()

            def feed_tile(j, carry):
                at = tile_of(j, 256)
                d_active = dot_nt(g[c, rows, :], wdown[at, :])
                grad = (slope[c, rows, at].astype(f32) * d_active).astype(low)
                d_hidden[rows, at] = grad
                up_sums[:, at] += column_sum(grad.astype(f32))
                return carry

            lax.fori_loop(0, feed // 256, feed_tile, 0)

            def in_tile(j, carry):
                at = tile_of(j, 256)
                wide_grad[rows, at] = dot_nt(d_hidden[rows, :], wup[at, :])
                return carry

            lax.fori_loop(0, width // 256, in_tile, 0)

        after_first(3, 4)
        for copy in own[4:-1]:
            copy.start()

        def middle_tile(i, carry):
            rows = tile_of(i, 64)
            grad_in = g[c, rows, :].astype(f32)
            total = norm_back(middle.at[c], grad_in, 1, 6, rows, None)
            d_middle[rows, :] = total
            rounded = total.astype(low)
            d_branch[rows, :] = rounded
            small[5:6, :] += column_sum(rounded.astype(f32))
            small[7:8, :] += column_sum(grad_in)
            return carry

        lax.fori_loop(0, length // 64, middle_tile, 0)
        own[3].start()

        @pl.when(c == 0)
        def _():
            loads[2].wait()

        def context_tile(j, carry):
            at = tile_of(j, 256)
            d_context[:, at] = dot_nt(d_branch[...], wout[at, :]).astype(low)
            return carry

        lax.fori_loop(0, width // 256, context_tile, 0)
        state[2].wait()
        after_first(0, 3)

        def attend(pair, carry):
            step = c * heads2 + pair
            slot = lax.rem(step, slots)
            probs_load(step).wait()
            at, key_at = tile_of(pair, 128), tile_of(pair + heads2, 128)
            value_at = tile_of(pair + 2 * heads2, 128)
            queries, keys_in, values_in = qkv[c, :, at], qkv[c, :, key_at], qkv[c, :, value_at]
            grad = d_context[:, at]
            queries_t, grad_t = queries.T, grad.T
            d_queries, keys_t, values_t = [], [], []
            for h in range(2):
                pick = jnp.where(low_lanes == (h == 0), 1.0, 0.0).astype(low)
                soft = probs[slot, h]
                soft_wide = soft.astype(f32)
                d_soft = dot_nt(grad * pick, values_in)
                delta = jnp.sum(soft_wide * d_soft, axis=-1, keepdims=True)
                d_scores = (soft_wide * (d_soft - delta)).astype(low)
                part = slice(h * HD, (h + 1) * HD)
                values_t.append(dot_nn(grad_t[part], soft))
                keys_t.append(dot_nn(queries_t[part], d_scores))
                d_queries.append(dot_nn(d_scores, keys_in))
            scale = HD**-0.5
            query_grad = (jnp.where(low_lanes, d_queries[0], d_queries[1]) * scale).astype(low)
            value_grad = jnp.concatenate(values_t, axis=0).T.astype(low)
            d_qkv[:, at] = query_grad
            d_qkv[:, key_at] = (jnp.concatenate(keys_t, axis=0) * scale).T.astype(low)
            d_qkv[:, value_at] = value_grad
            small[3:4, at] += column_sum(query_grad.astype(f32))
            small[4:5, at] += column_sum(value_grad.astype(f32))

            @pl.when(step + slots < pairs_total)
            def _():
                probs_load(step + slots).start()

            return carry

        lax.fori_loop(0, heads2, attend, 0)
        for copy in own[:3]:
            copy.start()

        @pl.when(c == 0)
        def _():
            loads[3].wait()

        state[3].wait()
        for h in range(2):
            rows = pl.ds(h * half, half)

            def in_tile(j, carry):
                at = tile_of(j, 256)
                wide_grad[rows, at] = dot_nt(d_qkv[rows, :], wqkv[at, :])
                return carry

            lax.fori_loop(0, width // 256, in_tile, 0)

            def last_tile(i, carry):
                part = tile_of(i, 64)
                total = norm_back(x.at[c], d_middle[part, :], 0, 2, part, None)
                d_low[c, part, :] = total.astype(low)
                return carry

            lax.fori_loop(h * (half // 64), (h + 1) * (half // 64), last_tile, 0)

            @pl.when(section == 1)
            def _():
                send_half(c, h).start()

        dx_save(c).start()
        return carry

    lax.fori_loop(0, clips, clip, 0)
    for copy in saves(clips - 1):
        copy.wait()
    for c in range(clips):
        dx_save(c).wait()
        for h in range(2):
            @pl.when(section == 1)
            def _():
                send_half(c, h).wait_send()


def unit_rows(members, width, stack_rows):
    return math.gcd(stack_rows // members, width)


def grads_kernel(
    members, info, left, right, dx, feat, chosen, cols, small_in, up_sums, stats, stack_h, feat_grad,
    turned, result, embed, small, blank, unit_sem, embed_sem, small_sem,
):
    low = jnp.bfloat16
    f32 = jnp.float32
    b = pl.program_id(0)
    width = left.shape[2]
    total_rows = 12 * width
    unit = unit_rows(members, width, total_rows)
    share = total_rows // members
    per_block, per_member = width // unit, share // unit
    embed_share = embed.shape[0] // members

    def unit_copy(block, u):
        spot = block * per_block + u
        slot = lax.rem(block, 2)
        return pltpu.make_async_copy(
            result.at[slot, pl.ds(u * unit, unit)],
            stack_h.at[spot // per_member, pl.ds(pl.multiple_of(
                lax.rem(spot, per_member) * unit, 16), unit)],
            unit_sem.at[slot, u])

    @pl.when((b == 0) | (b == 3) | (b == 4) | ((b > 7) & (b < 12)))
    def _():
        def turn(i, carry):
            at = tile_of(i, 128)
            turned[at, :] = left[0, :, at].T
            return carry

        lax.fori_loop(0, width // 128, turn, 0)

    @pl.when(b < 12)
    def _():
        @pl.when(b > 1)
        def _():
            for u in range(per_block):
                unit_copy(b - 2, u).wait()

        def part(i, carry):
            at = tile_of(i, 128)
            result[lax.rem(b, 2), at, :] = dot_nn(turned[at, :], right[0]).astype(low)
            return carry

        lax.fori_loop(0, width // 128, part, 0)
        for u in range(per_block):
            unit_copy(b, u).start()

    @pl.when(b == 12)
    def _():
        for block in (10, 11):
            for u in range(per_block):
                unit_copy(block, u).wait()
        feat_width = feat.shape[2]
        first = info[2].astype(f32)
        clips = feat.shape[0]
        blank[...] = jnp.zeros_like(blank)
        small[...] = jnp.zeros_like(small)
        small[0:8, :] = small_in[...]
        for i in range(up_sums.shape[1] // width):
            small[8 + i : 9 + i, :] = up_sums[:, i * width : (i + 1) * width]
        lane = lax.broadcasted_iota(jnp.int32, (1, width), 1)
        row = jnp.zeros((1, width), f32)
        for i in range(3):
            row = jnp.where(lane == i, jnp.sum(stats[i : i + 1, :], axis=1, keepdims=True), row)
        count = jnp.zeros((1, 1), f32)
        for c in range(clips):
            count = count + jnp.sum(cols[c][:, 1:2], axis=0, keepdims=True)
        small[15:16, :] = jnp.where(lane == 3, count, row)
        weight_sum = [jnp.zeros((feat_width, width), f32)] * 2
        place_sum = jnp.zeros(dx.shape[1:], f32)
        for c in range(clips):
            grad = dx[c]
            kept = jnp.where(cols[c][:, 0:1] > 0.0, jnp.zeros_like(grad), grad)
            feat_grad[c] = dot_nt(kept, chosen[c]).astype(low)
            second = info[c].astype(f32)
            flags = ((1.0 - second) * first, second * first)
            wide = dot_nn(feat[c].T, kept)
            sums = column_sum(kept.astype(f32))
            for kind in range(2):
                weight_sum[kind] = weight_sum[kind] + flags[kind] * wide
                small[12 + kind : 13 + kind, :] += flags[kind] * sums
            small[14:15, :] += first * (column_sum(grad.astype(f32)) - sums)
            place_sum = place_sum + grad.astype(f32)
        embed[0:feat_width, :] = weight_sum[0].astype(low)
        embed[feat_width : 2 * feat_width, :] = weight_sum[1].astype(low)
        embed[2 * feat_width :, :] = (place_sum * first).astype(low)
        blank[0] = small[...].astype(low)
        copies = []
        for w in range(members):
            copies.append(pltpu.make_async_copy(
                embed.at[pl.ds(w * embed_share, embed_share)],
                stack_h.at[w, pl.ds(share, embed_share)], embed_sem.at[w]))
            copies.append(pltpu.make_async_copy(
                blank.at[min(w, 1)],
                stack_h.at[w, pl.ds(share + embed_share, SMALL)], small_sem.at[w]))
        for copy in copies:
            copy.start()
        for copy in copies:
            copy.wait()


def unpack_kernel(per_block, blocks, total, attend, project, up, down):
    b = pl.program_id(0) // per_block
    values = total[0].astype(jnp.float32)

    @pl.when(b < 3)
    def _():
        attend[...] = values

    @pl.when(b == 3)
    def _():
        project[...] = values

    @pl.when((b > 3) & (b < 4 + blocks))
    def _():
        up[...] = values

    @pl.when(b > 3 + blocks)
    def _():
        down[...] = values


ANY = pl.BlockSpec(memory_space=pl.ANY)
VMEM = pl.BlockSpec(memory_space=pltpu.VMEM)
SMEM = pl.BlockSpec(memory_space=pltpu.SMEM)
LOW = jnp.bfloat16
WIDE = jnp.float32


def shaped(kind, *dims):
    return jax.ShapeDtypeStruct(dims, kind)


def run_forward(features, chosen, pos_embed, weights, cols, kind_offset, mask_row, bias_row,
                live_row, gains, vectors, up_bias):
    clips, length, feat_width = features.shape
    width, feed = weights[2].shape
    blocks = feed // width
    dma = pltpu.SemaphoreType.DMA
    vm = pltpu.VMEM
    return pl.pallas_call(
        forward_kernel,
        out_shape=(
            shaped(LOW, 3 + blocks, clips * length, width),
            shaped(WIDE, clips, length, width),
            shaped(LOW, clips, length, 3 * width),
            shaped(LOW, clips, H, length, length),
            shaped(WIDE, clips, length, width),
            shaped(LOW, clips, length, feed),
            shaped(LOW, clips, length, width // 2),
            shaped(WIDE, 8, width),
        ),
        in_specs=[ANY] * 7 + [VMEM] * 8,
        out_specs=(ANY,) * 7 + (VMEM,),
        scratch_shapes=[
            vm(features.shape, LOW), vm(chosen.shape, LOW), vm(pos_embed.shape, WIDE),
            vm((width, 3 * width), LOW), vm((width, width), LOW), vm((width, feed), LOW),
            vm((feed, width), LOW),
            vm((length, width), WIDE), vm((length, width), LOW), vm((length, 3 * width), LOW),
            vm((2, 2, length, length), LOW), vm((length, width), LOW), vm((length, width), WIDE),
            vm((length, width), LOW), vm((length, feed), LOW), vm((length, feed), LOW),
            vm((clips, length, width), LOW), vm((clips, length, width), LOW),
            dma((7,)), dma((7 + blocks,)), dma((2,)), dma((clips, 2)), dma((clips, 2)),
            dma((clips, 2)), dma((clips, 2)), dma((clips, 2)),
        ],
        compiler_params=pltpu.CompilerParams(
            collective_id=1, has_side_effects=True, vmem_limit_bytes=56 * 2**20
        ),
    )(features, chosen, pos_embed, *weights, cols, kind_offset, mask_row, bias_row, live_row,
      gains, vectors, up_bias)


def run_backward(cotangent, weights, x, qkv, probs, middle, slope, gains):
    clips, length, width = cotangent.shape
    feed = weights[2].shape[1]
    blocks = feed // width
    dma = pltpu.SemaphoreType.DMA
    vm = pltpu.VMEM
    return pl.pallas_call(
        backward_kernel,
        out_shape=(
            shaped(LOW, 5 + blocks, clips * length, width),
            shaped(LOW, clips, length, width),
            shaped(WIDE, 8, width),
            shaped(WIDE, 1, feed),
        ),
        in_specs=[ANY] * 10 + [VMEM],
        out_specs=(ANY, ANY, VMEM, VMEM),
        scratch_shapes=[
            vm((width, 3 * width), LOW), vm((width, width), LOW), vm((width, feed), LOW),
            vm((feed, width), LOW),
            vm((clips, length, width), WIDE), vm((clips, length, 3 * width), LOW),
            vm((3, 2, length, length), LOW), vm((clips, length, width), WIDE),
            vm((clips, length, feed), LOW), vm((clips, length, width), LOW),
            vm((length, feed), LOW), vm((length, width), WIDE), vm((length, width), WIDE),
            vm((length, width), LOW), vm((length, width), LOW), vm((length, 3 * width), LOW),
            vm((clips, length, width), LOW),
            dma((4,)), dma((clips, 5)), dma((3,)), dma((5 + blocks,)), dma((clips,)),
            dma((clips, 2)), dma((clips, 2)),
        ],
        compiler_params=pltpu.CompilerParams(
            collective_id=2, has_side_effects=True, vmem_limit_bytes=60 * 2**20
        ),
    )(cotangent, *weights, x, qkv, probs, middle, slope, gains)


def run_grads(members, info, left, right, dx, features, chosen, cols, small, up_sums, stats):
    rows, width = left.shape[1:]
    clips, length, feat_width = features.shape
    embed_rows = 2 * feat_width + length
    total_rows = 12 * width
    share, embed_share = total_rows // members, embed_rows // members
    per_block = width // unit_rows(members, width, total_rows)
    dma = pltpu.SemaphoreType.DMA

    def whole(array):
        zeros = (0,) * array.ndim
        return pl.BlockSpec(array.shape, lambda b: zeros)

    def left_at(b):
        return (jnp.where(b < 3, 0, jnp.where(b == 3, 1, jnp.where(b < 8, 2, jnp.minimum(b, 11) - 5))), 0, 0)

    def right_at(b):
        return (jnp.minimum(b, 8), 0, 0)

    return pl.pallas_call(
        functools.partial(grads_kernel, members),
        grid=(13,),
        out_shape=(
            shaped(LOW, members, share + embed_share + SMALL, width),
            shaped(LOW, clips, length, feat_width),
        ),
        in_specs=[
            SMEM,
            pl.BlockSpec((1, rows, width), left_at),
            pl.BlockSpec((1, rows, width), right_at),
            whole(dx), whole(features), whole(chosen), whole(cols), whole(small), whole(up_sums),
            whole(stats),
        ],
        out_specs=(ANY, pl.BlockSpec((clips, length, feat_width), lambda b: (0, 0, 0))),
        scratch_shapes=[
            pltpu.VMEM((width, rows), LOW),
            pltpu.VMEM((2, width, width), LOW),
            pltpu.VMEM((embed_rows, width), LOW),
            pltpu.VMEM((SMALL, width), WIDE),
            pltpu.VMEM((2, SMALL, width), LOW),
            dma((2, per_block)), dma((members,)), dma((members,)),
        ],
        compiler_params=pltpu.CompilerParams(vmem_limit_bytes=56 * 2**20),
    )(info, left, right, dx, features, chosen, cols, small, up_sums, stats)


def ring_sum(stacked, tail, feature_grad):
    members, rows, width = stacked.shape
    clips, length, feat_width = feature_grad.shape
    n = members // 2
    dma = pltpu.SemaphoreType.DMA
    half = width // 2
    sems = [dma((2, 2, n)) for _ in range(9)]
    sems += [dma((2, 2)), dma((2, 2, n)), dma((2, 2, n)), dma((3,))]
    return pl.pallas_call(
        functools.partial(ring_kernel, n, rows, tail),
        out_shape=(
            shaped(LOW, members, rows, width),
            shaped(LOW, members, tail, width),
            shaped(LOW, clips, length, feat_width // 2),
        ),
        in_specs=[ANY, ANY],
        out_specs=(ANY, ANY, ANY),
        scratch_shapes=[
            pltpu.VMEM((2, n, rows, half), LOW),
            pltpu.VMEM((2, n, rows, half), LOW),
            pltpu.VMEM((2, n - 1, rows, half), LOW),
            sems,
        ],
        compiler_params=pltpu.CompilerParams(
            collective_id=0, has_side_effects=True, vmem_limit_bytes=48 * 2**20
        ),
    )(stacked, feature_grad)


def run_unpack(total, blocks):
    members, rows, width = total.shape
    unit = unit_rows(members, width, 12 * width)
    per_block, per_member = width // unit, 12 * width // members // unit

    def within(first, count):
        def at(u):
            return jnp.clip(u - first * per_block, 0, count * per_block - 1)
        return at

    attend, project, up, down = within(0, 3), within(3, 1), within(4, blocks), within(4 + blocks, blocks)

    def across(at):
        return lambda u: (at(u) % per_block, at(u) // per_block)

    return pl.pallas_call(
        functools.partial(unpack_kernel, per_block, blocks),
        grid=(12 * per_block,),
        out_shape=(
            shaped(WIDE, width, 3 * width), shaped(WIDE, width, width),
            shaped(WIDE, width, blocks * width), shaped(WIDE, blocks * width, width),
        ),
        in_specs=[pl.BlockSpec((1, unit, width), lambda u: (u // per_member, u % per_member, 0))],
        out_specs=(
            pl.BlockSpec((unit, width), across(attend)),
            pl.BlockSpec((unit, width), lambda u: (project(u), 0)),
            pl.BlockSpec((unit, width), across(up)),
            pl.BlockSpec((unit, width), lambda u: (down(u), 0)),
        ),
    )(total)


def local(
    features,
    masked,
    valid,
    kinds,
    embed_weight,
    embed_vectors,
    pos_embed,
    norm_gains,
    vectors,
    qkv_weight,
    out_weight,
    up_weight,
    up_bias,
    down_weight,
    cotangent,
):
    is_first = lax.axis_index("section") == 0
    members = lax.axis_size("wide")
    clips, length, feat_width = features.shape
    width = pos_embed.shape[1]
    weights = (qkv_weight[0], out_weight[0], up_weight[0], down_weight[0])
    blocks = up_weight.shape[2] // width
    chosen = jnp.where(kinds[:, None, None] == 0, embed_weight[0], embed_weight[1])
    kind_offset = jnp.where(kinds[:, None] == 0, embed_vectors[0], embed_vectors[1])[:, None]
    lane = jnp.arange(128)
    cols = jnp.where(
        lane == 0, masked[:, :, None], jnp.where(lane == 1, valid[:, :, None], 0)
    ).astype(WIDE)
    live_row = jnp.where(valid > 0, 0.0, NEG)[:, None]
    rows = vectors[0]
    bias_row = jnp.concatenate([rows[1], jnp.zeros((width,), WIDE), rows[2]])[None]
    left, x, qkv, probs, middle, slope, output, stats = run_forward(
        features, chosen, pos_embed, weights, cols, kind_offset, embed_vectors[2:3], bias_row,
        live_row, norm_gains[0], rows, up_bias)
    right, dx, small, up_sums = run_backward(
        cotangent, weights, x, qkv, probs, middle, slope, norm_gains[0])
    info = jnp.concatenate([kinds, is_first.astype(jnp.int32)[None]])
    stacked, feature_grad = run_grads(
        members, info, left, right, dx, features, chosen, cols, small, up_sums, stats)
    embed_share = (2 * feat_width + length) // members
    tail = embed_share + SMALL
    total, cross, feature_out = ring_sum(stacked, tail, feature_grad)
    attend_total, project_total, up_total, down_total = run_unpack(total, blocks)
    ends = jnp.where(is_first, total[:, -tail:], cross)
    embed_total = ends[:, :embed_share].reshape(-1, width).astype(WIDE)
    small_total = total[0, -SMALL:].astype(WIDE)
    stat_row = small_total[15]
    rms_out = jnp.sqrt(stat_row[0:3] / (stat_row[3] * width))[None]
    return (
        output,
        feature_out,
        embed_total[: 2 * feat_width].reshape(2, feat_width, width),
        ends[0, embed_share + 12 : embed_share + 15].astype(WIDE),
        embed_total[2 * feat_width :],
        small_total[None, 0:2],
        small_total[None, 2:8],
        attend_total[None],
        project_total[None],
        up_total[None],
        small_total[8 : 8 + blocks].reshape(1, -1),
        down_total[None],
        rms_out,
    )


def solution(mesh):
    return jax.shard_map(
        local,
        mesh=mesh,
        in_specs=(
            P("wide", None, None),
            P("wide", None),
            P("wide", None),
            P("wide"),
            P(),
            P(),
            P(),
            P("section", None, None),
            P("section", None, None),
            P("section", None, None),
            P("section", None, None),
            P("section", None, None),
            P("section", None),
            P("section", None, None),
            P("wide", None, None),
        ),
        out_specs=(
            P("wide", None, "section"),
            P("wide", None, "section"),
            P(),
            P(),
            P(),
            P("section", None, None),
            P("section", None, None),
            P("section", None, None),
            P("section", None, None),
            P("section", None, None),
            P("section", None),
            P("section", None, None),
            P("section", None),
        ),
        check_vma=False,
    )
```

```python
import functools
import math

import jax
import jax.numpy as jnp
from jax import lax
from jax.experimental import pallas as pl
from jax.experimental.pallas import tpu as pltpu
from jax.sharding import PartitionSpec as P

H = 12
HD = 64
EPS = 1e-06
NEG = -1000000000.0


MESH = pl.DeviceIdType.MESH
SMALL = 16


def unit_rows(members, width):
    return math.gcd(12 * width // members, width)


def dot_nn(left, right):
    return jnp.dot(left, right, preferred_element_type=jnp.float32)


def dot_nt(left, right):
    return lax.dot_general(
        left, right, (((1,), (1,)), ((), ())), preferred_element_type=jnp.float32
    )


def tile_of(index, size):
    return pl.ds(pl.multiple_of(index * size, size), size)


def loop(count, body, unroll):
    def step(i, carry):
        for u in range(unroll):
            body(i * unroll + u, 0)
        return carry

    lax.fori_loop(0, count // unroll, step, 0)


def column_sum(values):
    return jnp.sum(values, axis=0, keepdims=True)


def row_mean(values):
    return jnp.mean(values, axis=-1, keepdims=True)


def gelu_pair(hidden):
    decay = jnp.exp(-0.5 * hidden * hidden)
    t = 1.0 / (1.0 + (0.3275911 * 0.5**0.5) * jnp.abs(hidden))
    poly = 1.061405429 * 0.5
    for term in (-1.453152027, 1.421413741, -0.284496736, 0.254829592):
        poly = poly * t + 0.5 * term
    upper = poly * t * decay
    cdf = jnp.where(hidden > 0.0, 1.0 - upper, upper)
    return hidden * cdf, cdf + hidden * decay * 0.3989422804014327


def fetch(pairs, sems):
    copies = [pltpu.make_async_copy(src, dst, sems.at[i]) for i, (src, dst) in enumerate(pairs)]
    for copy in copies:
        copy.start()
    return copies


def greet_partner():
    barrier = pltpu.get_barrier_semaphore()
    pl.semaphore_signal(
        barrier, inc=1, device_id={"section": 1 - lax.axis_index("section")}, device_id_type=MESH
    )
    pl.semaphore_wait(barrier, 1)


def to_partner(src, dst, send, recv):
    return pltpu.make_async_remote_copy(
        src_ref=src, dst_ref=dst, send_sem=send, recv_sem=recv,
        device_id={"section": 1 - lax.axis_index("section")}, device_id_type=MESH)


def forward_kernel(
    feat_h, chosen_h, pos_h, wqkv_h, wout_h, wup_h, wdown_h,
    cols, kind_offset, mask_row, bias_row, live_row, gains, vectors, up_bias,
    left_h, x_h, qkv_h, probs_h, middle_h, slope_h, out_h, stats,
    feat, chosen, pos, wqkv, wout, wup, wdown,
    x, normed, qkv, probs, context, middle, hidden_in, active, slope, y, landed,
    load_sem, save_sem, probs_sem, send_sem, recv_sem, back_send, back_recv, keep_sem,
):
    low = jnp.bfloat16
    section = lax.axis_index("section")
    clips, length, width = landed.shape
    half = length // 2
    feed = wup.shape[1]
    heads2 = width // 128
    blocks = feed // width
    greet_partner()
    loads = fetch(
        [(feat_h, feat), (chosen_h, chosen), (pos_h, pos), (wqkv_h, wqkv), (wout_h, wout),
         (wup_h, wup), (wdown_h, wdown)], load_sem)
    stats[...] = jnp.zeros_like(stats)
    low_lanes = lax.broadcasted_iota(jnp.int32, (1, 128), 1) < HD

    def save(index, src, dst):
        return pltpu.make_async_copy(src, dst, save_sem.at[index])

    def saves(c):
        rows = pl.ds(pl.multiple_of(c * length, length), length)
        pairs = [
            (x, x_h.at[c]), (normed, left_h.at[0, rows]), (qkv, qkv_h.at[c]),
            (context, left_h.at[1, rows]), (middle, middle_h.at[c]),
            (hidden_in, left_h.at[2, rows]), (slope, slope_h.at[c]),
        ] + [
            (active.at[:, pl.ds(b * width, width)], left_h.at[3 + b, rows]) for b in range(blocks)
        ]
        return [save(i, src, dst) for i, (src, dst) in enumerate(pairs)]

    def probs_save(c, pair):
        slot = lax.rem(pair, 2)
        return pltpu.make_async_copy(
            probs.at[slot], probs_h.at[c, pl.ds(pair * 2, 2)], probs_sem.at[slot])

    def send_half(c, h):
        rows = pl.ds(h * half, half)
        return to_partner(
            y.at[c, rows], landed.at[c, rows], send_sem.at[c, h], recv_sem.at[c, h])

    def back_half(c, h):
        rows = pl.ds(h * half, half)
        return to_partner(
            y.at[c, rows, pl.ds(0, width // 2)], out_h.at[c, rows],
            back_send.at[c, h], back_recv.at[c, h])

    def keep_half(c, h):
        rows = pl.ds(h * half, half)
        return pltpu.make_async_copy(
            y.at[c, rows, pl.ds(width // 2, width // 2)], out_h.at[c, rows], keep_sem.at[c, h])

    def clip(c, carry):
        def after_first(index):
            @pl.when(c > 0)
            def _():
                saves(c - 1)[index].wait()

        after_first(0)
        after_first(1)

        @pl.when(section == 0)
        def _():
            @pl.when(c == 0)
            def _():
                for copy in loads[:3]:
                    copy.wait()

            def tile(i, carry):
                rows = tile_of(i, 128)
                lifted = dot_nn(feat[c, rows, :], chosen[c]) + kind_offset[c]
                hidden = cols[c, rows, :][:, 0:1]
                x[rows, :] = jnp.where(hidden > 0.0, mask_row[...], lifted) + pos[rows, :]
                return carry

            loop(length // 128, tile, 4)

        @pl.when(section == 1)
        def _():
            @pl.when(c == 0)
            def _():
                for copy in loads[:3]:
                    copy.wait()

            for h in range(2):
                send_half(c, h).wait_recv()

            def tile(i, carry):
                rows = tile_of(i, 64)
                x[rows, :] = landed[c, rows, :].astype(jnp.float32)
                return carry

            loop(length // 64, tile, 4)

        own = saves(c)
        own[0].start()

        def norm_rows(source, target, which, shift, first, count):
            gain, offset = gains[which : which + 1, :], vectors[shift : shift + 1, :]

            def tile(i, carry):
                rows = tile_of(i, 64)
                values = source[rows, :]
                values = values - row_mean(values)
                scale = lax.rsqrt(row_mean(values * values) + EPS)
                target[rows, :] = (values * scale * gain + offset).astype(low)
                return carry

            loop(count, lambda i, carry: tile(first + i, carry), 4)

        norm_rows(x, normed, 0, 0, 0, length // 64)
        own[1].start()
        after_first(2)

        @pl.when(c == 0)
        def _():
            loads[3].wait()

        def qkv_tile(j, carry):
            at = tile_of(j, 256)
            qkv[:, at] = (dot_nn(normed[...], wqkv[:, at]) + bias_row[:, at]).astype(low)
            return carry

        loop(3 * width // 256, qkv_tile, 9)
        own[2].start()
        after_first(3)

        def attend(pair, carry):
            @pl.when((pair > 1) | (c > 0))
            def _():
                probs_save(c, pair).wait()

            at = tile_of(pair, 128)
            queries = qkv[:, at]
            keys_in = qkv[:, tile_of(pair + heads2, 128)]
            values_in = qkv[:, tile_of(pair + 2 * heads2, 128)]
            outs = []
            for h in range(2):
                pick = jnp.where(low_lanes == (h == 0), HD**-0.5, 0.0).astype(low)
                scores = dot_nt(queries * pick, keys_in) + live_row[c]
                top = jnp.max(scores, axis=-1, keepdims=True)
                scores = jnp.exp(scores - top)
                total = jnp.sum(scores, axis=-1, keepdims=True)
                soft = (scores * (1.0 / total)).astype(low)
                probs[lax.rem(pair, 2), h] = soft
                outs.append(dot_nn(soft, values_in))
            context[:, at] = jnp.where(low_lanes, outs[0], outs[1]).astype(low)
            probs_save(c, pair).start()
            return carry

        lax.fori_loop(0, heads2, attend, 0)
        own[3].start()
        after_first(4)

        @pl.when(c == 0)
        def _():
            loads[4].wait()

        live = cols[c][:, 1:2]

        def out_tile(j, carry):
            at = tile_of(j, 256)
            branch = dot_nn(context[...], wout[:, at]) + vectors[3:4, at]
            middle[:, at] = x[:, at] + branch
            stats[1:2, at] += column_sum(branch * branch * live)
            return carry

        loop(width // 256, out_tile, 3)
        own[4].start()
        for index in range(5, 7 + blocks):
            after_first(index)

        @pl.when(c == 0)
        def _():
            loads[5].wait()
            loads[6].wait()

        for h in range(2):
            rows = pl.ds(h * half, half)
            norm_rows(middle, hidden_in, 1, 4, h * (half // 64), half // 64)
            if h == 1:
                own[5].start()

            def up_tile(j, carry):
                at = tile_of(j, 256)
                hidden = dot_nn(hidden_in[rows, :], wup[:, at]) + up_bias[:, at]
                value, steep = gelu_pair(hidden)
                active[rows, at] = value.astype(low)
                slope[rows, at] = steep.astype(low)
                return carry

            loop(feed // 256, up_tile, 6)
            if h == 1:
                for copy in own[6:]:
                    copy.start()

            def down_tile(j, carry):
                at = tile_of(j, 256)
                mixer = dot_nn(active[rows, :], wdown[:, at]) + vectors[5:6, at]
                total = middle[rows, at] + mixer
                flags = cols[c, rows, :][:, 1:2]
                stats[0:1, at] += column_sum(total * total * flags)
                stats[2:3, at] += column_sum(mixer * mixer * flags)
                y[c, rows, at] = total.astype(low)
                return carry

            loop(width // 256, down_tile, 3)

            @pl.when(section == 0)
            def _():
                send_half(c, h).start()

            @pl.when(section == 1)
            def _():
                back_half(c, h).start()
                keep_half(c, h).start()
        return carry

    lax.fori_loop(0, clips, clip, 0)
    for pair in (heads2 - 2, heads2 - 1):
        probs_save(clips - 1, pair).wait()
    for copy in saves(clips - 1):
        copy.wait()
    for c in range(clips):
        for h in range(2):
            @pl.when(section == 0)
            def _():
                send_half(c, h).wait_send()
                back_half(c, h).wait_recv()

            @pl.when(section == 1)
            def _():
                back_half(c, h).wait_send()
                keep_half(c, h).wait()


def backward_kernel(
    cot_h, wqkv_h, wout_h, wup_h, wdown_h, x_h, qkv_h, probs_h, middle_h, slope_h, left_h, gains,
    right_h, dx_h, turned_h, small, up_sums,
    wqkv, wout, wup, wdown, x, qkv, probs, middle, slope, g,
    d_hidden, wide_grad, d_middle, d_branch, d_context, d_qkv, d_low, upright, turned,
    turn_sem, load_sem, state_sem, probs_sem, save_sem, dx_sem, send_sem, recv_sem,
):
    low = jnp.bfloat16
    f32 = jnp.float32
    section = lax.axis_index("section")
    clips, length, width = g.shape
    half = length // 2
    feed = wup.shape[1]
    heads2 = width // 128
    blocks = feed // width
    greet_partner()

    def cot_load(c):
        return pltpu.make_async_copy(cot_h.at[c], g.at[c], state_sem.at[c, 0])

    def state_loads(c):
        pairs = [(slope_h, slope), (middle_h, middle), (qkv_h, qkv), (x_h, x)]
        return [
            pltpu.make_async_copy(src.at[c], dst.at[c], state_sem.at[c, 1 + i])
            for i, (src, dst) in enumerate(pairs)
        ]

    @pl.when(section == 1)
    def _():
        cot_load(0).start()

    loads = fetch([(wdown_h, wdown), (wup_h, wup), (wout_h, wout), (wqkv_h, wqkv)], load_sem)
    for c in range(clips):
        for copy in state_loads(c):
            copy.start()

    @pl.when(section == 1)
    def _():
        for c in range(1, clips):
            cot_load(c).start()

    small[...] = jnp.zeros_like(small)
    up_sums[...] = jnp.zeros_like(up_sums)
    low_lanes = lax.broadcasted_iota(jnp.int32, (1, 128), 1) < HD
    slots = probs.shape[0]
    pairs_total = clips * heads2

    def probs_load(step):
        slot = lax.rem(step, slots)
        return pltpu.make_async_copy(
            probs_h.at[step // heads2, pl.ds(lax.rem(step, heads2) * 2, 2)],
            probs.at[slot], probs_sem.at[slot])

    for step in range(slots):
        probs_load(step).start()

    def saves(c):
        rows = pl.ds(pl.multiple_of(c * length, length), length)
        pairs = [(d_qkv.at[:, pl.ds(b * width, width)], right_h.at[b, rows]) for b in range(3)]
        pairs += [(d_branch, right_h.at[3, rows])]
        pairs += [
            (d_hidden.at[:, pl.ds(b * width, width)], right_h.at[4 + b, rows])
            for b in range(blocks)
        ]
        pairs += [(g.at[c], right_h.at[4 + blocks, rows])]
        return [pltpu.make_async_copy(s, d, save_sem.at[i]) for i, (s, d) in enumerate(pairs)]

    def send_half(c, h):
        rows = pl.ds(h * half, half)
        return to_partner(
            d_low.at[c, rows], g.at[c, rows], send_sem.at[c, h], recv_sem.at[c, h])

    def dx_save(c):
        return pltpu.make_async_copy(d_low.at[c], dx_h.at[c], dx_sem.at[c])

    def norm_back(source, carried, which, shift_row, rows, take):
        gain = gains[which : which + 1, :]
        values = source[rows, :]
        values = values - row_mean(values)
        scale = lax.rsqrt(row_mean(values * values) + EPS)
        values = values * scale
        grad = wide_grad[rows, :]
        small[which : which + 1, :] += column_sum(grad * values)
        small[shift_row : shift_row + 1, :] += column_sum(grad)
        grad = grad * gain
        return carried + scale * (grad - row_mean(grad) - values * row_mean(grad * values))

    def turn_lefts():
        def block(b, carry):
            come = pltpu.make_async_copy(left_h.at[b], upright, turn_sem.at[0])
            come.start()
            come.wait()

            def piece(i, carry):
                at = tile_of(i, 128)
                turned[at, :] = upright[:, at].T
                return carry

            loop(width // 128, piece, 2)
            leave = pltpu.make_async_copy(turned, turned_h.at[b], turn_sem.at[1])
            leave.start()
            leave.wait()
            return carry

        lax.fori_loop(0, left_h.shape[0], block, 0)

    @pl.when(section == 0)
    def _():
        turn_lefts()

    def clip(c, carry):
        def after_first(lo, hi):
            @pl.when(c > 0)
            def _():
                for copy in saves(c - 1)[lo:hi]:
                    copy.wait()

        after_first(4, 5 + blocks)

        @pl.when(section == 1)
        def _():
            cot_load(c).wait()

        state = state_loads(c)
        own = saves(c)

        @pl.when(c == 0)
        def _():
            loads[0].wait()
            loads[1].wait()

        state[0].wait()
        state[1].wait()
        for h in range(2):
            rows = pl.ds(h * half, half)

            @pl.when(section == 0)
            def _():
                send_half(c, h).wait_recv()

            if h == 1:
                own[-1].start()

            def feed_tile(j, carry):
                at = tile_of(j, 256)
                d_active = dot_nt(g[c, rows, :], wdown[at, :])
                grad = (slope[c, rows, at].astype(f32) * d_active).astype(low)
                d_hidden[rows, at] = grad
                up_sums[:, at] += column_sum(grad.astype(f32))
                return carry

            loop(feed // 256, feed_tile, 6)

            def in_tile(j, carry):
                at = tile_of(j, 256)
                wide_grad[rows, at] = dot_nt(d_hidden[rows, :], wup[at, :])
                return carry

            loop(width // 256, in_tile, 3)

        after_first(3, 4)
        for copy in own[4:-1]:
            copy.start()

        def middle_tile(i, carry):
            rows = tile_of(i, 64)
            grad_in = g[c, rows, :].astype(f32)
            total = norm_back(middle.at[c], grad_in, 1, 6, rows, None)
            d_middle[rows, :] = total
            rounded = total.astype(low)
            d_branch[rows, :] = rounded
            small[5:6, :] += column_sum(rounded.astype(f32))
            small[7:8, :] += column_sum(grad_in)
            return carry

        loop(length // 64, middle_tile, 4)
        own[3].start()

        @pl.when(c == 0)
        def _():
            loads[2].wait()

        def context_tile(j, carry):
            at = tile_of(j, 256)
            d_context[:, at] = dot_nt(d_branch[...], wout[at, :]).astype(low)
            return carry

        loop(width // 256, context_tile, 3)
        state[2].wait()
        after_first(0, 3)

        def attend(pair, carry):
            step = c * heads2 + pair
            slot = lax.rem(step, slots)
            probs_load(step).wait()
            at, key_at = tile_of(pair, 128), tile_of(pair + heads2, 128)
            value_at = tile_of(pair + 2 * heads2, 128)
            queries, keys_in, values_in = qkv[c, :, at], qkv[c, :, key_at], qkv[c, :, value_at]
            grad = d_context[:, at]
            queries_t, grad_t = queries.T, grad.T
            d_queries, keys_t, values_t = [], [], []
            for h in range(2):
                pick = jnp.where(low_lanes == (h == 0), 1.0, 0.0).astype(low)
                soft = probs[slot, h]
                soft_wide = soft.astype(f32)
                d_soft = dot_nt(grad * pick, values_in)
                delta = jnp.sum(soft_wide * d_soft, axis=-1, keepdims=True)
                d_scores = (soft_wide * (d_soft - delta)).astype(low)
                part = slice(h * HD, (h + 1) * HD)
                values_t.append(dot_nn(grad_t[part], soft))
                keys_t.append(dot_nn(queries_t[part], d_scores))
                d_queries.append(dot_nn(d_scores, keys_in))
            scale = HD**-0.5
            query_grad = (jnp.where(low_lanes, d_queries[0], d_queries[1]) * scale).astype(low)
            value_grad = jnp.concatenate(values_t, axis=0).T.astype(low)
            d_qkv[:, at] = query_grad
            d_qkv[:, key_at] = (jnp.concatenate(keys_t, axis=0) * scale).T.astype(low)
            d_qkv[:, value_at] = value_grad
            small[3:4, at] += column_sum(query_grad.astype(f32))
            small[4:5, at] += column_sum(value_grad.astype(f32))

            @pl.when(step + slots < pairs_total)
            def _():
                probs_load(step + slots).start()

            return carry

        lax.fori_loop(0, heads2, attend, 0)
        for copy in own[:3]:
            copy.start()

        @pl.when(c == 0)
        def _():
            loads[3].wait()

        state[3].wait()
        for h in range(2):
            rows = pl.ds(h * half, half)

            def in_tile(j, carry):
                at = tile_of(j, 256)
                wide_grad[rows, at] = dot_nt(d_qkv[rows, :], wqkv[at, :])
                return carry

            loop(width // 256, in_tile, 3)

            def last_tile(i, carry):
                part = tile_of(i, 64)
                total = norm_back(x.at[c], d_middle[part, :], 0, 2, part, None)
                d_low[c, part, :] = total.astype(low)
                return carry

            loop(half // 64, lambda i, carry: last_tile(h * (half // 64) + i, carry), 4)

            @pl.when(section == 1)
            def _():
                send_half(c, h).start()

        dx_save(c).start()
        return carry

    lax.fori_loop(0, clips, clip, 0)

    @pl.when(section == 1)
    def _():
        turn_lefts()

    for copy in saves(clips - 1):
        copy.wait()
    for c in range(clips):
        dx_save(c).wait()
        for h in range(2):
            @pl.when(section == 1)
            def _():
                send_half(c, h).wait_send()


def sums_kernel(
    members, info, turned_h, right_h, dx_h, feat_h, chosen_h, cols, small_in, up_sums, stats,
    o_ref, t_ref, e_ref, h_ref,
    lefts, rights, own, spare, part, ring, tails, tail_own, tail_part, tail_ring,
    dx, feat, chosen, feat_grad, embed, small, sems,
):
    (load_sem, embed_sem, part_send, part_recv, ring_send, ring_recv, gather_send, gather_recv,
     pair_send, pair_recv, keep_sem, cross_send, cross_recv, feat_sem) = sems
    low = jnp.bfloat16
    f32 = jnp.float32
    n = members // 2
    share, columns = own.shape[2:]
    width = 2 * columns
    tail = tails.shape[1]
    unit = unit_rows(members, width)
    per_block, per_member = width // unit, share // unit
    slots = own.shape[1]
    clips, length, feat_width = feat.shape
    me = lax.axis_index("wide")
    section = lax.axis_index("section")
    chip, core = me // 2, me % 2
    place = jnp.where(chip % 2 == 0, chip // 2, n - 1 - chip // 2)

    def member_at(position):
        position = lax.rem(position + 2 * n, n)
        return jnp.where(2 * position < n, 2 * position, 2 * (n - 1 - position) + 1) * 2 + core

    right, left = member_at(place + 1), member_at(place - 1)
    other = chip * 2 + 1 - core
    target = (right, left)

    barrier = pltpu.get_barrier_semaphore()
    for peer in (right, left, other):
        pl.semaphore_signal(barrier, inc=1, device_id={"wide": peer}, device_id_type=MESH)
    pl.semaphore_signal(barrier, inc=1, device_id={"section": 1 - section}, device_id_type=MESH)

    half = -(-share // 32) * 16
    spans = ((0, half), (half, share - half))
    mains = [(q, d) for q in range(2) for d in range(2)]
    streams = mains + [(2, 0), (2, 1)]

    def turn(position):
        return lax.rem(position + 2 * n, n)

    def reduce_at(d, step):
        return turn(place - step) if d == 0 else turn(place + step)

    def gather_at(d, index):
        return turn(place + 1 - index) if d == 0 else turn(place - 1 + index)

    def span(q):
        return pl.ds(*spans[q])

    def cols_of(d):
        return pl.ds(d * columns, columns)

    def remote(src, dst, send, recv, device):
        return pltpu.make_async_remote_copy(
            src_ref=src, dst_ref=dst, send_sem=send, recv_sem=recv,
            device_id=device, device_id_type=MESH)

    def block_of(spot):
        return spot // per_block

    def operand_copies(d, s):
        base = reduce_at(d, s) * 2 * per_member
        first, second = block_of(base), block_of(base + 2 * per_member - 1)
        copies = []
        for u in range(2 * per_member):
            block = block_of(base + u)
            source = jnp.where(
                block < 3, 0, jnp.where(block == 3, 1, jnp.where(block < 8, 2, block - 5)))
            row = pl.multiple_of(lax.rem(base + u, per_block) * unit, 16)
            copies.append(pltpu.make_async_copy(
                turned_h.at[source, pl.ds(row, unit)], lefts.at[d, u], load_sem.at[d, u]))
        for i, block in enumerate((first, second)):
            copies.append(pltpu.make_async_copy(
                right_h.at[jnp.minimum(block, 8), :, cols_of(d)], rights.at[d, i],
                load_sem.at[d, 2 * per_member + i]))
        return copies

    def load_operands(d, s):
        for copy in operand_copies(d, s):
            copy.start()

    def part_copy(d, s):
        return remote(
            spare.at[d, lax.rem(s, 2)], part.at[d, s], part_send.at[d, s], part_recv.at[d, s],
            {"wide": other})

    def ring_copy(q, d, s):
        if q == 2:
            src, dst = tail_own.at[d, s], tail_ring.at[d, s]
        else:
            src, dst = own.at[d, lax.rem(s, slots), span(q)], ring.at[d, s, span(q)]
        return remote(src, dst, ring_send.at[d, q, s], ring_recv.at[d, q, s],
                      {"wide": target[d]})

    def products(d, s, prefetch):
        for copy in operand_copies(d, s):
            copy.wait()
        base = reduce_at(d, s) * 2 * per_member
        first = block_of(base)

        def side(which, store):
            def body(u, carry):
                spot = which * per_member + u
                tile = dot_nn(lefts[d, spot], rights[d, block_of(base + spot) - first])
                store(pl.ds(pl.multiple_of(u * unit, 16), unit), tile.astype(low))
                return carry

            lax.fori_loop(0, per_member, body, 0)

        def store_spare(rows, tile):
            spare[d, lax.rem(s, 2), rows, :] = tile

        def store_own(rows, tile):
            own[d, lax.rem(s, slots), rows, :] = tile

        side(1 - core, store_spare)
        part_copy(d, s).start()
        side(core, store_own)
        prefetch()

    def final_of(q, d):
        return tail_own.at[d, n - 1] if q == 2 else own.at[d, (n - 1) % slots, span(q)]

    def spot_of(q, d, index, which):
        member = gather_at(d, index) * 2 + which
        if q == 2:
            return t_ref.at[member, :, cols_of(d)]
        return o_ref.at[member, span(q), cols_of(d)]

    def gather_copy(q, d, index, first=False):
        src = final_of(q, d) if first else spot_of(q, d, index, core)
        return remote(
            src, spot_of(q, d, index, core),
            gather_send.at[d, q, index], gather_recv.at[d, q, index], {"wide": target[d]})

    def gather_landed(q, d, index):
        return remote(
            final_of(q, d), spot_of(q, d, index + 1, core),
            gather_send.at[d, q, index], gather_recv.at[d, q, index], {"wide": target[d]})

    def pair_copy(q, d, index, first=False):
        src = final_of(q, d) if first else spot_of(q, d, index, core)
        return remote(
            src, spot_of(q, d, index, core),
            pair_send.at[d, q, index], pair_recv.at[d, q, index], {"wide": other})

    def pair_landed(q, d, index):
        return remote(
            final_of(q, d), spot_of(q, d, index, 1 - core),
            pair_send.at[d, q, index], pair_recv.at[d, q, index], {"wide": other})

    def keep_copy(q, d):
        return pltpu.make_async_copy(final_of(q, d), spot_of(q, d, 0, core), keep_sem.at[d, q])

    def cross_copy(d, index, mine, first=False):
        member = gather_at(d, index) * 2 + (core if mine else 1 - core)
        src = final_of(2, d) if first else t_ref.at[member, :, cols_of(d)]
        lane = 0 if mine else 1
        return remote(
            src, e_ref.at[member, :, cols_of(d)],
            cross_send.at[d, lane, index], cross_recv.at[d, lane, index],
            {"section": 1 - section})

    def hand_over(q, d):
        gather_copy(q, d, 0, True).start()
        pair_copy(q, d, 0, True).start()
        keep_copy(q, d).start()
        if q == 2:
            @pl.when(section == 0)
            def _():
                cross_copy(d, 0, True, True).start()

    def reduce_main(q, d, s, begin=False, end=False):
        if not begin:
            ring_copy(q, d, s - 1).wait_recv()

        def add(tile, carry):
            at = pl.ds(pl.multiple_of(spans[q][0] + tile * 16, 16), 16)
            slot = lax.rem(s, slots)
            total = own[d, slot, at].astype(f32) + part[d, s, at].astype(f32)
            if not begin:
                total = total + ring[d, s - 1, at].astype(f32)
            own[d, slot, at] = total.astype(low)
            return carry

        loop(spans[q][1] // 16, add, 1)
        if end:
            hand_over(q, d)
        else:
            ring_copy(q, d, s).start()

    def tail_part_copy(d, s):
        return remote(
            tails.at[reduce_at(d, s) * 2 + 1 - core, :, cols_of(d)], tail_part.at[d, s],
            part_send.at[d, n + s], part_recv.at[d, n + s], {"wide": other})

    def reduce_tail(d, s, begin=False, end=False):
        tail_part_copy(d, s).wait_recv()
        total = tails[reduce_at(d, s) * 2 + core, :, cols_of(d)].astype(f32)
        total = total + tail_part[d, s].astype(f32)
        if not begin:
            ring_copy(2, d, s - 1).wait_recv()
            total = total + tail_ring[d, s - 1].astype(f32)
        tail_own[d, s] = total.astype(low)
        if end:
            hand_over(2, d)
        else:
            ring_copy(2, d, s).start()

    feat_half = h_ref.shape[2]
    feat_keep = pltpu.make_async_copy(
        feat_grad.at[:, :, pl.ds(0, feat_half)], h_ref, feat_sem.at[0])
    feat_send = remote(
        feat_grad.at[:, :, pl.ds(feat_half, feat_half)], h_ref, feat_sem.at[1], feat_sem.at[2],
        {"section": 1 - section})

    def embed_back():
        first = (1 - section).astype(f32)
        small[...] = jnp.zeros_like(small)
        small[0:8, :] = small_in[...]
        for i in range(up_sums.shape[1] // width):
            small[8 + i : 9 + i, :] = up_sums[:, i * width : (i + 1) * width]
        lane = lax.broadcasted_iota(jnp.int32, (1, width), 1)
        row = jnp.zeros((1, width), f32)
        for i in range(3):
            row = jnp.where(lane == i, jnp.sum(stats[i : i + 1, :], axis=1, keepdims=True), row)
        count = jnp.zeros((1, 1), f32)
        for c in range(clips):
            count = count + jnp.sum(cols[c][:, 1:2], axis=0, keepdims=True)
        small[15:16, :] = jnp.where(lane == 3, count, row)
        embed[...] = jnp.zeros_like(embed)

        @pl.when(section == 0)
        def _():
            weight_sum = [jnp.zeros((feat_width, width), f32)] * 2
            place_sum = jnp.zeros((length, width), f32)
            for c in range(clips):
                grad = dx[c]
                kept = jnp.where(cols[c][:, 0:1] > 0.0, jnp.zeros_like(grad), grad)
                feat_grad[c] = dot_nt(kept, chosen[c]).astype(low)
                second = info[c].astype(f32)
                flags = (1.0 - second, second)
                wide = dot_nn(feat[c].T, kept)
                sums = column_sum(kept.astype(f32))
                for kind in range(2):
                    weight_sum[kind] = weight_sum[kind] + flags[kind] * wide
                    small[12 + kind : 13 + kind, :] += flags[kind] * sums
                small[14:15, :] += column_sum(grad.astype(f32)) - sums
                place_sum = place_sum + grad.astype(f32)
            embed[0:feat_width, :] = weight_sum[0].astype(low)
            embed[feat_width : 2 * feat_width, :] = weight_sum[1].astype(low)
            embed[2 * feat_width :, :] = place_sum.astype(low)
            feat_keep.start()
            feat_send.start()

        embed_share = tail - SMALL
        for w in range(members):
            tails[w, 0:embed_share, :] = embed[w * embed_share : (w + 1) * embed_share, :]
            if w == 0:
                tails[w, embed_share:, :] = small[...].astype(low)
            else:
                tails[w, embed_share:, :] = jnp.zeros((SMALL, width), low)

    embed_loads = [
        pltpu.make_async_copy(src, dst, embed_sem.at[i])
        for i, (src, dst) in enumerate(((dx_h, dx), (feat_h, feat), (chosen_h, chosen)))
    ]

    for d in range(2):
        load_operands(d, 0)
    for copy in embed_loads:
        copy.start()
    pl.semaphore_wait(barrier, 4)
    for d in range(2):
        products(d, 0, functools.partial(load_operands, d, 1))
    for d in range(2):
        part_copy(d, 0).wait_recv()
        for q in range(2):
            reduce_main(q, d, 0, begin=True)

    def prefetch_after(d, s):
        @pl.when(s < n)
        def _():
            load_operands(d, s)

    for d in range(2):
        products(d, 1, functools.partial(prefetch_after, d, 2))
    for copy in embed_loads:
        copy.wait()
    embed_back()

    def send_tails(s, carry):
        for d in range(2):
            tail_part_copy(d, s).start()
        return carry

    lax.fori_loop(0, n, send_tails, 0)

    def scatter_step(s, carry):
        for q in range(2):
            for d in range(2):
                if q == 0:
                    part_copy(d, s).wait_recv()
                reduce_main(q, d, s)

        for d in range(2):
            @pl.when(s > 0)
            def _():
                part_copy(d, s - 1).wait_send()

            @pl.when(s > 1)
            def _():
                for q in range(2):
                    ring_copy(q, d, s - 2).wait_send()

            products(d, s + 1, functools.partial(prefetch_after, d, s + 2))

        for d in range(2):
            @pl.when(s == 1)
            def _():
                reduce_tail(d, 0, begin=True)

            @pl.when(s > 1)
            def _():
                reduce_tail(d, s - 1)
        return carry

    lax.fori_loop(1, n - 1, scatter_step, 0)
    for q in range(2):
        for d in range(2):
            if q == 0:
                part_copy(d, n - 1).wait_recv()
            reduce_main(q, d, n - 1, end=True)
    for d in range(2):
        reduce_tail(d, n - 2, begin=n == 2)

    def gather_step(q, d, t):
        gather_landed(q, d, t).wait_recv()

        @pl.when(t < n - 2)
        def _():
            gather_copy(q, d, t + 1).start()

        pair_copy(q, d, t + 1).start()
        if q == 2:
            @pl.when(section == 0)
            def _():
                cross_copy(d, t + 1, True).start()

    def pass_pair(d, t):
        pair_landed(2, d, t).wait_recv()

        @pl.when(section == 0)
        def _():
            cross_copy(d, t, False).start()

    for q, d in mains:
        gather_step(q, d, 0)
    for d in range(2):
        reduce_tail(d, n - 1, end=True)

    def spread(t, carry):
        for q, d in mains:
            gather_step(q, d, t)
        for d in range(2):
            gather_step(2, d, t - 1)
            pass_pair(d, t - 1)
        return carry

    lax.fori_loop(1, n - 1, spread, 0)
    for d in range(2):
        gather_step(2, d, n - 2)
        pass_pair(d, n - 2)
    for d in range(2):
        pass_pair(d, n - 1)

    @pl.when(section == 0)
    def _():
        feat_keep.wait()
        feat_send.wait_send()

    @pl.when(section == 1)
    def _():
        feat_send.wait_recv()

    for q, d in streams:
        keep_copy(q, d).wait()
    for d in range(2):
        for s in range(max(n - 2, 0), n):
            part_copy(d, s).wait_send()
        for s in range(max(n - 3, 0), n - 1):
            for q in range(2):
                ring_copy(q, d, s).wait_send()

    def finish(s, carry):
        for d in range(2):
            tail_part_copy(d, s).wait_send()
            for q in range(3):
                pair_copy(q, d, s).wait_send()
                if q < 2:
                    pair_landed(q, d, s).wait_recv()

            @pl.when(s < n - 1)
            def _():
                ring_copy(2, d, s).wait_send()
                for q in range(3):
                    gather_copy(q, d, s).wait_send()

            for mine in (True, False):
                @pl.when(section == 0)
                def _():
                    cross_copy(d, s, mine).wait_send()

                @pl.when(section == 1)
                def _():
                    cross_copy(d, s, mine).wait_recv()
        return carry

    lax.fori_loop(0, n, finish, 0)


def unpack_kernel(
    blocks, total, attend, project, up, down, coming, going, in_sem, out_sem
):
    members, share, width = total.shape
    slots, unit = coming.shape[:2]
    per_block, per_member = width // unit, share // unit
    count = members * per_member

    def in_copy(u):
        slot = lax.rem(u, slots)
        row = pl.multiple_of(lax.rem(u, per_member) * unit, 16)
        return pltpu.make_async_copy(
            total.at[u // per_member, pl.ds(row, unit)], coming.at[slot], in_sem.at[slot])

    def out_copy(u, dst, row, column):
        slot = lax.rem(u, slots)
        return pltpu.make_async_copy(
            going.at[slot],
            dst.at[pl.ds(pl.multiple_of(row, 16), unit), pl.ds(pl.multiple_of(column, 128), width)],
            out_sem.at[slot])

    for u in range(slots):
        in_copy(u).start()

    def step(u, carry):
        slot = lax.rem(u, slots)
        in_copy(u).wait()

        @pl.when(u >= slots)
        def _():
            out_copy(u, project, 0, 0).wait()

        going[slot] = coming[slot].astype(jnp.float32)
        block, row = u // per_block, lax.rem(u, per_block) * unit

        @pl.when(block < 3)
        def _():
            out_copy(u, attend, row, block * width).start()

        @pl.when(block == 3)
        def _():
            out_copy(u, project, row, 0).start()

        @pl.when((block > 3) & (block < 4 + blocks))
        def _():
            out_copy(u, up, row, (block - 4) * width).start()

        @pl.when(block > 3 + blocks)
        def _():
            out_copy(u, down, (u - (4 + blocks) * per_block) * unit, 0).start()

        @pl.when(u + slots < count)
        def _():
            in_copy(u + slots).start()

        return carry

    lax.fori_loop(0, count, step, 0)
    for u in range(count - slots, count):
        out_copy(u, project, 0, 0).wait()


ANY = pl.BlockSpec(memory_space=pl.ANY)
VMEM = pl.BlockSpec(memory_space=pltpu.VMEM)
SMEM = pl.BlockSpec(memory_space=pltpu.SMEM)
LOW = jnp.bfloat16
WIDE = jnp.float32


def shaped(kind, *dims):
    return jax.ShapeDtypeStruct(dims, kind)


def run_forward(features, chosen, pos_embed, weights, cols, kind_offset, mask_row, bias_row,
                live_row, gains, vectors, up_bias):
    clips, length, feat_width = features.shape
    width, feed = weights[2].shape
    blocks = feed // width
    dma = pltpu.SemaphoreType.DMA
    vm = pltpu.VMEM
    return pl.pallas_call(
        forward_kernel,
        out_shape=(
            shaped(LOW, 3 + blocks, clips * length, width),
            shaped(WIDE, clips, length, width),
            shaped(LOW, clips, length, 3 * width),
            shaped(LOW, clips, H, length, length),
            shaped(WIDE, clips, length, width),
            shaped(LOW, clips, length, feed),
            shaped(LOW, clips, length, width // 2),
            shaped(WIDE, 8, width),
        ),
        in_specs=[ANY] * 7 + [VMEM] * 8,
        out_specs=(ANY,) * 7 + (VMEM,),
        scratch_shapes=[
            vm(features.shape, LOW), vm(chosen.shape, LOW), vm(pos_embed.shape, WIDE),
            vm((width, 3 * width), LOW), vm((width, width), LOW), vm((width, feed), LOW),
            vm((feed, width), LOW),
            vm((length, width), WIDE), vm((length, width), LOW), vm((length, 3 * width), LOW),
            vm((2, 2, length, length), LOW), vm((length, width), LOW), vm((length, width), WIDE),
            vm((length, width), LOW), vm((length, feed), LOW), vm((length, feed), LOW),
            vm((clips, length, width), LOW), vm((clips, length, width), LOW),
            dma((7,)), dma((7 + blocks,)), dma((2,)), dma((clips, 2)), dma((clips, 2)),
            dma((clips, 2)), dma((clips, 2)), dma((clips, 2)),
        ],
        compiler_params=pltpu.CompilerParams(
            collective_id=1, has_side_effects=True, vmem_limit_bytes=56 * 2**20
        ),
    )(features, chosen, pos_embed, *weights, cols, kind_offset, mask_row, bias_row, live_row,
      gains, vectors, up_bias)


def run_backward(cotangent, weights, x, qkv, probs, middle, slope, left, gains):
    clips, length, width = cotangent.shape
    feed = weights[2].shape[1]
    blocks = feed // width
    dma = pltpu.SemaphoreType.DMA
    vm = pltpu.VMEM
    return pl.pallas_call(
        backward_kernel,
        out_shape=(
            shaped(LOW, 5 + blocks, clips * length, width),
            shaped(LOW, clips, length, width),
            shaped(LOW, left.shape[0], width, clips * length),
            shaped(WIDE, 8, width),
            shaped(WIDE, 1, feed),
        ),
        in_specs=[ANY] * 11 + [VMEM],
        out_specs=(ANY, ANY, ANY, VMEM, VMEM),
        scratch_shapes=[
            vm((width, 3 * width), LOW), vm((width, width), LOW), vm((width, feed), LOW),
            vm((feed, width), LOW),
            vm((clips, length, width), WIDE), vm((clips, length, 3 * width), LOW),
            vm((3, 2, length, length), LOW), vm((clips, length, width), WIDE),
            vm((clips, length, feed), LOW), vm((clips, length, width), LOW),
            vm((length, feed), LOW), vm((length, width), WIDE), vm((length, width), WIDE),
            vm((length, width), LOW), vm((length, width), LOW), vm((length, 3 * width), LOW),
            vm((clips, length, width), LOW),
            vm((clips * length, width), LOW), vm((width, clips * length), LOW),
            dma((2,)), dma((4,)), dma((clips, 5)), dma((3,)), dma((5 + blocks,)), dma((clips,)),
            dma((clips, 2)), dma((clips, 2)),
        ],
        compiler_params=pltpu.CompilerParams(
            collective_id=2, has_side_effects=True, vmem_limit_bytes=60 * 2**20
        ),
    )(cotangent, *weights, x, qkv, probs, middle, slope, left, gains)


def run_sums(members, info, turned, right, dx, features, chosen, cols, small, up_sums, stats):
    width, rows = turned.shape[1:]
    clips, length, feat_width = features.shape
    n = members // 2
    share = 12 * width // members
    embed_rows = 2 * feat_width + length
    tail = embed_rows // members + SMALL
    unit = unit_rows(members, width)
    per_member = share // unit
    half = width // 2
    dma = pltpu.SemaphoreType.DMA
    vm = pltpu.VMEM
    sems = [dma((2, 2 * per_member + 2)), dma((3,)), dma((2, 2 * n)), dma((2, 2 * n))]
    sems += [dma((2, 3, n)) for _ in range(6)]
    sems += [dma((2, 3)), dma((2, 2, n)), dma((2, 2, n)), dma((3,))]
    return pl.pallas_call(
        functools.partial(sums_kernel, members),
        out_shape=(
            shaped(LOW, members, share, width),
            shaped(LOW, members, tail, width),
            shaped(LOW, members, tail, width),
            shaped(LOW, clips, length, feat_width // 2),
        ),
        in_specs=[SMEM] + [ANY] * 5 + [VMEM] * 4,
        out_specs=(ANY,) * 4,
        scratch_shapes=[
            vm((2, 2 * per_member, unit, rows), LOW), vm((2, 2, rows, half), LOW),
            vm((2, 3, share, half), LOW), vm((2, 2, share, half), LOW),
            vm((2, n, share, half), LOW), vm((2, n - 1, share, half), LOW),
            vm((members, tail, width), LOW), vm((2, n, tail, half), LOW),
            vm((2, n, tail, half), LOW), vm((2, n - 1, tail, half), LOW),
            vm((clips, length, width), LOW), vm(features.shape, LOW), vm(chosen.shape, LOW),
            vm(features.shape, LOW), vm((embed_rows, width), LOW), vm((SMALL, width), WIDE),
            sems,
        ],
        compiler_params=pltpu.CompilerParams(
            collective_id=0, has_side_effects=True, vmem_limit_bytes=60 * 2**20
        ),
    )(info, turned, right, dx, features, chosen, cols, small, up_sums, stats)


def run_unpack(total, blocks):
    members, share, width = total.shape
    unit = unit_rows(members, width)
    slots = 6
    dma = pltpu.SemaphoreType.DMA
    return pl.pallas_call(
        functools.partial(unpack_kernel, blocks),
        out_shape=(
            shaped(WIDE, width, 3 * width), shaped(WIDE, width, width),
            shaped(WIDE, width, blocks * width), shaped(WIDE, blocks * width, width),
        ),
        in_specs=[ANY],
        out_specs=(ANY,) * 4,
        scratch_shapes=[
            pltpu.VMEM((slots, unit, width), LOW), pltpu.VMEM((slots, unit, width), WIDE),
            dma((slots,)), dma((slots,)),
        ],
        compiler_params=pltpu.CompilerParams(vmem_limit_bytes=32 * 2**20),
    )(total)


def local(
    features,
    masked,
    valid,
    kinds,
    embed_weight,
    embed_vectors,
    pos_embed,
    norm_gains,
    vectors,
    qkv_weight,
    out_weight,
    up_weight,
    up_bias,
    down_weight,
    cotangent,
):
    is_first = lax.axis_index("section") == 0
    members = lax.axis_size("wide")
    clips, length, feat_width = features.shape
    width = pos_embed.shape[1]
    weights = (qkv_weight[0], out_weight[0], up_weight[0], down_weight[0])
    blocks = up_weight.shape[2] // width
    chosen = jnp.where(kinds[:, None, None] == 0, embed_weight[0], embed_weight[1])
    kind_offset = jnp.where(kinds[:, None] == 0, embed_vectors[0], embed_vectors[1])[:, None]
    lane = jnp.arange(128)
    cols = jnp.where(
        lane == 0, masked[:, :, None], jnp.where(lane == 1, valid[:, :, None], 0)
    ).astype(WIDE)
    live_row = jnp.where(valid > 0, 0.0, NEG)[:, None]
    rows = vectors[0]
    bias_row = jnp.concatenate([rows[1], jnp.zeros((width,), WIDE), rows[2]])[None]
    left, x, qkv, probs, middle, slope, output, stats = run_forward(
        features, chosen, pos_embed, weights, cols, kind_offset, embed_vectors[2:3], bias_row,
        live_row, norm_gains[0], rows, up_bias)
    right, dx, turned, small, up_sums = run_backward(
        cotangent, weights, x, qkv, probs, middle, slope, left, norm_gains[0])
    total, tails, cross, feature_out = run_sums(
        members, kinds, turned, right, dx, features, chosen, cols, small, up_sums, stats)
    attend_total, project_total, up_total, down_total = run_unpack(total, blocks)
    embed_share = (2 * feat_width + length) // members
    ends = jnp.where(is_first, tails, cross)
    embed_total = ends[:, :embed_share].reshape(-1, width).astype(WIDE)
    small_total = tails[0, -SMALL:].astype(WIDE)
    stat_row = small_total[15]
    rms_out = jnp.sqrt(stat_row[0:3] / (stat_row[3] * width))[None]
    return (
        output,
        feature_out,
        embed_total[: 2 * feat_width].reshape(2, feat_width, width),
        ends[0, embed_share + 12 : embed_share + 15].astype(WIDE),
        embed_total[2 * feat_width :],
        small_total[None, 0:2],
        small_total[None, 2:8],
        attend_total[None],
        project_total[None],
        up_total[None],
        small_total[8 : 8 + blocks].reshape(1, -1),
        down_total[None],
        rms_out,
    )


def solution(mesh):
    return jax.shard_map(
        local,
        mesh=mesh,
        in_specs=(
            P("wide", None, None),
            P("wide", None),
            P("wide", None),
            P("wide"),
            P(),
            P(),
            P(),
            P("section", None, None),
            P("section", None, None),
            P("section", None, None),
            P("section", None, None),
            P("section", None, None),
            P("section", None),
            P("section", None, None),
            P("wide", None, None),
        ),
        out_specs=(
            P("wide", None, "section"),
            P("wide", None, "section"),
            P(),
            P(),
            P(),
            P("section", None, None),
            P("section", None, None),
            P("section", None, None),
            P("section", None, None),
            P("section", None, None),
            P("section", None),
            P("section", None, None),
            P("section", None),
        ),
        check_vma=False,
    )
```

```python
import functools
import math

import jax
import jax.numpy as jnp
from jax import lax
from jax.experimental import pallas as pl
from jax.experimental.pallas import tpu as pltpu
from jax.sharding import PartitionSpec as P

H = 12
HD = 64
EPS = 1e-06
NEG = -1000000000.0


MESH = pl.DeviceIdType.MESH
SMALL = 16


def unit_rows(members, width):
    return math.gcd(12 * width // members, width)


def dot_nn(left, right):
    return jnp.dot(left, right, preferred_element_type=jnp.float32)


def dot_nt(left, right):
    return lax.dot_general(
        left, right, (((1,), (1,)), ((), ())), preferred_element_type=jnp.float32
    )


def tile_of(index, size):
    if isinstance(index, int):
        return pl.ds(index * size, size)
    return pl.ds(pl.multiple_of(index * size, size), size)


def loop(count, body, unroll):
    if count == unroll:
        for i in range(count):
            body(i, 0)
        return

    def step(i, carry):
        for u in range(unroll):
            body(i * unroll + u, 0)
        return carry

    lax.fori_loop(0, count // unroll, step, 0)


def column_sum(values):
    return jnp.sum(values, axis=0, keepdims=True)


def row_mean(values):
    return jnp.mean(values, axis=-1, keepdims=True)


def pick_kind(kind, first, second):
    keep = (kind == 0).astype(jnp.float32)
    return first.astype(jnp.float32) * keep + second.astype(jnp.float32) * (1.0 - keep)


def gelu_pair(hidden):
    decay = jnp.exp(-0.5 * hidden * hidden)
    t = 1.0 / (1.0 + (0.3275911 * 0.5**0.5) * jnp.abs(hidden))
    poly = 1.061405429 * 0.5
    for term in (-1.453152027, 1.421413741, -0.284496736, 0.254829592):
        poly = poly * t + 0.5 * term
    upper = poly * t * decay
    cdf = jnp.where(hidden > 0.0, 1.0 - upper, upper)
    return hidden * cdf, cdf + hidden * decay * 0.3989422804014327


def fetch(pairs, sems):
    copies = [pltpu.make_async_copy(src, dst, sems.at[i]) for i, (src, dst) in enumerate(pairs)]
    for copy in copies:
        copy.start()
    return copies


def greet_partner():
    barrier = pltpu.get_barrier_semaphore()
    pl.semaphore_signal(
        barrier, inc=1, device_id={"section": 1 - lax.axis_index("section")}, device_id_type=MESH
    )
    pl.semaphore_wait(barrier, 1)


def to_partner(src, dst, send, recv):
    return pltpu.make_async_remote_copy(
        src_ref=src, dst_ref=dst, send_sem=send, recv_sem=recv,
        device_id={"section": 1 - lax.axis_index("section")}, device_id_type=MESH)


def forward_kernel(
    kinds, feat_h, masked_h, valid_h, embw_h, embv_h, pos_h, gains_h, vectors_h, wqkv_h, wout_h,
    wup_h, upb_h, wdown_h,
    left_h, x_h, qkv_h, probs_h, middle_h, slope_h, out_h, cols, stats,
    feat, masked, valid, embw, embv, pos, gains, vectors, wqkv, wout, wup, up_bias, wdown,
    chosen, live_row,
    x, normed, qkv, probs, context, middle, hidden_in, active, slope, y, landed,
    load_sem, save_sem, probs_sem, send_sem, recv_sem, back_send, back_recv, keep_sem,
):
    low = jnp.bfloat16
    section = lax.axis_index("section")
    clips, length, width = landed.shape
    half = length // 2
    feed = wup.shape[1]
    heads2 = width // 128
    blocks = feed // width
    loads = fetch(
        [(masked_h, masked), (valid_h, valid), (gains_h.at[0], gains),
         (vectors_h.at[0], vectors), (upb_h, up_bias),
         (feat_h, feat), (embw_h, embw), (embv_h, embv), (pos_h, pos),
         (wqkv_h.at[0], wqkv), (wout_h.at[0], wout), (wup_h.at[0], wup), (wdown_h.at[0], wdown)],
        load_sem)
    greet_partner()
    stats[...] = jnp.zeros_like(stats)
    for copy in loads[:9]:
        copy.wait()
    sublane = lax.broadcasted_iota(jnp.int32, (128, length), 0)
    for c in range(clips):
        flags = jnp.where(sublane == 0, masked[c : c + 1, :], 0)
        flags = jnp.where(sublane == 1, valid[c : c + 1, :], flags)
        cols[c] = flags.astype(jnp.float32).T
        live_row[c] = jnp.where(valid[c : c + 1, :] > 0, 0.0, NEG)
    low_lanes = lax.broadcasted_iota(jnp.int32, (1, 128), 1) < HD

    def save(index, src, dst):
        return pltpu.make_async_copy(src, dst, save_sem.at[index])

    def saves(c):
        rows = pl.ds(pl.multiple_of(c * length, length), length)
        pairs = [
            (x, x_h.at[c]), (normed, left_h.at[0, rows]), (qkv, qkv_h.at[c]),
            (context, left_h.at[1, rows]), (middle, middle_h.at[c]),
            (hidden_in, left_h.at[2, rows]), (slope, slope_h.at[c]),
        ] + [
            (active.at[:, pl.ds(b * width, width)], left_h.at[3 + b, rows]) for b in range(blocks)
        ]
        return [save(i, src, dst) for i, (src, dst) in enumerate(pairs)]

    def probs_save(c, pair):
        slot = lax.rem(pair, 2)
        return pltpu.make_async_copy(
            probs.at[slot], probs_h.at[c, pl.ds(pair * 2, 2)], probs_sem.at[slot])

    def send_half(c, h):
        rows = pl.ds(h * half, half)
        return to_partner(
            y.at[c, rows], landed.at[c, rows], send_sem.at[c, h], recv_sem.at[c, h])

    def back_half(c, h):
        rows = pl.ds(h * half, half)
        return to_partner(
            y.at[c, rows, pl.ds(0, width // 2)], out_h.at[c, rows],
            back_send.at[c, h], back_recv.at[c, h])

    def keep_half(c, h):
        rows = pl.ds(h * half, half)
        return pltpu.make_async_copy(
            y.at[c, rows, pl.ds(width // 2, width // 2)], out_h.at[c, rows], keep_sem.at[c, h])

    def clip(c, carry):
        def after_first(index):
            @pl.when(c > 0)
            def _():
                saves(c - 1)[index].wait()

        after_first(0)
        after_first(1)

        @pl.when(section == 0)
        def _():
            chosen[...] = pick_kind(kinds[c], embw[0], embw[1]).astype(low)
            offset = pick_kind(kinds[c], embv[0:1, :], embv[1:2, :])

            def tile(i, carry):
                rows = tile_of(i, 128)
                lifted = dot_nn(feat[c, rows, :], chosen[...]) + offset
                hidden = cols[c, rows, :][:, 0:1]
                x[rows, :] = jnp.where(hidden > 0.0, embv[2:3, :], lifted) + pos[rows, :]
                return carry

            loop(length // 128, tile, 4)

        @pl.when(section == 1)
        def _():
            for h in range(2):
                send_half(c, h).wait_recv()

            def tile(i, carry):
                rows = tile_of(i, 64)
                x[rows, :] = landed[c, rows, :].astype(jnp.float32)
                return carry

            loop(length // 64, tile, 4)

        own = saves(c)
        own[0].start()

        def norm_rows(source, target, which, shift, first, count):
            gain, offset = gains[which : which + 1, :], vectors[shift : shift + 1, :]

            def tile(i, carry):
                rows = tile_of(i, 64)
                values = source[rows, :]
                values = values - row_mean(values)
                scale = lax.rsqrt(row_mean(values * values) + EPS)
                target[rows, :] = (values * scale * gain + offset).astype(low)
                return carry

            loop(count, lambda i, carry: tile(first + i, carry), 4)

        norm_rows(x, normed, 0, 0, 0, length // 64)
        own[1].start()
        after_first(2)

        @pl.when(c == 0)
        def _():
            loads[9].wait()

        def qkv_tile(j, carry):
            at = tile_of(j, 256)
            part = dot_nn(normed[...], wqkv[:, at])
            if j < width // 256:
                part = part + vectors[1:2, at]
            elif j >= 2 * width // 256:
                part = part + vectors[2:3, tile_of(j - 2 * width // 256, 256)]
            qkv[:, at] = part.astype(low)
            return carry

        loop(3 * width // 256, qkv_tile, 9)
        own[2].start()
        after_first(3)

        def attend(pair, carry):
            @pl.when((pair > 1) | (c > 0))
            def _():
                probs_save(c, pair).wait()

            at = tile_of(pair, 128)
            queries = qkv[:, at]
            keys_in = qkv[:, tile_of(pair + heads2, 128)]
            values_in = qkv[:, tile_of(pair + 2 * heads2, 128)]
            outs = []
            for h in range(2):
                pick = jnp.where(low_lanes == (h == 0), HD**-0.5, 0.0).astype(low)
                scores = dot_nt(queries * pick, keys_in) + live_row[c]
                top = jnp.max(scores, axis=-1, keepdims=True)
                scores = jnp.exp(scores - top)
                total = jnp.sum(scores, axis=-1, keepdims=True)
                soft = (scores * (1.0 / total)).astype(low)
                probs[lax.rem(pair, 2), h] = soft
                outs.append(dot_nn(soft, values_in))
            context[:, at] = jnp.where(low_lanes, outs[0], outs[1]).astype(low)
            probs_save(c, pair).start()
            return carry

        lax.fori_loop(0, heads2, attend, 0)
        own[3].start()
        after_first(4)

        @pl.when(c == 0)
        def _():
            loads[10].wait()

        live = cols[c][:, 1:2]

        def out_tile(j, carry):
            at = tile_of(j, 256)
            branch = dot_nn(context[...], wout[:, at]) + vectors[3:4, at]
            middle[:, at] = x[:, at] + branch
            stats[1:2, at] += column_sum(branch * branch * live)
            return carry

        loop(width // 256, out_tile, 3)
        own[4].start()
        for index in range(5, 7 + blocks):
            after_first(index)

        @pl.when(c == 0)
        def _():
            loads[11].wait()
            loads[12].wait()

        for h in range(2):
            rows = pl.ds(h * half, half)
            norm_rows(middle, hidden_in, 1, 4, h * (half // 64), half // 64)
            if h == 1:
                own[5].start()

            def up_tile(j, carry):
                at = tile_of(j, 256)
                hidden = dot_nn(hidden_in[rows, :], wup[:, at]) + up_bias[:, at]
                value, steep = gelu_pair(hidden)
                active[rows, at] = value.astype(low)
                slope[rows, at] = steep.astype(low)
                return carry

            loop(feed // 256, up_tile, 6)
            if h == 1:
                for copy in own[6:]:
                    copy.start()

            def down_tile(j, carry):
                at = tile_of(j, 256)
                mixer = dot_nn(active[rows, :], wdown[:, at]) + vectors[5:6, at]
                total = middle[rows, at] + mixer
                flags = cols[c, rows, :][:, 1:2]
                stats[0:1, at] += column_sum(total * total * flags)
                stats[2:3, at] += column_sum(mixer * mixer * flags)
                y[c, rows, at] = total.astype(low)
                return carry

            loop(width // 256, down_tile, 3)

            @pl.when(section == 0)
            def _():
                send_half(c, h).start()

            @pl.when(section == 1)
            def _():
                back_half(c, h).start()
                keep_half(c, h).start()
        return carry

    lax.fori_loop(0, clips, clip, 0)
    for pair in (heads2 - 2, heads2 - 1):
        probs_save(clips - 1, pair).wait()
    for copy in saves(clips - 1):
        copy.wait()
    for c in range(clips):
        for h in range(2):
            @pl.when(section == 0)
            def _():
                send_half(c, h).wait_send()
                back_half(c, h).wait_recv()

            @pl.when(section == 1)
            def _():
                back_half(c, h).wait_send()
                keep_half(c, h).wait()


def backward_kernel(
    cot_h, wqkv_h, wout_h, wup_h, wdown_h, x_h, qkv_h, probs_h, middle_h, slope_h, left_h, gains_h,
    right_h, dx_h, turned_h, small, up_sums,
    wqkv, wout, wup, wdown, gains, x, qkv, probs, middle, slope, g,
    d_hidden, wide_grad, d_middle, d_branch, d_context, d_qkv, d_low, upright, turned,
    turn_sem, load_sem, state_sem, probs_sem, save_sem, dx_sem, send_sem, recv_sem,
):
    low = jnp.bfloat16
    f32 = jnp.float32
    section = lax.axis_index("section")
    clips, length, width = g.shape
    half = length // 2
    feed = wup.shape[1]
    heads2 = width // 128
    blocks = feed // width
    greet_partner()

    def cot_load(c):
        return pltpu.make_async_copy(cot_h.at[c], g.at[c], state_sem.at[c, 0])

    def state_loads(c):
        pairs = [(slope_h, slope), (middle_h, middle), (qkv_h, qkv), (x_h, x)]
        return [
            pltpu.make_async_copy(src.at[c], dst.at[c], state_sem.at[c, 1 + i])
            for i, (src, dst) in enumerate(pairs)
        ]

    @pl.when(section == 1)
    def _():
        cot_load(0).start()

    loads = fetch(
        [(gains_h.at[0], gains), (wdown_h.at[0], wdown), (wup_h.at[0], wup), (wout_h.at[0], wout),
         (wqkv_h.at[0], wqkv)], load_sem)
    for c in range(clips):
        for copy in state_loads(c):
            copy.start()

    @pl.when(section == 1)
    def _():
        for c in range(1, clips):
            cot_load(c).start()

    small[...] = jnp.zeros_like(small)
    up_sums[...] = jnp.zeros_like(up_sums)
    low_lanes = lax.broadcasted_iota(jnp.int32, (1, 128), 1) < HD
    slots = probs.shape[0]
    pairs_total = clips * heads2

    def probs_load(step):
        slot = lax.rem(step, slots)
        return pltpu.make_async_copy(
            probs_h.at[step // heads2, pl.ds(lax.rem(step, heads2) * 2, 2)],
            probs.at[slot], probs_sem.at[slot])

    for step in range(slots):
        probs_load(step).start()

    def saves(c):
        rows = pl.ds(pl.multiple_of(c * length, length), length)
        pairs = [(d_qkv.at[:, pl.ds(b * width, width)], right_h.at[b, rows]) for b in range(3)]
        pairs += [(d_branch, right_h.at[3, rows])]
        pairs += [
            (d_hidden.at[:, pl.ds(b * width, width)], right_h.at[4 + b, rows])
            for b in range(blocks)
        ]
        pairs += [(g.at[c], right_h.at[4 + blocks, rows])]
        return [pltpu.make_async_copy(s, d, save_sem.at[i]) for i, (s, d) in enumerate(pairs)]

    def send_half(c, h):
        rows = pl.ds(h * half, half)
        return to_partner(
            d_low.at[c, rows], g.at[c, rows], send_sem.at[c, h], recv_sem.at[c, h])

    def dx_save(c):
        return pltpu.make_async_copy(d_low.at[c], dx_h.at[c], dx_sem.at[c])

    def norm_back(source, carried, which, shift_row, rows, take):
        gain = gains[which : which + 1, :]
        values = source[rows, :]
        values = values - row_mean(values)
        scale = lax.rsqrt(row_mean(values * values) + EPS)
        values = values * scale
        grad = wide_grad[rows, :]
        small[which : which + 1, :] += column_sum(grad * values)
        small[shift_row : shift_row + 1, :] += column_sum(grad)
        grad = grad * gain
        return carried + scale * (grad - row_mean(grad) - values * row_mean(grad * values))

    def turn_lefts():
        def block(b, carry):
            come = pltpu.make_async_copy(left_h.at[b], upright, turn_sem.at[0])
            come.start()
            come.wait()

            def piece(i, carry):
                at = tile_of(i, 128)
                turned[at, :] = upright[:, at].T
                return carry

            loop(width // 128, piece, 2)
            leave = pltpu.make_async_copy(turned, turned_h.at[b], turn_sem.at[1])
            leave.start()
            leave.wait()
            return carry

        lax.fori_loop(0, left_h.shape[0], block, 0)

    @pl.when(section == 0)
    def _():
        turn_lefts()

    def clip(c, carry):
        def after_first(lo, hi):
            @pl.when(c > 0)
            def _():
                for copy in saves(c - 1)[lo:hi]:
                    copy.wait()

        after_first(4, 5 + blocks)

        @pl.when(section == 1)
        def _():
            cot_load(c).wait()

        state = state_loads(c)
        own = saves(c)

        @pl.when(c == 0)
        def _():
            for copy in loads[:3]:
                copy.wait()

        state[0].wait()
        state[1].wait()
        for h in range(2):
            rows = pl.ds(h * half, half)

            @pl.when(section == 0)
            def _():
                send_half(c, h).wait_recv()

            if h == 1:
                own[-1].start()

            def feed_tile(j, carry):
                at = tile_of(j, 256)
                d_active = dot_nt(g[c, rows, :], wdown[at, :])
                grad = (slope[c, rows, at].astype(f32) * d_active).astype(low)
                d_hidden[rows, at] = grad
                up_sums[:, at] += column_sum(grad.astype(f32))
                return carry

            loop(feed // 256, feed_tile, 6)

            def in_tile(j, carry):
                at = tile_of(j, 256)
                wide_grad[rows, at] = dot_nt(d_hidden[rows, :], wup[at, :])
                return carry

            loop(width // 256, in_tile, 3)

        after_first(3, 4)
        for copy in own[4:-1]:
            copy.start()

        def middle_tile(i, carry):
            rows = tile_of(i, 64)
            grad_in = g[c, rows, :].astype(f32)
            total = norm_back(middle.at[c], grad_in, 1, 6, rows, None)
            d_middle[rows, :] = total
            rounded = total.astype(low)
            d_branch[rows, :] = rounded
            small[5:6, :] += column_sum(rounded.astype(f32))
            small[7:8, :] += column_sum(grad_in)
            return carry

        loop(length // 64, middle_tile, 4)
        own[3].start()

        @pl.when(c == 0)
        def _():
            loads[3].wait()

        def context_tile(j, carry):
            at = tile_of(j, 256)
            d_context[:, at] = dot_nt(d_branch[...], wout[at, :]).astype(low)
            return carry

        loop(width // 256, context_tile, 3)
        state[2].wait()
        after_first(0, 3)

        def attend(pair, carry):
            step = c * heads2 + pair
            slot = lax.rem(step, slots)
            probs_load(step).wait()
            at, key_at = tile_of(pair, 128), tile_of(pair + heads2, 128)
            value_at = tile_of(pair + 2 * heads2, 128)
            queries, keys_in, values_in = qkv[c, :, at], qkv[c, :, key_at], qkv[c, :, value_at]
            grad = d_context[:, at]
            queries_t, grad_t = queries.T, grad.T
            d_queries, keys_t, values_t = [], [], []
            for h in range(2):
                pick = jnp.where(low_lanes == (h == 0), 1.0, 0.0).astype(low)
                soft = probs[slot, h]
                soft_wide = soft.astype(f32)
                d_soft = dot_nt(grad * pick, values_in)
                delta = jnp.sum(soft_wide * d_soft, axis=-1, keepdims=True)
                d_scores = (soft_wide * (d_soft - delta)).astype(low)
                part = slice(h * HD, (h + 1) * HD)
                values_t.append(dot_nn(grad_t[part], soft))
                keys_t.append(dot_nn(queries_t[part], d_scores))
                d_queries.append(dot_nn(d_scores, keys_in))
            scale = HD**-0.5
            query_grad = (jnp.where(low_lanes, d_queries[0], d_queries[1]) * scale).astype(low)
            value_grad = jnp.concatenate(values_t, axis=0).T.astype(low)
            d_qkv[:, at] = query_grad
            d_qkv[:, key_at] = (jnp.concatenate(keys_t, axis=0) * scale).T.astype(low)
            d_qkv[:, value_at] = value_grad
            small[3:4, at] += column_sum(query_grad.astype(f32))
            small[4:5, at] += column_sum(value_grad.astype(f32))

            @pl.when(step + slots < pairs_total)
            def _():
                probs_load(step + slots).start()

            return carry

        lax.fori_loop(0, heads2, attend, 0)
        for copy in own[:3]:
            copy.start()

        @pl.when(c == 0)
        def _():
            loads[4].wait()

        state[3].wait()
        for h in range(2):
            rows = pl.ds(h * half, half)

            def in_tile(j, carry):
                at = tile_of(j, 256)
                wide_grad[rows, at] = dot_nt(d_qkv[rows, :], wqkv[at, :])
                return carry

            loop(width // 256, in_tile, 3)

            def last_tile(i, carry):
                part = tile_of(i, 64)
                total = norm_back(x.at[c], d_middle[part, :], 0, 2, part, None)
                d_low[c, part, :] = total.astype(low)
                return carry

            loop(half // 64, lambda i, carry: last_tile(h * (half // 64) + i, carry), 4)

            @pl.when(section == 1)
            def _():
                send_half(c, h).start()

        dx_save(c).start()
        return carry

    lax.fori_loop(0, clips, clip, 0)

    @pl.when(section == 1)
    def _():
        turn_lefts()

    for copy in saves(clips - 1):
        copy.wait()
    for c in range(clips):
        dx_save(c).wait()
        for h in range(2):
            @pl.when(section == 1)
            def _():
                send_half(c, h).wait_send()


def sums_kernel(
    members, kinds, turned_h, right_h, dx_h, feat_h, embw_h, cols, small_in, up_sums, stats,
    o_ref, t_ref, e_ref, h_ref,
    lefts, rights, chunk, part, ring, tails, tail_own, tail_part, tail_ring,
    dx, feat, embw, feat_grad, embed, small, sems,
):
    (load_sem, embed_sem, part_send, part_recv, ring_send, ring_recv, gather_send, gather_recv,
     pair_send, pair_recv, keep_sem, cross_send, cross_recv, feat_sem) = sems
    low = jnp.bfloat16
    f32 = jnp.float32
    n = members // 2
    share, columns = chunk.shape[3:]
    width = 2 * columns
    tail = tails.shape[1]
    unit = unit_rows(members, width)
    per_block, per_member = width // unit, share // unit
    slots = chunk.shape[1]
    clips, length, feat_width = feat.shape
    me = lax.axis_index("wide")
    section = lax.axis_index("section")
    chip, core = me // 2, me % 2
    place = jnp.where(chip % 2 == 0, chip // 2, n - 1 - chip // 2)

    def member_at(position):
        position = lax.rem(position + 2 * n, n)
        return jnp.where(2 * position < n, 2 * position, 2 * (n - 1 - position) + 1) * 2 + core

    right, left = member_at(place + 1), member_at(place - 1)
    other = chip * 2 + 1 - core
    target = (right, left)

    barrier = pltpu.get_barrier_semaphore()
    for peer in (right, left, other):
        pl.semaphore_signal(barrier, inc=1, device_id={"wide": peer}, device_id_type=MESH)
    @pl.when(section == 1)
    def _():
        pl.semaphore_signal(barrier, inc=1, device_id={"section": 0}, device_id_type=MESH)

    pieces = ring_send.shape[1] - 1
    piece = -(-share // (16 * pieces)) * 16
    spans = [(q * piece, min(piece, share - q * piece)) for q in range(pieces)]
    mains = [(q, d) for q in range(pieces) for d in range(2)]
    streams = mains + [(pieces, 0), (pieces, 1)]

    def turn(position):
        return lax.rem(position + 2 * n, n)

    def reduce_at(d, step):
        return turn(place - step) if d == 0 else turn(place + step)

    def gather_at(d, index):
        return turn(place + 1 - index) if d == 0 else turn(place - 1 + index)

    def span(q):
        return pl.ds(*spans[q])

    def cols_of(d):
        return pl.ds(d * columns, columns)

    def remote(src, dst, send, recv, device):
        return pltpu.make_async_remote_copy(
            src_ref=src, dst_ref=dst, send_sem=send, recv_sem=recv,
            device_id=device, device_id_type=MESH)

    def block_of(spot):
        return spot // per_block

    def operand_copies(d, s):
        base = reduce_at(d, s) * 2 * per_member
        first, second = block_of(base), block_of(base + 2 * per_member - 1)
        copies = []
        for u in range(2 * per_member):
            block = block_of(base + u)
            source = jnp.where(
                block < 3, 0, jnp.where(block == 3, 1, jnp.where(block < 8, 2, block - 5)))
            row = pl.multiple_of(lax.rem(base + u, per_block) * unit, 16)
            copies.append(pltpu.make_async_copy(
                turned_h.at[source, pl.ds(row, unit)], lefts.at[d, u], load_sem.at[d, u]))
        for i, block in enumerate((first, second)):
            copies.append(pltpu.make_async_copy(
                right_h.at[jnp.minimum(block, 8), :, cols_of(d)], rights.at[d, i],
                load_sem.at[d, 2 * per_member + i]))
        return copies

    def load_operands(d, s):
        for copy in operand_copies(d, s):
            copy.start()

    def part_copy(d, s):
        return remote(
            chunk.at[d, lax.rem(s, slots), 1 - core], part.at[d, s], part_send.at[d, s], part_recv.at[d, s],
            {"wide": other})

    def ring_copy(q, d, s):
        if q == pieces:
            src, dst = tail_own.at[d, s], tail_ring.at[d, s]
        else:
            src, dst = chunk.at[d, lax.rem(s, slots), core, span(q)], ring.at[d, s, span(q)]
        return remote(src, dst, ring_send.at[d, q, s], ring_recv.at[d, q, s],
                      {"wide": target[d]})

    def products(d, s, prefetch):
        for copy in operand_copies(d, s):
            copy.wait()
        base = reduce_at(d, s) * 2 * per_member
        first = block_of(base)

        for u in range(0, 2 * per_member, 2):
            rows = lefts[d, u : u + 2].reshape(2 * unit, lefts.shape[3])
            tile = dot_nn(rows, rights[d, block_of(base + u) - first]).astype(low)
            for i in range(2):
                which, row = (u + i) // per_member, (u + i) % per_member * unit
                chunk[d, lax.rem(s, slots), which, pl.ds(row, unit), :] = (
                    tile[i * unit : (i + 1) * unit])
        part_copy(d, s).start()
        prefetch()

    def final_of(q, d):
        return tail_own.at[d, n - 1] if q == pieces else chunk.at[d, (n - 1) % slots, core, span(q)]

    def spot_of(q, d, index, which):
        member = gather_at(d, index) * 2 + which
        if q == pieces:
            return t_ref.at[member, :, cols_of(d)]
        return o_ref.at[member, span(q), cols_of(d)]

    def gather_copy(q, d, index, first=False):
        src = final_of(q, d) if first else spot_of(q, d, index, core)
        return remote(
            src, spot_of(q, d, index, core),
            gather_send.at[d, q, index], gather_recv.at[d, q, index], {"wide": target[d]})

    def gather_landed(q, d, index):
        return remote(
            final_of(q, d), spot_of(q, d, index + 1, core),
            gather_send.at[d, q, index], gather_recv.at[d, q, index], {"wide": target[d]})

    def pair_copy(q, d, index, first=False):
        src = final_of(q, d) if first else spot_of(q, d, index, core)
        return remote(
            src, spot_of(q, d, index, core),
            pair_send.at[d, q, index], pair_recv.at[d, q, index], {"wide": other})

    def pair_landed(q, d, index):
        return remote(
            final_of(q, d), spot_of(q, d, index, 1 - core),
            pair_send.at[d, q, index], pair_recv.at[d, q, index], {"wide": other})

    def keep_copy(q, d):
        return pltpu.make_async_copy(final_of(q, d), spot_of(q, d, 0, core), keep_sem.at[d, q])

    def cross_copy(d, index, mine, first=False):
        member = gather_at(d, index) * 2 + (core if mine else 1 - core)
        src = final_of(pieces, d) if first else t_ref.at[member, :, cols_of(d)]
        lane = 0 if mine else 1
        return remote(
            src, e_ref.at[member, :, cols_of(d)],
            cross_send.at[d, lane, index], cross_recv.at[d, lane, index],
            {"section": 1 - section})

    def hand_over(q, d):
        gather_copy(q, d, 0, True).start()
        pair_copy(q, d, 0, True).start()
        keep_copy(q, d).start()
        if q == pieces:
            @pl.when(section == 0)
            def _():
                cross_copy(d, 0, True, True).start()

    def reduce_main(q, d, s, begin=False, end=False):
        if not begin:
            ring_copy(q, d, s - 1).wait_recv()

        def add(tile, carry):
            at = pl.ds(pl.multiple_of(spans[q][0] + tile * 16, 16), 16)
            slot = lax.rem(s, slots)
            total = chunk[d, slot, core, at].astype(f32) + part[d, s, at].astype(f32)
            if not begin:
                total = total + ring[d, s - 1, at].astype(f32)
            chunk[d, slot, core, at] = total.astype(low)
            return carry

        loop(spans[q][1] // 16, add, 1)
        if end:
            hand_over(q, d)
        else:
            ring_copy(q, d, s).start()

    def tail_part_copy(d, s):
        return remote(
            tails.at[reduce_at(d, s) * 2 + 1 - core, :, cols_of(d)], tail_part.at[d, s],
            part_send.at[d, n + s], part_recv.at[d, n + s], {"wide": other})

    def reduce_tail(d, s, begin=False, end=False):
        tail_part_copy(d, s).wait_recv()
        total = tails[reduce_at(d, s) * 2 + core, :, cols_of(d)].astype(f32)
        total = total + tail_part[d, s].astype(f32)
        if not begin:
            ring_copy(pieces, d, s - 1).wait_recv()
            total = total + tail_ring[d, s - 1].astype(f32)
        tail_own[d, s] = total.astype(low)
        if end:
            hand_over(pieces, d)
        else:
            ring_copy(pieces, d, s).start()

    feat_half = h_ref.shape[2]
    feat_keep = pltpu.make_async_copy(
        feat_grad.at[:, :, pl.ds(0, feat_half)], h_ref, feat_sem.at[0])
    feat_send = remote(
        feat_grad.at[:, :, pl.ds(feat_half, feat_half)], h_ref, feat_sem.at[1], feat_sem.at[2],
        {"section": 1 - section})

    def embed_back():
        first = (1 - section).astype(f32)
        small[...] = jnp.zeros_like(small)
        small[0:8, :] = small_in[...]
        for i in range(up_sums.shape[1] // width):
            small[8 + i : 9 + i, :] = up_sums[:, i * width : (i + 1) * width]
        lane = lax.broadcasted_iota(jnp.int32, (1, width), 1)
        row = jnp.zeros((1, width), f32)
        for i in range(3):
            row = jnp.where(lane == i, jnp.sum(stats[i : i + 1, :], axis=1, keepdims=True), row)
        count = jnp.zeros((1, 1), f32)
        for c in range(clips):
            count = count + jnp.sum(cols[c][:, 1:2], axis=0, keepdims=True)
        small[15:16, :] = jnp.where(lane == 3, count, row)
        embed[...] = jnp.zeros_like(embed)

        @pl.when(section == 0)
        def _():
            weight_sum = [jnp.zeros((feat_width, width), f32)] * 2
            place_sum = jnp.zeros((length, width), f32)
            for c in range(clips):
                grad = dx[c]
                kept = jnp.where(cols[c][:, 0:1] > 0.0, jnp.zeros_like(grad), grad)
                chosen = pick_kind(kinds[c], embw[0], embw[1]).astype(low)
                feat_grad[c] = dot_nt(kept, chosen).astype(low)
                second = kinds[c].astype(f32)
                flags = (1.0 - second, second)
                wide = dot_nn(feat[c].T, kept)
                sums = column_sum(kept.astype(f32))
                for kind in range(2):
                    weight_sum[kind] = weight_sum[kind] + flags[kind] * wide
                    small[12 + kind : 13 + kind, :] += flags[kind] * sums
                small[14:15, :] += column_sum(grad.astype(f32)) - sums
                place_sum = place_sum + grad.astype(f32)
            embed[0:feat_width, :] = weight_sum[0].astype(low)
            embed[feat_width : 2 * feat_width, :] = weight_sum[1].astype(low)
            embed[2 * feat_width :, :] = place_sum.astype(low)
            feat_keep.start()
            feat_send.start()

        embed_share = tail - SMALL
        for w in range(members):
            tails[w, 0:embed_share, :] = embed[w * embed_share : (w + 1) * embed_share, :]
            if w == 0:
                tails[w, embed_share:, :] = small[...].astype(low)
            else:
                tails[w, embed_share:, :] = jnp.zeros((SMALL, width), low)

    embed_loads = [
        pltpu.make_async_copy(src, dst, embed_sem.at[i])
        for i, (src, dst) in enumerate(((dx_h, dx), (feat_h, feat), (embw_h, embw)))
    ]

    for d in range(2):
        load_operands(d, 0)
    for copy in embed_loads:
        copy.start()
    pl.semaphore_wait(barrier, jnp.where(section == 0, 4, 3))
    for d in range(2):
        products(d, 0, functools.partial(load_operands, d, 1))
    for d in range(2):
        part_copy(d, 0).wait_recv()
        for q in range(pieces):
            reduce_main(q, d, 0, begin=True)

    def prefetch_after(d, s):
        @pl.when(s < n)
        def _():
            load_operands(d, s)

    for d in range(2):
        products(d, 1, functools.partial(prefetch_after, d, 2))
    for copy in embed_loads:
        copy.wait()
    embed_back()

    def send_tails(s, carry):
        for d in range(2):
            tail_part_copy(d, s).start()
        return carry

    lax.fori_loop(0, n, send_tails, 0)

    def scatter_step(s, carry):
        for q in range(pieces):
            for d in range(2):
                if q == 0:
                    part_copy(d, s).wait_recv()
                reduce_main(q, d, s)

        for d in range(2):
            @pl.when(s > 1)
            def _():
                part_copy(d, s - 2).wait_send()
                for q in range(pieces):
                    ring_copy(q, d, s - 2).wait_send()

            products(d, s + 1, functools.partial(prefetch_after, d, s + 2))

        for d in range(2):
            @pl.when(s == 1)
            def _():
                reduce_tail(d, 0, begin=True)

            @pl.when(s > 1)
            def _():
                reduce_tail(d, s - 1)
        return carry

    lax.fori_loop(1, n - 1, scatter_step, 0)
    for q in range(pieces):
        for d in range(2):
            if q == 0:
                part_copy(d, n - 1).wait_recv()
            reduce_main(q, d, n - 1, end=True)
    for d in range(2):
        reduce_tail(d, n - 2, begin=n == 2)

    def gather_step(q, d, t):
        gather_landed(q, d, t).wait_recv()

        @pl.when(t < n - 2)
        def _():
            gather_copy(q, d, t + 1).start()

        pair_copy(q, d, t + 1).start()
        if q == pieces:
            @pl.when(section == 0)
            def _():
                cross_copy(d, t + 1, True).start()

    def pass_pair(d, t):
        pair_landed(pieces, d, t).wait_recv()

        @pl.when(section == 0)
        def _():
            cross_copy(d, t, False).start()

    for q, d in mains:
        gather_step(q, d, 0)
    for d in range(2):
        reduce_tail(d, n - 1, end=True)

    def spread(t, carry):
        for q, d in mains:
            gather_step(q, d, t)
        for d in range(2):
            gather_step(pieces, d, t - 1)
            pass_pair(d, t - 1)
        return carry

    lax.fori_loop(1, n - 1, spread, 0)
    for d in range(2):
        gather_step(pieces, d, n - 2)
        pass_pair(d, n - 2)
    for d in range(2):
        pass_pair(d, n - 1)

    @pl.when(section == 0)
    def _():
        feat_keep.wait()
        feat_send.wait_send()

    @pl.when(section == 1)
    def _():
        feat_send.wait_recv()

    for q, d in streams:
        keep_copy(q, d).wait()
    for d in range(2):
        for s in range(max(n - 3, 0), n):
            part_copy(d, s).wait_send()
        for s in range(max(n - 3, 0), n - 1):
            for q in range(pieces):
                ring_copy(q, d, s).wait_send()

    def finish(s, carry):
        for d in range(2):
            tail_part_copy(d, s).wait_send()
            for q in range(pieces + 1):
                pair_copy(q, d, s).wait_send()
                if q < pieces:
                    pair_landed(q, d, s).wait_recv()

            @pl.when(s < n - 1)
            def _():
                ring_copy(pieces, d, s).wait_send()
                for q in range(pieces + 1):
                    gather_copy(q, d, s).wait_send()

            for mine in (True, False):
                @pl.when(section == 0)
                def _():
                    cross_copy(d, s, mine).wait_send()

                @pl.when(section == 1)
                def _():
                    cross_copy(d, s, mine).wait_recv()
        return carry

    lax.fori_loop(0, n, finish, 0)


def finish_kernel(
    blocks, total, tails, cross, out_in, feat_in,
    out, feat, embed, places, attend, project, up, down, embed_vectors, gains, vectors, up_bias, rms,
    coming, going, ends, wide_ends, out_hold, feat_hold, in_sem, out_sem, ends_sem, plain_sem,
    embed_sem,
):
    members, share, width = total.shape
    section = lax.axis_index("section")
    tail = tails.shape[1]
    embed_share = tail - SMALL
    held = [(out_in, out_hold, out), (feat_in, feat_hold, feat)]
    plain_in = [
        pltpu.make_async_copy(src, hold, plain_sem.at[i]) for i, (src, hold, _) in enumerate(held)
    ]
    plain_out = [
        pltpu.make_async_copy(hold, dst, plain_sem.at[2 + i])
        for i, (_, hold, dst) in enumerate(held)
    ]
    slots, unit = coming.shape[:2]
    per_block, per_member = width // unit, share // unit
    count = members * per_member

    def in_copy(u):
        slot = lax.rem(u, slots)
        row = pl.multiple_of(lax.rem(u, per_member) * unit, 16)
        return pltpu.make_async_copy(
            total.at[u // per_member, pl.ds(row, unit)], coming.at[slot], in_sem.at[slot])

    def out_copy(u, dst, row, column):
        slot = lax.rem(u, slots)
        return pltpu.make_async_copy(
            going.at[slot],
            dst.at[pl.ds(pl.multiple_of(row, 16), unit), pl.ds(pl.multiple_of(column, 128), width)],
            out_sem.at[slot])

    own_ends = pltpu.make_async_copy(tails, ends.at[0], ends_sem.at[0])
    far_ends = pltpu.make_async_copy(cross, ends.at[1], ends_sem.at[1])
    for u in range(slots):
        in_copy(u).start()
    own_ends.start()
    far_ends.start()
    for copy in plain_in:
        copy.start()

    def step(u, carry):
        slot = lax.rem(u, slots)
        in_copy(u).wait()

        @pl.when(u >= slots)
        def _():
            out_copy(u, project, 0, 0).wait()

        going[slot] = coming[slot].astype(jnp.float32)
        block, row = u // per_block, lax.rem(u, per_block) * unit

        @pl.when(block < 3)
        def _():
            out_copy(u, attend, row, block * width).start()

        @pl.when(block == 3)
        def _():
            out_copy(u, project, row, 0).start()

        @pl.when((block > 3) & (block < 4 + blocks))
        def _():
            out_copy(u, up, row, (block - 4) * width).start()

        @pl.when(block > 3 + blocks)
        def _():
            out_copy(u, down, (u - (4 + blocks) * per_block) * unit, 0).start()

        @pl.when(u + slots < count)
        def _():
            in_copy(u + slots).start()

        return carry

    lax.fori_loop(0, count, step, 0)
    for copy in plain_in:
        copy.wait()
    for copy in plain_out:
        copy.start()
    own_ends.wait()
    far_ends.wait()
    small = ends[0, 0, embed_share:, :].astype(jnp.float32)
    gains[...] = small[0:2, :]
    vectors[...] = small[2:8, :]
    for i in range(blocks):
        up_bias[:, i * width : (i + 1) * width] = small[8 + i : 9 + i, :]
    stat = small[15:16, :]
    rms[...] = jnp.sqrt(stat[:, 0:3] / (stat[:, 3:4] * width))
    embed_vectors[...] = ends[section, 0, embed_share:, :].astype(jnp.float32)[12:15, :]

    def widen(w, carry):
        wide_ends[w] = ends[section, w, 0:embed_share, :].astype(jnp.float32)
        return carry

    lax.fori_loop(0, members, widen, 0)
    per_weight = embed.shape[0] // embed_share
    leave = []
    for w in range(members):
        at = w if w < per_weight else w - per_weight
        dst = embed if w < per_weight else places
        leave.append(pltpu.make_async_copy(
            wide_ends.at[w], dst.at[pl.ds(at * embed_share, embed_share)], embed_sem.at[w]))
    for copy in leave:
        copy.start()
    for copy in leave + plain_out:
        copy.wait()
    for u in range(count - slots, count):
        out_copy(u, project, 0, 0).wait()


ANY = pl.BlockSpec(memory_space=pl.ANY)
VMEM = pl.BlockSpec(memory_space=pltpu.VMEM)
SMEM = pl.BlockSpec(memory_space=pltpu.SMEM)
LOW = jnp.bfloat16
WIDE = jnp.float32
PIECES = 2


def shaped(kind, *dims):
    return jax.ShapeDtypeStruct(dims, kind)


def run_forward(features, masked, valid, kinds, embed_weight, embed_vectors, pos_embed, norm_gains,
                vectors, qkv_weight, out_weight, up_weight, up_bias, down_weight):
    clips, length, feat_width = features.shape
    width, feed = up_weight.shape[1:]
    blocks = feed // width
    dma = pltpu.SemaphoreType.DMA
    vm = pltpu.VMEM
    return pl.pallas_call(
        forward_kernel,
        out_shape=(
            shaped(LOW, 3 + blocks, clips * length, width),
            shaped(WIDE, clips, length, width),
            shaped(LOW, clips, length, 3 * width),
            shaped(LOW, clips, H, length, length),
            shaped(WIDE, clips, length, width),
            shaped(LOW, clips, length, feed),
            shaped(LOW, clips, length, width // 2),
            shaped(WIDE, clips, length, 128),
            shaped(WIDE, 8, width),
        ),
        in_specs=[SMEM] + [ANY] * 13,
        out_specs=(ANY,) * 7 + (VMEM,) * 2,
        scratch_shapes=[
            vm(features.shape, LOW), vm(masked.shape, jnp.int32), vm(valid.shape, jnp.int32),
            vm(embed_weight.shape, LOW), vm(embed_vectors.shape, WIDE), vm(pos_embed.shape, WIDE),
            vm(norm_gains.shape[1:], WIDE), vm(vectors.shape[1:], WIDE),
            vm((width, 3 * width), LOW), vm((width, width), LOW), vm((width, feed), LOW),
            vm(up_bias.shape, WIDE), vm((feed, width), LOW),
            vm((feat_width, width), LOW), vm((clips, 1, length), WIDE),
            vm((length, width), WIDE), vm((length, width), LOW), vm((length, 3 * width), LOW),
            vm((2, 2, length, length), LOW), vm((length, width), LOW), vm((length, width), WIDE),
            vm((length, width), LOW), vm((length, feed), LOW), vm((length, feed), LOW),
            vm((clips, length, width), LOW), vm((clips, length, width), LOW),
            dma((13,)), dma((7 + blocks,)), dma((2,)), dma((clips, 2)), dma((clips, 2)),
            dma((clips, 2)), dma((clips, 2)), dma((clips, 2)),
        ],
        compiler_params=pltpu.CompilerParams(
            collective_id=1, has_side_effects=True, vmem_limit_bytes=56 * 2**20
        ),
    )(kinds, features, masked, valid, embed_weight, embed_vectors, pos_embed, norm_gains, vectors,
      qkv_weight, out_weight, up_weight, up_bias, down_weight)


def run_backward(cotangent, weights, x, qkv, probs, middle, slope, left, gains):
    clips, length, width = cotangent.shape
    feed = weights[2].shape[2]
    blocks = feed // width
    dma = pltpu.SemaphoreType.DMA
    vm = pltpu.VMEM
    return pl.pallas_call(
        backward_kernel,
        out_shape=(
            shaped(LOW, 5 + blocks, clips * length, width),
            shaped(LOW, clips, length, width),
            shaped(LOW, left.shape[0], width, clips * length),
            shaped(WIDE, 8, width),
            shaped(WIDE, 1, feed),
        ),
        in_specs=[ANY] * 12,
        out_specs=(ANY, ANY, ANY, VMEM, VMEM),
        scratch_shapes=[
            vm((width, 3 * width), LOW), vm((width, width), LOW), vm((width, feed), LOW),
            vm((feed, width), LOW), vm(gains.shape[1:], WIDE),
            vm((clips, length, width), WIDE), vm((clips, length, 3 * width), LOW),
            vm((3, 2, length, length), LOW), vm((clips, length, width), WIDE),
            vm((clips, length, feed), LOW), vm((clips, length, width), LOW),
            vm((length, feed), LOW), vm((length, width), WIDE), vm((length, width), WIDE),
            vm((length, width), LOW), vm((length, width), LOW), vm((length, 3 * width), LOW),
            vm((clips, length, width), LOW),
            vm((clips * length, width), LOW), vm((width, clips * length), LOW),
            dma((2,)), dma((5,)), dma((clips, 5)), dma((3,)), dma((5 + blocks,)), dma((clips,)),
            dma((clips, 2)), dma((clips, 2)),
        ],
        compiler_params=pltpu.CompilerParams(
            collective_id=2, has_side_effects=True, vmem_limit_bytes=60 * 2**20
        ),
    )(cotangent, *weights, x, qkv, probs, middle, slope, left, gains)


def run_sums(members, kinds, turned, right, dx, features, embed_weight, cols, small, up_sums, stats):
    width, rows = turned.shape[1:]
    clips, length, feat_width = features.shape
    n = members // 2
    share = 12 * width // members
    embed_rows = 2 * feat_width + length
    tail = embed_rows // members + SMALL
    unit = unit_rows(members, width)
    per_member = share // unit
    half = width // 2
    dma = pltpu.SemaphoreType.DMA
    vm = pltpu.VMEM
    sems = [dma((2, 2 * per_member + 2)), dma((3,)), dma((2, 2 * n)), dma((2, 2 * n))]
    sems += [dma((2, PIECES + 1, n)) for _ in range(6)]
    sems += [dma((2, PIECES + 1)), dma((2, 2, n)), dma((2, 2, n)), dma((3,))]
    return pl.pallas_call(
        functools.partial(sums_kernel, members),
        out_shape=(
            shaped(LOW, members, share, width),
            shaped(LOW, members, tail, width),
            shaped(LOW, members, tail, width),
            shaped(LOW, clips, length, feat_width // 2),
        ),
        in_specs=[SMEM] + [ANY] * 5 + [VMEM] * 4,
        out_specs=(ANY,) * 4,
        scratch_shapes=[
            vm((2, 2 * per_member, unit, rows), LOW), vm((2, 2, rows, half), LOW),
            vm((2, 3, 2, share, half), LOW),
            vm((2, n, share, half), LOW), vm((2, n - 1, share, half), LOW),
            vm((members, tail, width), LOW), vm((2, n, tail, half), LOW),
            vm((2, n, tail, half), LOW), vm((2, n - 1, tail, half), LOW),
            vm((clips, length, width), LOW), vm(features.shape, LOW), vm(embed_weight.shape, LOW),
            vm(features.shape, LOW), vm((embed_rows, width), LOW), vm((SMALL, width), WIDE),
            sems,
        ],
        compiler_params=pltpu.CompilerParams(
            collective_id=0, has_side_effects=True, vmem_limit_bytes=60 * 2**20
        ),
    )(kinds, turned, right, dx, features, embed_weight, cols, small, up_sums, stats)


def run_finish(total, tails, cross, output, feature_out, feed, feat_width):
    members, share, width = total.shape
    unit = unit_rows(members, width)
    blocks = feed // width
    embed_share = tails.shape[1] - SMALL
    places = members * embed_share - 2 * feat_width
    slots = 12
    dma = pltpu.SemaphoreType.DMA
    vm = pltpu.VMEM
    return pl.pallas_call(
        functools.partial(finish_kernel, blocks),
        out_shape=(
            shaped(LOW, *output.shape), shaped(LOW, *feature_out.shape),
            shaped(WIDE, 2 * feat_width, width), shaped(WIDE, places, width),
            shaped(WIDE, width, 3 * width), shaped(WIDE, width, width),
            shaped(WIDE, width, feed), shaped(WIDE, feed, width),
            shaped(WIDE, 3, width), shaped(WIDE, 2, width), shaped(WIDE, 6, width),
            shaped(WIDE, 1, feed), shaped(WIDE, 1, 3),
        ),
        in_specs=[ANY] * 5,
        out_specs=(ANY,) * 8 + (VMEM,) * 5,
        scratch_shapes=[
            vm((slots, unit, width), LOW), vm((slots, unit, width), WIDE),
            vm((2, *tails.shape), LOW), vm((members, embed_share, width), WIDE),
            vm(output.shape, LOW), vm(feature_out.shape, LOW),
            dma((slots,)), dma((slots,)), dma((2,)), dma((4,)), dma((members,)),
        ],
        compiler_params=pltpu.CompilerParams(vmem_limit_bytes=56 * 2**20),
    )(total, tails, cross, output, feature_out)


def local(
    features,
    masked,
    valid,
    kinds,
    embed_weight,
    embed_vectors,
    pos_embed,
    norm_gains,
    vectors,
    qkv_weight,
    out_weight,
    up_weight,
    up_bias,
    down_weight,
    cotangent,
):
    members = lax.axis_size("wide")
    clips, length, feat_width = features.shape
    width = pos_embed.shape[1]
    feed = up_weight.shape[2]
    left, x, qkv, probs, middle, slope, output, cols, stats = run_forward(
        features, masked, valid, kinds, embed_weight, embed_vectors, pos_embed, norm_gains, vectors,
        qkv_weight, out_weight, up_weight, up_bias, down_weight)
    weights = (qkv_weight, out_weight, up_weight, down_weight)
    right, dx, turned, small, up_sums = run_backward(
        cotangent, weights, x, qkv, probs, middle, slope, left, norm_gains)
    total, tails, cross, feature_out = run_sums(
        members, kinds, turned, right, dx, features, embed_weight, cols, small, up_sums, stats)
    (output, feature_out, embed, places, attend, project, up, down, embed_rows, gain_rows,
     vector_rows, up_rows, rms) = run_finish(
        total, tails, cross, output, feature_out, feed, feat_width)
    return (
        output,
        feature_out,
        embed.reshape(2, feat_width, width),
        embed_rows,
        places,
        gain_rows[None],
        vector_rows[None],
        attend[None],
        project[None],
        up[None],
        up_rows,
        down[None],
        rms,
    )


def solution(mesh):
    return jax.shard_map(
        local,
        mesh=mesh,
        in_specs=(
            P("wide", None, None),
            P("wide", None),
            P("wide", None),
            P("wide"),
            P(),
            P(),
            P(),
            P("section", None, None),
            P("section", None, None),
            P("section", None, None),
            P("section", None, None),
            P("section", None, None),
            P("section", None),
            P("section", None, None),
            P("wide", None, None),
        ),
        out_specs=(
            P("wide", None, "section"),
            P("wide", None, "section"),
            P(),
            P(),
            P(),
            P("section", None, None),
            P("section", None, None),
            P("section", None, None),
            P("section", None, None),
            P("section", None, None),
            P("section", None),
            P("section", None, None),
            P("section", None),
        ),
        check_vma=False,
    )
```

```python
import functools
import math

import jax
import jax.numpy as jnp
from jax import lax
from jax.experimental import pallas as pl
from jax.experimental.pallas import tpu as pltpu
from jax.sharding import PartitionSpec as P

H = 12
HD = 64
EPS = 1e-06
NEG = -1000000000.0


MESH = pl.DeviceIdType.MESH
SMALL = 16


def unit_rows(members, width):
    return math.gcd(12 * width // members, width)


def dot_nn(left, right):
    return jnp.dot(left, right, preferred_element_type=jnp.float32)


def dot_nt(left, right):
    return lax.dot_general(
        left, right, (((1,), (1,)), ((), ())), preferred_element_type=jnp.float32
    )


def tile_of(index, size):
    if isinstance(index, int):
        return pl.ds(index * size, size)
    return pl.ds(pl.multiple_of(index * size, size), size)


def loop(count, body, unroll):
    if count == unroll:
        for i in range(count):
            body(i, 0)
        return

    def step(i, carry):
        for u in range(unroll):
            body(i * unroll + u, 0)
        return carry

    lax.fori_loop(0, count // unroll, step, 0)


def column_sum(values):
    return jnp.sum(values, axis=0, keepdims=True)


def row_mean(values):
    return jnp.mean(values, axis=-1, keepdims=True)


def pick_kind(kind, first, second):
    keep = (kind == 0).astype(jnp.float32)
    return first.astype(jnp.float32) * keep + second.astype(jnp.float32) * (1.0 - keep)


def gelu_pair(hidden):
    decay = jnp.exp(-0.5 * hidden * hidden)
    cdf = 0.5 + 0.5 * lax.erf(hidden * 0.5**0.5)
    return hidden * cdf, cdf + hidden * decay * 0.3989422804014327


def fetch(pairs, sems):
    copies = [pltpu.make_async_copy(src, dst, sems.at[i]) for i, (src, dst) in enumerate(pairs)]
    for copy in copies:
        copy.start()
    return copies


def greet_partner():
    barrier = pltpu.get_barrier_semaphore()
    pl.semaphore_signal(
        barrier, inc=1, device_id={"section": 1 - lax.axis_index("section")}, device_id_type=MESH
    )
    pl.semaphore_wait(barrier, 1)


def to_partner(src, dst, send, recv):
    return pltpu.make_async_remote_copy(
        src_ref=src, dst_ref=dst, send_sem=send, recv_sem=recv,
        device_id={"section": 1 - lax.axis_index("section")}, device_id_type=MESH)


def forward_kernel(
    kinds, feat_h, masked_h, valid_h, embw_h, embv_h, pos_h, gains_h, vectors_h, wqkv_h, wout_h,
    wup_h, upb_h, wdown_h,
    left_h, x_h, qkv_h, probs_h, inverse_h, exact_h, middle_h, slope_h, out_h, cols, stats,
    feat, masked, valid, embw, embv, pos, gains, vectors, wqkv, wout, wup, up_bias, wdown,
    chosen, dead_keys, inverse, exact,
    x, normed, qkv, probs, context, middle, hidden_in, active, slope, y, landed,
    load_sem, save_sem, probs_sem, send_sem, recv_sem, back_send, back_recv, keep_sem,
):
    low = jnp.bfloat16
    section = lax.axis_index("section")
    clips, length, width = landed.shape
    half = length // 2
    feed = wup.shape[1]
    heads2 = width // 128
    blocks = feed // width
    loads = fetch(
        [(masked_h, masked), (valid_h, valid), (gains_h.at[0], gains),
         (vectors_h, vectors), (upb_h, up_bias),
         (feat_h, feat), (embw_h, embw), (embv_h, embv), (pos_h, pos),
         (wqkv_h.at[0], wqkv), (wout_h.at[0], wout), (wup_h.at[0], wup), (wdown_h.at[0], wdown)],
        load_sem)
    greet_partner()
    stats[...] = jnp.zeros_like(stats)
    for copy in loads[:9]:
        copy.wait()
    sublane = lax.broadcasted_iota(jnp.int32, (128, length), 0)
    for c in range(clips):
        flags = jnp.where(sublane == 0, masked[c : c + 1, :], 0)
        flags = jnp.where(sublane == 1, valid[c : c + 1, :], flags)
        cols[c] = flags.astype(jnp.float32).T
    low_lanes = lax.broadcasted_iota(jnp.int32, (1, 128), 1) < HD

    def save(index, src, dst):
        return pltpu.make_async_copy(src, dst, save_sem.at[index])

    def saves(c):
        rows = pl.ds(pl.multiple_of(c * length, length), length)
        pairs = [
            (x, x_h.at[c]), (normed, left_h.at[0, rows]), (qkv, qkv_h.at[c]),
            (context, left_h.at[1, rows]), (middle, middle_h.at[c]),
            (hidden_in, left_h.at[2, rows]), (slope, slope_h.at[c]),
        ] + [
            (active.at[:, pl.ds(b * width, width)], left_h.at[3 + b, rows]) for b in range(blocks)
        ] + [(inverse, inverse_h.at[c]), (exact, exact_h.at[c])]
        return [save(i, src, dst) for i, (src, dst) in enumerate(pairs)]

    def probs_save(c, pair):
        slot = lax.rem(pair, 2)
        return pltpu.make_async_copy(
            probs.at[slot], probs_h.at[c, pl.ds(pair * 2, 2)], probs_sem.at[slot])

    def send_half(c, h):
        rows = pl.ds(h * half, half)
        return to_partner(
            y.at[c, rows], landed.at[c, rows], send_sem.at[c, h], recv_sem.at[c, h])

    def back_half(c, h):
        rows = pl.ds(h * half, half)
        return to_partner(
            y.at[c, rows, pl.ds(0, width // 2)], out_h.at[c, rows],
            back_send.at[c, h], back_recv.at[c, h])

    def keep_half(c, h):
        rows = pl.ds(h * half, half)
        return pltpu.make_async_copy(
            y.at[c, rows, pl.ds(width // 2, width // 2)], out_h.at[c, rows], keep_sem.at[c, h])

    def clip(c, carry):
        def after_first(index):
            @pl.when(c > 0)
            def _():
                saves(c - 1)[index].wait()

        after_first(0)
        after_first(1)

        @pl.when(section == 0)
        def _():
            chosen[...] = pick_kind(kinds[c], embw[0], embw[1]).astype(low)
            offset = pick_kind(kinds[c], embv[0:1, :], embv[1:2, :])

            def tile(i, carry):
                rows = tile_of(i, 128)
                lifted = dot_nn(feat[c, rows, :], chosen[...]) + offset
                hidden = cols[c, rows, :][:, 0:1]
                x[rows, :] = jnp.where(hidden > 0.0, embv[2:3, :], lifted) + pos[rows, :]
                return carry

            loop(length // 128, tile, 4)

        @pl.when(section == 1)
        def _():
            for h in range(2):
                send_half(c, h).wait_recv()

            def tile(i, carry):
                rows = tile_of(i, 64)
                x[rows, :] = landed[c, rows, :].astype(jnp.float32)
                return carry

            loop(length // 64, tile, 4)

        own = saves(c)
        own[0].start()

        def norm_rows(source, target, which, shift, first, count):
            gain, offset = gains[which : which + 1, :], vectors[shift]

            def tile(i, carry):
                rows = tile_of(i, 64)
                values = source[rows, :]
                values = values - row_mean(values)
                scale = lax.rsqrt(row_mean(values * values) + EPS)
                target[rows, :] = (values * scale * gain + offset).astype(low)
                return carry

            loop(count, lambda i, carry: tile(first + i, carry), 4)

        norm_rows(x, normed, 0, 0, 0, length // 64)
        own[1].start()
        after_first(2)

        @pl.when(c == 0)
        def _():
            loads[9].wait()

        def qkv_tile(j, carry):
            at = tile_of(j, 256)
            part = dot_nn(normed[...], wqkv[:, at])
            if j < width // 256:
                part = part + vectors[1, :, at]
            elif j >= 2 * width // 256:
                part = part + vectors[2, :, tile_of(j - 2 * width // 256, 256)]
            qkv[:, at] = part.astype(low)
            return carry

        loop(3 * width // 256, qkv_tile, 9)
        own[2].start()
        after_first(3)
        after_first(7 + blocks)
        after_first(8 + blocks)

        lane = lax.broadcasted_iota(jnp.int32, (1, 128), 1)
        scale, one, zero = (jnp.full((1, 128), v, low) for v in (HD**-0.5, 1.0, 0.0))
        dead_keys[...] = jnp.broadcast_to(
            jnp.where(cols[c][:, 1:2] > 0.0, 0.0, NEG), dead_keys.shape).astype(low)

        def attend(pair, carry):
            @pl.when((pair > 1) | (c > 0))
            def _():
                probs_save(c, pair).wait()

            at = tile_of(pair, 128)
            queries = qkv[:, at]
            keys_in = qkv[:, tile_of(pair + heads2, 128)]
            values_in = qkv[:, tile_of(pair + 2 * heads2, 128)]
            outs = []
            for h in range(2):
                mine = low_lanes == (h == 0)
                extra = lane == (64 if h == 0 else 0)
                scaled = jnp.where(mine, queries * scale, jnp.where(extra, one, zero))
                scores = dot_nt(scaled, jnp.where(extra, dead_keys[...], keys_in))
                top = jnp.max(scores, axis=-1, keepdims=True)
                soft = jnp.exp(scores - top).astype(low)
                probs[lax.rem(pair, 2), h] = soft
                outs.append(dot_nn(soft, jnp.where(mine, values_in, one)))
            total = pltpu.roll(jnp.where(low_lanes, outs[1], outs[0]), 64, 1)
            scale_back = 1.0 / total
            inverse[:, at] = scale_back
            mixed = jnp.where(low_lanes, outs[0], outs[1]) * scale_back
            exact[:, at] = mixed
            context[:, at] = mixed.astype(low)
            probs_save(c, pair).start()
            return carry

        lax.fori_loop(0, heads2, attend, 0)
        own[3].start()
        own[7 + blocks].start()
        own[8 + blocks].start()
        after_first(4)

        @pl.when(c == 0)
        def _():
            loads[10].wait()

        live = cols[c][:, 1:2]

        def out_tile(j, carry):
            at = tile_of(j, 256)
            branch = dot_nn(context[...], wout[:, at]) + vectors[3, :, at]
            middle[:, at] = x[:, at] + branch
            stats[1:2, at] += column_sum(branch * branch * live)
            return carry

        loop(width // 256, out_tile, 3)
        own[4].start()
        for index in range(5, 7 + blocks):
            after_first(index)

        @pl.when(c == 0)
        def _():
            loads[11].wait()
            loads[12].wait()

        for h in range(2):
            rows = pl.ds(h * half, half)
            norm_rows(middle, hidden_in, 1, 4, h * (half // 64), half // 64)
            if h == 1:
                own[5].start()

            def up_tile(j, carry):
                at = tile_of(j, 256)
                hidden = dot_nn(hidden_in[rows, :], wup[:, at]) + up_bias[:, at]
                value, steep = gelu_pair(hidden)
                active[rows, at] = value.astype(low)
                slope[rows, at] = steep.astype(low)
                return carry

            loop(feed // 256, up_tile, 12)
            if h == 1:
                for copy in own[6 : 7 + blocks]:
                    copy.start()

            def down_tile(j, carry):
                at = tile_of(j, 256)
                mixer = dot_nn(active[rows, :], wdown[:, at]) + vectors[5, :, at]
                total = middle[rows, at] + mixer
                flags = cols[c, rows, :][:, 1:2]
                stats[0:1, at] += column_sum(total * total * flags)
                stats[2:3, at] += column_sum(mixer * mixer * flags)
                y[c, rows, at] = total.astype(low)
                return carry

            loop(width // 256, down_tile, 3)

            @pl.when(section == 0)
            def _():
                send_half(c, h).start()

            @pl.when(section == 1)
            def _():
                back_half(c, h).start()
                keep_half(c, h).start()
        return carry

    lax.fori_loop(0, clips, clip, 0)
    for pair in (heads2 - 2, heads2 - 1):
        probs_save(clips - 1, pair).wait()
    for copy in saves(clips - 1):
        copy.wait()
    for c in range(clips):
        for h in range(2):
            @pl.when(section == 0)
            def _():
                send_half(c, h).wait_send()
                back_half(c, h).wait_recv()

            @pl.when(section == 1)
            def _():
                back_half(c, h).wait_send()
                keep_half(c, h).wait()


def backward_kernel(
    cot_h, wqkv_h, wout_h, wup_h, wdown_h, x_h, qkv_h, probs_h, inverse_h, exact_h, middle_h, slope_h, left_h, gains_h,
    right_h, dx_h, turned_h, small, up_sums,
    wqkv, wout, wup, wdown, gains, x, qkv, probs, inverse, context, middle, slope, g,
    d_hidden, wide_grad, d_middle, d_branch, d_context, d_qkv, d_low, upright, turned,
    turn_sem, load_sem, state_sem, probs_sem, save_sem, dx_sem, send_sem, recv_sem,
):
    low = jnp.bfloat16
    f32 = jnp.float32
    section = lax.axis_index("section")
    clips, length, width = g.shape
    half = length // 2
    feed = wup.shape[1]
    heads2 = width // 128
    blocks = feed // width
    greet_partner()

    def cot_load(c):
        return pltpu.make_async_copy(cot_h.at[c], g.at[c], state_sem.at[c, 0])

    def state_loads(c):
        pairs = [(slope_h, slope), (middle_h, middle), (qkv_h, qkv), (x_h, x), (inverse_h, inverse),
                 (exact_h, context)]
        return [
            pltpu.make_async_copy(src.at[c], dst.at[c], state_sem.at[c, 1 + i])
            for i, (src, dst) in enumerate(pairs)
        ]

    @pl.when(section == 1)
    def _():
        cot_load(0).start()

    loads = fetch(
        [(gains_h.at[0], gains), (wdown_h.at[0], wdown), (wup_h.at[0], wup), (wout_h.at[0], wout),
         (wqkv_h.at[0], wqkv)], load_sem)
    for c in range(clips):
        for copy in state_loads(c):
            copy.start()

    @pl.when(section == 1)
    def _():
        for c in range(1, clips):
            cot_load(c).start()

    small[...] = jnp.zeros_like(small)
    up_sums[...] = jnp.zeros_like(up_sums)
    low_lanes = lax.broadcasted_iota(jnp.int32, (1, 128), 1) < HD
    slots = probs.shape[0]
    pairs_total = clips * heads2

    def probs_load(step):
        slot = lax.rem(step, slots)
        return pltpu.make_async_copy(
            probs_h.at[step // heads2, pl.ds(lax.rem(step, heads2) * 2, 2)],
            probs.at[slot], probs_sem.at[slot])

    for step in range(slots):
        probs_load(step).start()

    def saves(c):
        rows = pl.ds(pl.multiple_of(c * length, length), length)
        pairs = [(d_qkv.at[:, pl.ds(b * width, width)], right_h.at[b, rows]) for b in range(3)]
        pairs += [(d_branch, right_h.at[3, rows])]
        pairs += [
            (d_hidden.at[:, pl.ds(b * width, width)], right_h.at[4 + b, rows])
            for b in range(blocks)
        ]
        pairs += [(g.at[c], right_h.at[4 + blocks, rows])]
        return [pltpu.make_async_copy(s, d, save_sem.at[i]) for i, (s, d) in enumerate(pairs)]

    def send_half(c, h):
        rows = pl.ds(h * half, half)
        return to_partner(
            d_low.at[c, rows], g.at[c, rows], send_sem.at[c, h], recv_sem.at[c, h])

    def dx_save(c):
        return pltpu.make_async_copy(d_low.at[c], dx_h.at[c], dx_sem.at[c])

    def norm_back(source, carried, which, shift_row, rows, take):
        gain = gains[which : which + 1, :]
        values = source[rows, :]
        values = values - row_mean(values)
        scale = lax.rsqrt(row_mean(values * values) + EPS)
        values = values * scale
        grad = wide_grad[rows, :]
        small[which : which + 1, :] += column_sum(grad * values)
        small[shift_row : shift_row + 1, :] += column_sum(grad)
        grad = grad * gain
        return carried + scale * (grad - row_mean(grad) - values * row_mean(grad * values))

    def turn_lefts():
        def block(b, carry):
            come = pltpu.make_async_copy(left_h.at[b], upright, turn_sem.at[0])
            come.start()
            come.wait()

            def piece(i, carry):
                at = tile_of(i, 128)
                turned[at, :] = upright[:, at].T
                return carry

            loop(width // 128, piece, 2)
            leave = pltpu.make_async_copy(turned, turned_h.at[b], turn_sem.at[1])
            leave.start()
            leave.wait()
            return carry

        lax.fori_loop(0, left_h.shape[0], block, 0)

    @pl.when(section == 0)
    def _():
        turn_lefts()

    def clip(c, carry):
        def after_first(lo, hi):
            @pl.when(c > 0)
            def _():
                for copy in saves(c - 1)[lo:hi]:
                    copy.wait()

        after_first(4, 5 + blocks)

        @pl.when(section == 1)
        def _():
            cot_load(c).wait()

        state = state_loads(c)
        own = saves(c)

        @pl.when(c == 0)
        def _():
            for copy in loads[:3]:
                copy.wait()

        state[0].wait()
        state[1].wait()
        for h in range(2):
            rows = pl.ds(h * half, half)

            @pl.when(section == 0)
            def _():
                send_half(c, h).wait_recv()

            if h == 1:
                own[-1].start()

            def feed_tile(j, carry):
                at = tile_of(j, 256)
                d_active = dot_nt(g[c, rows, :], wdown[at, :])
                grad = (slope[c, rows, at].astype(f32) * d_active).astype(low)
                d_hidden[rows, at] = grad
                up_sums[:, at] += column_sum(grad.astype(f32))
                return carry

            loop(feed // 256, feed_tile, 12)

            def in_tile(j, carry):
                at = tile_of(j, 256)
                wide_grad[rows, at] = dot_nt(d_hidden[rows, :], wup[at, :])
                return carry

            loop(width // 256, in_tile, 3)

        after_first(3, 4)
        for copy in own[4:-1]:
            copy.start()

        def middle_tile(i, carry):
            rows = tile_of(i, 64)
            grad_in = g[c, rows, :].astype(f32)
            total = norm_back(middle.at[c], grad_in, 1, 6, rows, None)
            d_middle[rows, :] = total
            rounded = total.astype(low)
            d_branch[rows, :] = rounded
            small[5:6, :] += column_sum(rounded.astype(f32))
            small[7:8, :] += column_sum(grad_in)
            return carry

        loop(length // 64, middle_tile, 4)
        own[3].start()

        @pl.when(c == 0)
        def _():
            loads[3].wait()

        def context_tile(j, carry):
            at = tile_of(j, 256)
            d_context[:, at] = dot_nt(d_branch[...], wout[at, :]).astype(low)
            return carry

        loop(width // 256, context_tile, 3)
        state[2].wait()
        state[4].wait()
        state[5].wait()
        after_first(0, 3)

        def attend(pair, carry):
            step = c * heads2 + pair
            slot = lax.rem(step, slots)
            probs_load(step).wait()
            at, key_at = tile_of(pair, 128), tile_of(pair + heads2, 128)
            value_at = tile_of(pair + 2 * heads2, 128)
            queries, keys_in, values_in = qkv[c, :, at], qkv[c, :, key_at], qkv[c, :, value_at]
            grad_wide = d_context[:, at].astype(f32) * inverse[c, :, at]
            grad = grad_wide.astype(low)
            along = grad.astype(f32) * context[c, :, at]
            queries_t, grad_t = queries.T, grad.T
            d_queries, keys_t, values_t = [], [], []
            for h in range(2):
                mine = low_lanes == (h == 0)
                soft = probs[slot, h]
                delta = jnp.sum(jnp.where(mine, along, 0.0), axis=-1, keepdims=True)
                d_soft = dot_nt(jnp.where(mine, grad, jnp.zeros_like(grad)), values_in)
                d_scores = (soft.astype(f32) * (d_soft - delta)).astype(low)
                part = slice(h * HD, (h + 1) * HD)
                values_t.append(dot_nn(grad_t[part], soft))
                keys_t.append(dot_nn(queries_t[part], d_scores))
                d_queries.append(dot_nn(d_scores, keys_in))
            scale = HD**-0.5
            query_grad = (jnp.where(low_lanes, d_queries[0], d_queries[1]) * scale).astype(low)
            value_grad = jnp.concatenate(values_t, axis=0).T.astype(low)
            d_qkv[:, at] = query_grad
            d_qkv[:, key_at] = (jnp.concatenate(keys_t, axis=0) * scale).T.astype(low)
            d_qkv[:, value_at] = value_grad
            small[3:4, at] += column_sum(query_grad.astype(f32))
            small[4:5, at] += column_sum(value_grad.astype(f32))

            @pl.when(step + slots < pairs_total)
            def _():
                probs_load(step + slots).start()

            return carry

        lax.fori_loop(0, heads2, attend, 0)
        for copy in own[:3]:
            copy.start()

        @pl.when(c == 0)
        def _():
            loads[4].wait()

        state[3].wait()
        for h in range(2):
            rows = pl.ds(h * half, half)

            def in_tile(j, carry):
                at = tile_of(j, 256)
                wide_grad[rows, at] = dot_nt(d_qkv[rows, :], wqkv[at, :])
                return carry

            loop(width // 256, in_tile, 3)

            def last_tile(i, carry):
                part = tile_of(i, 64)
                total = norm_back(x.at[c], d_middle[part, :], 0, 2, part, None)
                d_low[c, part, :] = total.astype(low)
                return carry

            loop(half // 64, lambda i, carry: last_tile(h * (half // 64) + i, carry), 4)

            @pl.when(section == 1)
            def _():
                send_half(c, h).start()

        dx_save(c).start()
        return carry

    lax.fori_loop(0, clips, clip, 0)

    @pl.when(section == 1)
    def _():
        turn_lefts()

    for copy in saves(clips - 1):
        copy.wait()
    for c in range(clips):
        dx_save(c).wait()
        for h in range(2):
            @pl.when(section == 1)
            def _():
                send_half(c, h).wait_send()


def sums_kernel(
    members, kinds, turned_h, right_h, dx_h, feat_h, embw_h, cols, small_in, up_sums, stats,
    o_ref, t_ref, e_ref, h_ref,
    lefts, rights, chunk, part, ring, tails, tail_own, tail_part, tail_ring,
    dx, feat, embw, feat_grad, embed, small, sems,
):
    (load_sem, embed_sem, part_send, part_recv, ring_send, ring_recv, gather_send, gather_recv,
     pair_send, pair_recv, keep_sem, cross_send, cross_recv, feat_sem) = sems
    low = jnp.bfloat16
    f32 = jnp.float32
    n = members // 2
    share, columns = chunk.shape[3:]
    width = 2 * columns
    tail = tails.shape[1]
    unit = unit_rows(members, width)
    per_block, per_member = width // unit, share // unit
    slots = chunk.shape[1]
    clips, length, feat_width = feat.shape
    me = lax.axis_index("wide")
    section = lax.axis_index("section")
    chip, core = me // 2, me % 2
    place = jnp.where(chip % 2 == 0, chip // 2, n - 1 - chip // 2)

    def member_at(position):
        position = lax.rem(position + 2 * n, n)
        return jnp.where(2 * position < n, 2 * position, 2 * (n - 1 - position) + 1) * 2 + core

    right, left = member_at(place + 1), member_at(place - 1)
    other = chip * 2 + 1 - core
    target = (right, left)

    barrier = pltpu.get_barrier_semaphore()
    for peer in (right, left, other):
        pl.semaphore_signal(barrier, inc=1, device_id={"wide": peer}, device_id_type=MESH)
    @pl.when(section == 1)
    def _():
        pl.semaphore_signal(barrier, inc=1, device_id={"section": 0}, device_id_type=MESH)

    pieces = ring_send.shape[1] - 1
    piece = -(-share // (16 * pieces)) * 16
    spans = [(q * piece, min(piece, share - q * piece)) for q in range(pieces)]
    mains = [(q, d) for q in range(pieces) for d in range(2)]
    streams = mains + [(pieces, 0), (pieces, 1)]

    def turn(position):
        return lax.rem(position + 2 * n, n)

    def reduce_at(d, step):
        return turn(place - step) if d == 0 else turn(place + step)

    def gather_at(d, index):
        return turn(place + 1 - index) if d == 0 else turn(place - 1 + index)

    def span(q):
        return pl.ds(*spans[q])

    def cols_of(d):
        return pl.ds(d * columns, columns)

    def remote(src, dst, send, recv, device):
        return pltpu.make_async_remote_copy(
            src_ref=src, dst_ref=dst, send_sem=send, recv_sem=recv,
            device_id=device, device_id_type=MESH)

    def block_of(spot):
        return spot // per_block

    def operand_copies(d, s):
        base = reduce_at(d, s) * 2 * per_member
        first, second = block_of(base), block_of(base + 2 * per_member - 1)
        copies = []
        for u in range(2 * per_member):
            block = block_of(base + u)
            source = jnp.where(
                block < 3, 0, jnp.where(block == 3, 1, jnp.where(block < 8, 2, block - 5)))
            row = pl.multiple_of(lax.rem(base + u, per_block) * unit, 16)
            copies.append(pltpu.make_async_copy(
                turned_h.at[source, pl.ds(row, unit)], lefts.at[d, u], load_sem.at[d, u]))
        for i, block in enumerate((first, second)):
            copies.append(pltpu.make_async_copy(
                right_h.at[jnp.minimum(block, 8), :, cols_of(d)], rights.at[d, i],
                load_sem.at[d, 2 * per_member + i]))
        return copies

    def load_operands(d, s):
        for copy in operand_copies(d, s):
            copy.start()

    def part_copy(d, s):
        return remote(
            chunk.at[d, lax.rem(s, slots), 1 - core], part.at[d, s], part_send.at[d, s], part_recv.at[d, s],
            {"wide": other})

    def ring_copy(q, d, s):
        if q == pieces:
            src, dst = tail_own.at[d, s], tail_ring.at[d, s]
        else:
            src, dst = chunk.at[d, lax.rem(s, slots), core, span(q)], ring.at[d, s, span(q)]
        return remote(src, dst, ring_send.at[d, q, s], ring_recv.at[d, q, s],
                      {"wide": target[d]})

    def products(d, s, prefetch):
        for copy in operand_copies(d, s):
            copy.wait()
        base = reduce_at(d, s) * 2 * per_member
        first = block_of(base)

        for u in range(0, 2 * per_member, 2):
            rows = lefts[d, u : u + 2].reshape(2 * unit, lefts.shape[3])
            tile = dot_nn(rows, rights[d, block_of(base + u) - first]).astype(low)
            for i in range(2):
                which, row = (u + i) // per_member, (u + i) % per_member * unit
                chunk[d, lax.rem(s, slots), which, pl.ds(row, unit), :] = (
                    tile[i * unit : (i + 1) * unit])
        part_copy(d, s).start()
        prefetch()

    def final_of(q, d):
        return tail_own.at[d, n - 1] if q == pieces else chunk.at[d, (n - 1) % slots, core, span(q)]

    def spot_of(q, d, index, which):
        member = gather_at(d, index) * 2 + which
        if q == pieces:
            return t_ref.at[member, :, cols_of(d)]
        return o_ref.at[member, span(q), cols_of(d)]

    def gather_copy(q, d, index, first=False):
        src = final_of(q, d) if first else spot_of(q, d, index, core)
        return remote(
            src, spot_of(q, d, index, core),
            gather_send.at[d, q, index], gather_recv.at[d, q, index], {"wide": target[d]})

    def gather_landed(q, d, index):
        return remote(
            final_of(q, d), spot_of(q, d, index + 1, core),
            gather_send.at[d, q, index], gather_recv.at[d, q, index], {"wide": target[d]})

    def pair_copy(q, d, index, first=False):
        src = final_of(q, d) if first else spot_of(q, d, index, core)
        return remote(
            src, spot_of(q, d, index, core),
            pair_send.at[d, q, index], pair_recv.at[d, q, index], {"wide": other})

    def pair_landed(q, d, index):
        return remote(
            final_of(q, d), spot_of(q, d, index, 1 - core),
            pair_send.at[d, q, index], pair_recv.at[d, q, index], {"wide": other})

    def keep_copy(q, d):
        return pltpu.make_async_copy(final_of(q, d), spot_of(q, d, 0, core), keep_sem.at[d, q])

    def cross_copy(d, index, mine, first=False):
        member = gather_at(d, index) * 2 + (core if mine else 1 - core)
        src = final_of(pieces, d) if first else t_ref.at[member, :, cols_of(d)]
        lane = 0 if mine else 1
        return remote(
            src, e_ref.at[member, :, cols_of(d)],
            cross_send.at[d, lane, index], cross_recv.at[d, lane, index],
            {"section": 1 - section})

    def hand_over(q, d):
        gather_copy(q, d, 0, True).start()
        pair_copy(q, d, 0, True).start()
        keep_copy(q, d).start()
        if q == pieces:
            @pl.when(section == 0)
            def _():
                cross_copy(d, 0, True, True).start()

    def reduce_main(q, d, s, begin=False, end=False):
        if not begin:
            ring_copy(q, d, s - 1).wait_recv()

        def add(tile, carry):
            at = pl.ds(pl.multiple_of(spans[q][0] + tile * 16, 16), 16)
            slot = lax.rem(s, slots)
            total = chunk[d, slot, core, at].astype(f32) + part[d, s, at].astype(f32)
            if not begin:
                total = total + ring[d, s - 1, at].astype(f32)
            chunk[d, slot, core, at] = total.astype(low)
            return carry

        loop(spans[q][1] // 16, add, 1)
        if end:
            hand_over(q, d)
        else:
            ring_copy(q, d, s).start()

    def tail_part_copy(d, s):
        return remote(
            tails.at[reduce_at(d, s) * 2 + 1 - core, :, cols_of(d)], tail_part.at[d, s],
            part_send.at[d, n + s], part_recv.at[d, n + s], {"wide": other})

    def reduce_tail(d, s, begin=False, end=False):
        tail_part_copy(d, s).wait_recv()
        total = tails[reduce_at(d, s) * 2 + core, :, cols_of(d)].astype(f32)
        total = total + tail_part[d, s].astype(f32)
        if not begin:
            ring_copy(pieces, d, s - 1).wait_recv()
            total = total + tail_ring[d, s - 1].astype(f32)
        tail_own[d, s] = total.astype(low)
        if end:
            hand_over(pieces, d)
        else:
            ring_copy(pieces, d, s).start()

    feat_half = h_ref.shape[2]
    feat_keep = pltpu.make_async_copy(
        feat_grad.at[:, :, pl.ds(0, feat_half)], h_ref, feat_sem.at[0])
    feat_send = remote(
        feat_grad.at[:, :, pl.ds(feat_half, feat_half)], h_ref, feat_sem.at[1], feat_sem.at[2],
        {"section": 1 - section})

    def embed_back():
        first = (1 - section).astype(f32)
        small[...] = jnp.zeros_like(small)
        small[0:8, :] = small_in[...]
        for i in range(up_sums.shape[1] // width):
            small[8 + i : 9 + i, :] = up_sums[:, i * width : (i + 1) * width]
        lane = lax.broadcasted_iota(jnp.int32, (1, width), 1)
        row = jnp.zeros((1, width), f32)
        for i in range(3):
            row = jnp.where(lane == i, jnp.sum(stats[i : i + 1, :], axis=1, keepdims=True), row)
        count = jnp.zeros((1, 1), f32)
        for c in range(clips):
            count = count + jnp.sum(cols[c][:, 1:2], axis=0, keepdims=True)
        small[15:16, :] = jnp.where(lane == 3, count, row)
        embed[...] = jnp.zeros_like(embed)

        @pl.when(section == 0)
        def _():
            weight_sum = [jnp.zeros((feat_width, width), f32)] * 2
            place_sum = jnp.zeros((length, width), f32)
            for c in range(clips):
                grad = dx[c]
                kept = jnp.where(cols[c][:, 0:1] > 0.0, jnp.zeros_like(grad), grad)
                chosen = pick_kind(kinds[c], embw[0], embw[1]).astype(low)
                feat_grad[c] = dot_nt(kept, chosen).astype(low)
                second = kinds[c].astype(f32)
                flags = (1.0 - second, second)
                wide = dot_nn(feat[c].T, kept)
                sums = column_sum(kept.astype(f32))
                for kind in range(2):
                    weight_sum[kind] = weight_sum[kind] + flags[kind] * wide
                    small[12 + kind : 13 + kind, :] += flags[kind] * sums
                small[14:15, :] += column_sum(grad.astype(f32)) - sums
                place_sum = place_sum + grad.astype(f32)
            embed[0:feat_width, :] = weight_sum[0].astype(low)
            embed[feat_width : 2 * feat_width, :] = weight_sum[1].astype(low)
            embed[2 * feat_width :, :] = place_sum.astype(low)
            feat_keep.start()
            feat_send.start()

        embed_share = tail - SMALL
        for w in range(members):
            tails[w, 0:embed_share, :] = embed[w * embed_share : (w + 1) * embed_share, :]
            if w == 0:
                tails[w, embed_share:, :] = small[...].astype(low)
            else:
                tails[w, embed_share:, :] = jnp.zeros((SMALL, width), low)

    embed_loads = [
        pltpu.make_async_copy(src, dst, embed_sem.at[i])
        for i, (src, dst) in enumerate(((dx_h, dx), (feat_h, feat), (embw_h, embw)))
    ]

    for d in range(2):
        load_operands(d, 0)
    for copy in embed_loads:
        copy.start()
    pl.semaphore_wait(barrier, jnp.where(section == 0, 4, 3))
    for d in range(2):
        products(d, 0, functools.partial(load_operands, d, 1))
    for d in range(2):
        part_copy(d, 0).wait_recv()
        for q in range(pieces):
            reduce_main(q, d, 0, begin=True)

    def prefetch_after(d, s):
        @pl.when(s < n)
        def _():
            load_operands(d, s)

    for d in range(2):
        products(d, 1, functools.partial(prefetch_after, d, 2))
    for copy in embed_loads:
        copy.wait()
    embed_back()

    def send_tails(s, carry):
        for d in range(2):
            tail_part_copy(d, s).start()
        return carry

    lax.fori_loop(0, n, send_tails, 0)

    def scatter_step(s, carry):
        for q in range(pieces):
            for d in range(2):
                if q == 0:
                    part_copy(d, s).wait_recv()
                reduce_main(q, d, s)

        for d in range(2):
            @pl.when(s > 1)
            def _():
                part_copy(d, s - 2).wait_send()
                for q in range(pieces):
                    ring_copy(q, d, s - 2).wait_send()

            products(d, s + 1, functools.partial(prefetch_after, d, s + 2))

        for d in range(2):
            @pl.when(s == 1)
            def _():
                reduce_tail(d, 0, begin=True)

            @pl.when(s > 1)
            def _():
                reduce_tail(d, s - 1)
        return carry

    lax.fori_loop(1, n - 1, scatter_step, 0)
    for q in range(pieces):
        for d in range(2):
            if q == 0:
                part_copy(d, n - 1).wait_recv()
            reduce_main(q, d, n - 1, end=True)
    for d in range(2):
        reduce_tail(d, n - 2, begin=n == 2)

    def gather_step(q, d, t):
        gather_landed(q, d, t).wait_recv()

        @pl.when(t < n - 2)
        def _():
            gather_copy(q, d, t + 1).start()

        pair_copy(q, d, t + 1).start()
        if q == pieces:
            @pl.when(section == 0)
            def _():
                cross_copy(d, t + 1, True).start()

    def pass_pair(d, t):
        pair_landed(pieces, d, t).wait_recv()

        @pl.when(section == 0)
        def _():
            cross_copy(d, t, False).start()

    for q, d in mains:
        gather_step(q, d, 0)
    for d in range(2):
        reduce_tail(d, n - 1, end=True)

    def spread(t, carry):
        for q, d in mains:
            gather_step(q, d, t)
        for d in range(2):
            gather_step(pieces, d, t - 1)
            pass_pair(d, t - 1)
        return carry

    lax.fori_loop(1, n - 1, spread, 0)
    for d in range(2):
        gather_step(pieces, d, n - 2)
        pass_pair(d, n - 2)
    for d in range(2):
        pass_pair(d, n - 1)

    @pl.when(section == 0)
    def _():
        feat_keep.wait()
        feat_send.wait_send()

    @pl.when(section == 1)
    def _():
        feat_send.wait_recv()

    for q, d in streams:
        keep_copy(q, d).wait()
    for d in range(2):
        for s in range(max(n - 3, 0), n):
            part_copy(d, s).wait_send()
        for s in range(max(n - 3, 0), n - 1):
            for q in range(pieces):
                ring_copy(q, d, s).wait_send()

    def finish(s, carry):
        for d in range(2):
            tail_part_copy(d, s).wait_send()
            for q in range(pieces + 1):
                pair_copy(q, d, s).wait_send()
                if q < pieces:
                    pair_landed(q, d, s).wait_recv()

            @pl.when(s < n - 1)
            def _():
                ring_copy(pieces, d, s).wait_send()
                for q in range(pieces + 1):
                    gather_copy(q, d, s).wait_send()

            for mine in (True, False):
                @pl.when(section == 0)
                def _():
                    cross_copy(d, s, mine).wait_send()

                @pl.when(section == 1)
                def _():
                    cross_copy(d, s, mine).wait_recv()
        return carry

    lax.fori_loop(0, n, finish, 0)


def finish_kernel(
    blocks, total, tails, cross, out_in, feat_in,
    out, feat, embed, places, attend, project, up, down, embed_vectors, gains, vectors, up_bias, rms,
    coming, going, ends, wide_ends, out_hold, feat_hold, in_sem, out_sem, ends_sem, plain_sem,
    embed_sem,
):
    members, share, width = total.shape
    section = lax.axis_index("section")
    tail = tails.shape[1]
    embed_share = tail - SMALL
    held = [(out_in, out_hold, out), (feat_in, feat_hold, feat)]
    plain_in = [
        pltpu.make_async_copy(src, hold, plain_sem.at[i]) for i, (src, hold, _) in enumerate(held)
    ]
    plain_out = [
        pltpu.make_async_copy(hold, dst, plain_sem.at[2 + i])
        for i, (_, hold, dst) in enumerate(held)
    ]
    slots, unit = coming.shape[:2]
    per_block, per_member = width // unit, share // unit
    count = members * per_member

    def in_copy(u):
        slot = lax.rem(u, slots)
        row = pl.multiple_of(lax.rem(u, per_member) * unit, 16)
        return pltpu.make_async_copy(
            total.at[u // per_member, pl.ds(row, unit)], coming.at[slot], in_sem.at[slot])

    def out_copy(u, dst, row, column):
        slot = lax.rem(u, slots)
        return pltpu.make_async_copy(
            going.at[slot],
            dst.at[pl.ds(pl.multiple_of(row, 16), unit), pl.ds(pl.multiple_of(column, 128), width)],
            out_sem.at[slot])

    own_ends = pltpu.make_async_copy(tails, ends.at[0], ends_sem.at[0])
    far_ends = pltpu.make_async_copy(cross, ends.at[1], ends_sem.at[1])
    for u in range(slots):
        in_copy(u).start()
    own_ends.start()
    far_ends.start()
    for copy in plain_in:
        copy.start()

    def step(u, carry):
        slot = lax.rem(u, slots)
        in_copy(u).wait()

        @pl.when(u >= slots)
        def _():
            out_copy(u, project, 0, 0).wait()

        going[slot] = coming[slot].astype(jnp.float32)
        block, row = u // per_block, lax.rem(u, per_block) * unit

        @pl.when(block < 3)
        def _():
            out_copy(u, attend, row, block * width).start()

        @pl.when(block == 3)
        def _():
            out_copy(u, project, row, 0).start()

        @pl.when((block > 3) & (block < 4 + blocks))
        def _():
            out_copy(u, up, row, (block - 4) * width).start()

        @pl.when(block > 3 + blocks)
        def _():
            out_copy(u, down, (u - (4 + blocks) * per_block) * unit, 0).start()

        @pl.when(u + slots < count)
        def _():
            in_copy(u + slots).start()

        return carry

    lax.fori_loop(0, count, step, 0)
    for copy in plain_in:
        copy.wait()
    for copy in plain_out:
        copy.start()
    own_ends.wait()
    far_ends.wait()
    small = ends[0, 0, embed_share:, :].astype(jnp.float32)
    gains[...] = small[0:2, :]
    for i in range(6):
        vectors[i] = small[2 + i : 3 + i, :]
    for i in range(blocks):
        up_bias[:, i * width : (i + 1) * width] = small[8 + i : 9 + i, :]
    stat = small[15:16, :]
    rms[...] = jnp.sqrt(stat[:, 0:3] / (stat[:, 3:4] * width))
    embed_vectors[...] = ends[section, 0, embed_share:, :].astype(jnp.float32)[12:15, :]

    def widen(w, carry):
        wide_ends[w] = ends[section, w, 0:embed_share, :].astype(jnp.float32)
        return carry

    lax.fori_loop(0, members, widen, 0)
    per_weight = embed.shape[0] // embed_share
    leave = []
    for w in range(members):
        at = w if w < per_weight else w - per_weight
        dst = embed if w < per_weight else places
        leave.append(pltpu.make_async_copy(
            wide_ends.at[w], dst.at[pl.ds(at * embed_share, embed_share)], embed_sem.at[w]))
    for copy in leave:
        copy.start()
    for copy in leave + plain_out:
        copy.wait()
    for u in range(count - slots, count):
        out_copy(u, project, 0, 0).wait()


ANY = pl.BlockSpec(memory_space=pl.ANY)
VMEM = pl.BlockSpec(memory_space=pltpu.VMEM)
SMEM = pl.BlockSpec(memory_space=pltpu.SMEM)
LOW = jnp.bfloat16
WIDE = jnp.float32
PIECES = 2


def shaped(kind, *dims):
    return jax.ShapeDtypeStruct(dims, kind)


def run_forward(features, masked, valid, kinds, embed_weight, embed_vectors, pos_embed, norm_gains,
                vectors, qkv_weight, out_weight, up_weight, up_bias, down_weight):
    clips, length, feat_width = features.shape
    width, feed = up_weight.shape[1:]
    blocks = feed // width
    dma = pltpu.SemaphoreType.DMA
    vm = pltpu.VMEM
    return pl.pallas_call(
        forward_kernel,
        out_shape=(
            shaped(LOW, 3 + blocks, clips * length, width),
            shaped(WIDE, clips, length, width),
            shaped(LOW, clips, length, 3 * width),
            shaped(LOW, clips, H, length, length),
            shaped(WIDE, clips, length, width),
            shaped(WIDE, clips, length, width),
            shaped(WIDE, clips, length, width),
            shaped(LOW, clips, length, feed),
            shaped(LOW, clips, length, width // 2),
            shaped(WIDE, clips, length, 128),
            shaped(WIDE, 8, width),
        ),
        in_specs=[SMEM] + [ANY] * 13,
        out_specs=(ANY,) * 9 + (VMEM,) * 2,
        scratch_shapes=[
            vm(features.shape, LOW), vm(masked.shape, jnp.int32), vm(valid.shape, jnp.int32),
            vm(embed_weight.shape, LOW), vm(embed_vectors.shape, WIDE), vm(pos_embed.shape, WIDE),
            vm(norm_gains.shape[1:], WIDE), vm(vectors.shape, WIDE),
            vm((width, 3 * width), LOW), vm((width, width), LOW), vm((width, feed), LOW),
            vm(up_bias.shape, WIDE), vm((feed, width), LOW),
            vm((feat_width, width), LOW), vm((length, 128), LOW), vm((length, width), WIDE),
            vm((length, width), WIDE),
            vm((length, width), WIDE), vm((length, width), LOW), vm((length, 3 * width), LOW),
            vm((2, 2, length, length), LOW), vm((length, width), LOW), vm((length, width), WIDE),
            vm((length, width), LOW), vm((length, feed), LOW), vm((length, feed), LOW),
            vm((clips, length, width), LOW), vm((clips, length, width), LOW),
            dma((13,)), dma((9 + blocks,)), dma((2,)), dma((clips, 2)), dma((clips, 2)),
            dma((clips, 2)), dma((clips, 2)), dma((clips, 2)),
        ],
        compiler_params=pltpu.CompilerParams(
            collective_id=1, has_side_effects=True, vmem_limit_bytes=56 * 2**20
        ),
    )(kinds, features, masked, valid, embed_weight, embed_vectors, pos_embed, norm_gains, vectors,
      qkv_weight, out_weight, up_weight, up_bias, down_weight)


def run_backward(cotangent, weights, x, qkv, probs, inverse, exact, middle, slope, left, gains):
    clips, length, width = cotangent.shape
    feed = weights[2].shape[2]
    blocks = feed // width
    dma = pltpu.SemaphoreType.DMA
    vm = pltpu.VMEM
    return pl.pallas_call(
        backward_kernel,
        out_shape=(
            shaped(LOW, 5 + blocks, clips * length, width),
            shaped(LOW, clips, length, width),
            shaped(LOW, left.shape[0], width, clips * length),
            shaped(WIDE, 8, width),
            shaped(WIDE, 1, feed),
        ),
        in_specs=[ANY] * 14,
        out_specs=(ANY, ANY, ANY, VMEM, VMEM),
        scratch_shapes=[
            vm((width, 3 * width), LOW), vm((width, width), LOW), vm((width, feed), LOW),
            vm((feed, width), LOW), vm(gains.shape[1:], WIDE),
            vm((clips, length, width), WIDE), vm((clips, length, 3 * width), LOW),
            vm((2, 2, length, length), LOW), vm((clips, length, width), WIDE),
            vm((clips, length, width), WIDE), vm((clips, length, width), WIDE),
            vm((clips, length, feed), LOW), vm((clips, length, width), LOW),
            vm((length, feed), LOW), vm((length, width), WIDE), vm((length, width), WIDE),
            vm((length, width), LOW), vm((length, width), LOW), vm((length, 3 * width), LOW),
            vm((clips, length, width), LOW),
            vm((clips * length, width), LOW), vm((width, clips * length), LOW),
            dma((2,)), dma((5,)), dma((clips, 7)), dma((3,)), dma((5 + blocks,)), dma((clips,)),
            dma((clips, 2)), dma((clips, 2)),
        ],
        compiler_params=pltpu.CompilerParams(
            collective_id=2, has_side_effects=True, vmem_limit_bytes=62 * 2**20
        ),
    )(cotangent, *weights, x, qkv, probs, inverse, exact, middle, slope, left, gains)


def run_sums(members, kinds, turned, right, dx, features, embed_weight, cols, small, up_sums, stats):
    width, rows = turned.shape[1:]
    clips, length, feat_width = features.shape
    n = members // 2
    share = 12 * width // members
    embed_rows = 2 * feat_width + length
    tail = embed_rows // members + SMALL
    unit = unit_rows(members, width)
    per_member = share // unit
    half = width // 2
    dma = pltpu.SemaphoreType.DMA
    vm = pltpu.VMEM
    sems = [dma((2, 2 * per_member + 2)), dma((3,)), dma((2, 2 * n)), dma((2, 2 * n))]
    sems += [dma((2, PIECES + 1, n)) for _ in range(6)]
    sems += [dma((2, PIECES + 1)), dma((2, 2, n)), dma((2, 2, n)), dma((3,))]
    return pl.pallas_call(
        functools.partial(sums_kernel, members),
        out_shape=(
            shaped(LOW, members, share, width),
            shaped(LOW, members, tail, width),
            shaped(LOW, members, tail, width),
            shaped(LOW, clips, length, feat_width // 2),
        ),
        in_specs=[SMEM] + [ANY] * 5 + [VMEM] * 4,
        out_specs=(ANY,) * 4,
        scratch_shapes=[
            vm((2, 2 * per_member, unit, rows), LOW), vm((2, 2, rows, half), LOW),
            vm((2, 3, 2, share, half), LOW),
            vm((2, n, share, half), LOW), vm((2, n - 1, share, half), LOW),
            vm((members, tail, width), LOW), vm((2, n, tail, half), LOW),
            vm((2, n, tail, half), LOW), vm((2, n - 1, tail, half), LOW),
            vm((clips, length, width), LOW), vm(features.shape, LOW), vm(embed_weight.shape, LOW),
            vm(features.shape, LOW), vm((embed_rows, width), LOW), vm((SMALL, width), WIDE),
            sems,
        ],
        compiler_params=pltpu.CompilerParams(
            collective_id=0, has_side_effects=True, vmem_limit_bytes=60 * 2**20
        ),
    )(kinds, turned, right, dx, features, embed_weight, cols, small, up_sums, stats)


def run_finish(total, tails, cross, output, feature_out, feed, feat_width):
    members, share, width = total.shape
    unit = unit_rows(members, width)
    blocks = feed // width
    embed_share = tails.shape[1] - SMALL
    places = members * embed_share - 2 * feat_width
    slots = 12
    dma = pltpu.SemaphoreType.DMA
    vm = pltpu.VMEM
    return pl.pallas_call(
        functools.partial(finish_kernel, blocks),
        out_shape=(
            shaped(LOW, *output.shape), shaped(LOW, *feature_out.shape),
            shaped(WIDE, 2 * feat_width, width), shaped(WIDE, places, width),
            shaped(WIDE, width, 3 * width), shaped(WIDE, width, width),
            shaped(WIDE, width, feed), shaped(WIDE, feed, width),
            shaped(WIDE, 3, width), shaped(WIDE, 2, width), shaped(WIDE, 6, 1, width),
            shaped(WIDE, 1, feed), shaped(WIDE, 1, 3),
        ),
        in_specs=[ANY] * 5,
        out_specs=(ANY,) * 8 + (VMEM,) * 5,
        scratch_shapes=[
            vm((slots, unit, width), LOW), vm((slots, unit, width), WIDE),
            vm((2, *tails.shape), LOW), vm((members, embed_share, width), WIDE),
            vm(output.shape, LOW), vm(feature_out.shape, LOW),
            dma((slots,)), dma((slots,)), dma((2,)), dma((4,)), dma((members,)),
        ],
        compiler_params=pltpu.CompilerParams(vmem_limit_bytes=56 * 2**20),
    )(total, tails, cross, output, feature_out)


def local(
    features,
    masked,
    valid,
    kinds,
    embed_weight,
    embed_vectors,
    pos_embed,
    norm_gains,
    vectors,
    qkv_weight,
    out_weight,
    up_weight,
    up_bias,
    down_weight,
    cotangent,
):
    members = lax.axis_size("wide")
    clips, length, feat_width = features.shape
    width = pos_embed.shape[1]
    feed = up_weight.shape[2]
    left, x, qkv, probs, inverse, exact, middle, slope, output, cols, stats = run_forward(
        features, masked, valid, kinds, embed_weight, embed_vectors, pos_embed, norm_gains,
        vectors.transpose(1, 0, 2), qkv_weight, out_weight, up_weight, up_bias, down_weight)
    weights = (qkv_weight, out_weight, up_weight, down_weight)
    right, dx, turned, small, up_sums = run_backward(
        cotangent, weights, x, qkv, probs, inverse, exact, middle, slope, left, norm_gains)
    total, tails, cross, feature_out = run_sums(
        members, kinds, turned, right, dx, features, embed_weight, cols, small, up_sums, stats)
    (output, feature_out, embed, places, attend, project, up, down, embed_rows, gain_rows,
     vector_rows, up_rows, rms) = run_finish(
        total, tails, cross, output, feature_out, feed, feat_width)
    return (
        output,
        feature_out,
        embed.reshape(2, feat_width, width),
        embed_rows,
        places,
        gain_rows[None],
        vector_rows.transpose(1, 0, 2),
        attend[None],
        project[None],
        up[None],
        up_rows,
        down[None],
        rms,
    )


def solution(mesh):
    return jax.shard_map(
        local,
        mesh=mesh,
        in_specs=(
            P("wide", None, None),
            P("wide", None),
            P("wide", None),
            P("wide"),
            P(),
            P(),
            P(),
            P("section", None, None),
            P("section", None, None),
            P("section", None, None),
            P("section", None, None),
            P("section", None, None),
            P("section", None),
            P("section", None, None),
            P("wide", None, None),
        ),
        out_specs=(
            P("wide", None, "section"),
            P("wide", None, "section"),
            P(),
            P(),
            P(),
            P("section", None, None),
            P("section", None, None),
            P("section", None, None),
            P("section", None, None),
            P("section", None, None),
            P("section", None),
            P("section", None, None),
            P("section", None),
        ),
        check_vma=False,
    )
```

```python
import functools
import math

import jax
import jax.numpy as jnp
from jax import lax
from jax.experimental import pallas as pl
from jax.experimental.pallas import tpu as pltpu
from jax.sharding import PartitionSpec as P

H = 12
HD = 64
EPS = 1e-06
NEG = -1000000000.0


MESH = pl.DeviceIdType.MESH
SMALL = 16


def unit_rows(members, width):
    return math.gcd(12 * width // members, width)


def dot_nn(left, right):
    return jnp.dot(left, right, preferred_element_type=jnp.float32)


def dot_nt(left, right):
    return lax.dot_general(
        left, right, (((1,), (1,)), ((), ())), preferred_element_type=jnp.float32
    )


def tile_of(index, size):
    if isinstance(index, int):
        return pl.ds(index * size, size)
    return pl.ds(pl.multiple_of(index * size, size), size)


def loop(count, body, unroll):
    if count == unroll:
        for i in range(count):
            body(i, 0)
        return

    def step(i, carry):
        for u in range(unroll):
            body(i * unroll + u, 0)
        return carry

    lax.fori_loop(0, count // unroll, step, 0)


def column_sum(values):
    return jnp.sum(values, axis=0, keepdims=True)


def row_mean(values):
    return jnp.mean(values, axis=-1, keepdims=True)


def pick_kind(kind, first, second):
    keep = (kind == 0).astype(jnp.float32)
    return first.astype(jnp.float32) * keep + second.astype(jnp.float32) * (1.0 - keep)


def gelu_pair(hidden):
    decay = jnp.exp(-0.5 * hidden * hidden)
    cdf = 0.5 + 0.5 * lax.erf(hidden * 0.5**0.5)
    return hidden * cdf, cdf + hidden * decay * 0.3989422804014327


def fetches(pairs, sems):
    return [pltpu.make_async_copy(src, dst, sems.at[i]) for i, (src, dst) in enumerate(pairs)]


def greet_partner():
    barrier = pltpu.get_barrier_semaphore()
    pl.semaphore_signal(
        barrier, inc=1, device_id={"section": 1 - lax.axis_index("section")}, device_id_type=MESH
    )
    pl.semaphore_wait(barrier, 1)


def to_partner(src, dst, send, recv):
    return pltpu.make_async_remote_copy(
        src_ref=src, dst_ref=dst, send_sem=send, recv_sem=recv,
        device_id={"section": 1 - lax.axis_index("section")}, device_id_type=MESH)


def forward_kernel(
    kinds, feat_h, masked_h, valid_h, embw_h, embv_h, pos_h, gains_h, vectors_h, wqkv_h, wout_h,
    wup_h, upb_h, wdown_h,
    left_h, x_h, qkv_h, probs_h, inverse_h, exact_h, middle_h, slope_h, out_h, cols, stats,
    feat, masked, valid, embw, embv, pos, gains, vectors, wqkv, wout, wup, up_bias, wdown,
    chosen, dead_keys, inverse, exact,
    x, normed, qkv, probs, context, middle, hidden_in, active, slope, y, landed,
    load_sem, save_sem, probs_sem, send_sem, recv_sem, back_send, back_recv, keep_sem,
):
    low = jnp.bfloat16
    section = lax.axis_index("section")
    clips, length, width = landed.shape
    half = length // 2
    feed = wup.shape[1]
    heads2 = width // 128
    blocks = feed // width
    loads = fetches(
        [(masked_h, masked), (valid_h, valid), (gains_h.at[0], gains),
         (vectors_h, vectors), (upb_h, up_bias),
         (feat_h, feat), (embw_h, embw), (embv_h, embv), (pos_h, pos),
         (wqkv_h.at[0], wqkv), (wout_h.at[0], wout), (wup_h.at[0], wup), (wdown_h.at[0], wdown)],
        load_sem)
    for copy in loads:
        copy.start()
    greet_partner()
    stats[...] = jnp.zeros_like(stats)
    for copy in loads[:9]:
        copy.wait()
    sublane = lax.broadcasted_iota(jnp.int32, (128, length), 0)
    for c in range(clips):
        flags = jnp.where(sublane == 0, masked[c : c + 1, :], 0)
        flags = jnp.where(sublane == 1, valid[c : c + 1, :], flags)
        cols[c] = flags.astype(jnp.float32).T
    low_lanes = lax.broadcasted_iota(jnp.int32, (1, 128), 1) < HD

    def save(index, src, dst):
        return pltpu.make_async_copy(src, dst, save_sem.at[index])

    def saves(c):
        rows = pl.ds(pl.multiple_of(c * length, length), length)
        pairs = [
            (x, x_h.at[c]), (normed, left_h.at[0, rows]), (qkv, qkv_h.at[c]),
            (context, left_h.at[1, rows]), (middle, middle_h.at[c]),
            (hidden_in, left_h.at[2, rows]), (slope, slope_h.at[c]),
        ] + [
            (active.at[:, pl.ds(b * width, width)], left_h.at[3 + b, rows]) for b in range(blocks)
        ] + [(inverse, inverse_h.at[c]), (exact, exact_h.at[c])]
        return [save(i, src, dst) for i, (src, dst) in enumerate(pairs)]

    def probs_save(c, pair):
        slot = lax.rem(pair, 2)
        return pltpu.make_async_copy(
            probs.at[slot], probs_h.at[c, pl.ds(pair * 2, 2)], probs_sem.at[slot])

    def send_half(c, h):
        rows = pl.ds(h * half, half)
        return to_partner(
            y.at[c, rows], landed.at[c, rows], send_sem.at[c, h], recv_sem.at[c, h])

    def back_half(c, h):
        rows = pl.ds(h * half, half)
        return to_partner(
            y.at[c, rows, pl.ds(0, width // 2)], out_h.at[c, rows],
            back_send.at[c, h], back_recv.at[c, h])

    def keep_half(c, h):
        rows = pl.ds(h * half, half)
        return pltpu.make_async_copy(
            y.at[c, rows, pl.ds(width // 2, width // 2)], out_h.at[c, rows], keep_sem.at[c, h])

    def clip(c, carry):
        def after_first(index):
            @pl.when(c > 0)
            def _():
                saves(c - 1)[index].wait()

        after_first(0)
        after_first(1)

        @pl.when(section == 0)
        def _():
            chosen[...] = pick_kind(kinds[c], embw[0], embw[1]).astype(low)
            offset = pick_kind(kinds[c], embv[0:1, :], embv[1:2, :])

            def tile(i, carry):
                rows = tile_of(i, 128)
                lifted = dot_nn(feat[c, rows, :], chosen[...]) + offset
                hidden = cols[c, rows, :][:, 0:1]
                x[rows, :] = jnp.where(hidden > 0.0, embv[2:3, :], lifted) + pos[rows, :]
                return carry

            loop(length // 128, tile, 4)

        @pl.when(section == 1)
        def _():
            for h in range(2):
                send_half(c, h).wait_recv()

            def tile(i, carry):
                rows = tile_of(i, 64)
                x[rows, :] = landed[c, rows, :].astype(jnp.float32)
                return carry

            loop(length // 64, tile, 4)

        own = saves(c)
        own[0].start()

        def norm_rows(source, target, which, shift, first, count):
            gain, offset = gains[which : which + 1, :], vectors[shift]

            def tile(i, carry):
                rows = tile_of(i, 64)
                values = source[rows, :]
                values = values - row_mean(values)
                scale = lax.rsqrt(row_mean(values * values) + EPS)
                target[rows, :] = (values * scale * gain + offset).astype(low)
                return carry

            loop(count, lambda i, carry: tile(first + i, carry), 4)

        norm_rows(x, normed, 0, 0, 0, length // 64)
        own[1].start()
        after_first(2)

        @pl.when(c == 0)
        def _():
            loads[9].wait()

        def qkv_tile(j, carry):
            at = tile_of(j, 256)
            part = dot_nn(normed[...], wqkv[:, at])
            if j < width // 256:
                part = part + vectors[1, :, at]
            elif j >= 2 * width // 256:
                part = part + vectors[2, :, tile_of(j - 2 * width // 256, 256)]
            qkv[:, at] = part.astype(low)
            return carry

        loop(3 * width // 256, qkv_tile, 9)
        own[2].start()
        after_first(3)
        after_first(7 + blocks)
        after_first(8 + blocks)

        lane = lax.broadcasted_iota(jnp.int32, (1, 128), 1)
        scale, one, zero = (jnp.full((1, 128), v, low) for v in (HD**-0.5, 1.0, 0.0))
        dead_keys[...] = jnp.broadcast_to(
            jnp.where(cols[c][:, 1:2] > 0.0, 0.0, NEG), dead_keys.shape).astype(low)

        def attend(pair, carry):
            @pl.when((pair > 1) | (c > 0))
            def _():
                probs_save(c, pair).wait()

            at = tile_of(pair, 128)
            queries = qkv[:, at]
            keys_in = qkv[:, tile_of(pair + heads2, 128)]
            values_in = qkv[:, tile_of(pair + 2 * heads2, 128)]
            raw, softs = [], []
            for h in range(2):
                extra = lane == (64 if h == 0 else 0)
                scaled = jnp.where(
                    low_lanes == (h == 0), queries * scale, jnp.where(extra, one, zero))
                raw.append(dot_nt(scaled, jnp.where(extra, dead_keys[...], keys_in)))
            for h in range(2):
                top = jnp.max(raw[h], axis=-1, keepdims=True)
                soft = jnp.exp(raw[h] - top).astype(low)
                probs[lax.rem(pair, 2), h] = soft
                softs.append(soft)
            outs = [
                dot_nn(softs[h], jnp.where(low_lanes == (h == 0), values_in, one))
                for h in range(2)
            ]
            total = pltpu.roll(jnp.where(low_lanes, outs[1], outs[0]), 64, 1)
            scale_back = 1.0 / total
            inverse[:, at] = scale_back
            mixed = jnp.where(low_lanes, outs[0], outs[1]) * scale_back
            exact[:, at] = mixed
            context[:, at] = mixed.astype(low)
            probs_save(c, pair).start()
            return carry

        lax.fori_loop(0, heads2, attend, 0)
        own[3].start()
        own[7 + blocks].start()
        own[8 + blocks].start()
        after_first(4)

        @pl.when(c == 0)
        def _():
            loads[10].wait()

        live = cols[c][:, 1:2]

        def out_tile(j, carry):
            at = tile_of(j, 256)
            branch = dot_nn(context[...], wout[:, at]) + vectors[3, :, at]
            middle[:, at] = x[:, at] + branch
            stats[1:2, at] += column_sum(branch * branch * live)
            return carry

        loop(width // 256, out_tile, 3)
        own[4].start()
        for index in range(5, 7 + blocks):
            after_first(index)

        @pl.when(c == 0)
        def _():
            loads[11].wait()
            loads[12].wait()

        for h in range(2):
            rows = pl.ds(h * half, half)
            norm_rows(middle, hidden_in, 1, 4, h * (half // 64), half // 64)
            if h == 1:
                own[5].start()

            def up_tile(j, carry):
                at = tile_of(j, 256)
                hidden = dot_nn(hidden_in[rows, :], wup[:, at]) + up_bias[:, at]
                value, steep = gelu_pair(hidden)
                active[rows, at] = value.astype(low)
                slope[rows, at] = steep.astype(low)
                return carry

            loop(feed // 256, up_tile, 12)
            if h == 1:
                for copy in own[6 : 7 + blocks]:
                    copy.start()

            def down_tile(j, carry):
                at = tile_of(j, 256)
                mixer = dot_nn(active[rows, :], wdown[:, at]) + vectors[5, :, at]
                total = middle[rows, at] + mixer
                flags = cols[c, rows, :][:, 1:2]
                stats[0:1, at] += column_sum(total * total * flags)
                stats[2:3, at] += column_sum(mixer * mixer * flags)
                y[c, rows, at] = total.astype(low)
                return carry

            loop(width // 256, down_tile, 3)

            @pl.when(section == 0)
            def _():
                send_half(c, h).start()

            @pl.when(section == 1)
            def _():
                back_half(c, h).start()
                keep_half(c, h).start()
        return carry

    lax.fori_loop(0, clips, clip, 0)
    for pair in (heads2 - 2, heads2 - 1):
        probs_save(clips - 1, pair).wait()
    for copy in saves(clips - 1):
        copy.wait()
    for c in range(clips):
        for h in range(2):
            @pl.when(section == 0)
            def _():
                send_half(c, h).wait_send()
                back_half(c, h).wait_recv()

            @pl.when(section == 1)
            def _():
                back_half(c, h).wait_send()
                keep_half(c, h).wait()


def backward_kernel(
    cot_h, wqkv_h, wout_h, wup_h, wdown_h, x_h, qkv_h, probs_h, inverse_h, exact_h, middle_h, slope_h, left_h, gains_h,
    right_h, dx_h, turned_h, small, up_sums,
    wqkv, wout, wup, wdown, gains, x, qkv, probs, inverse, context, middle, slope, g,
    d_hidden, wide_grad, d_middle, d_branch, d_context, d_qkv, d_low, upright, turned,
    turn_sem, load_sem, state_sem, probs_sem, save_sem, dx_sem, send_sem, recv_sem,
):
    low = jnp.bfloat16
    f32 = jnp.float32
    section = lax.axis_index("section")
    clips, length, width = g.shape
    half = length // 2
    feed = wup.shape[1]
    heads2 = width // 128
    blocks = feed // width
    greet_partner()

    def cot_load(c):
        return pltpu.make_async_copy(cot_h.at[c], g.at[c], state_sem.at[c, 0])

    def state_loads(c):
        pairs = [(slope_h, slope), (middle_h, middle), (qkv_h, qkv), (x_h, x), (inverse_h, inverse),
                 (exact_h, context)]
        return [
            pltpu.make_async_copy(src.at[c], dst.at[c], state_sem.at[c, 1 + i])
            for i, (src, dst) in enumerate(pairs)
        ]

    loads = fetches(
        [(gains_h.at[0], gains), (wdown_h.at[0], wdown), (wup_h.at[0], wup), (wout_h.at[0], wout),
         (wqkv_h.at[0], wqkv)], load_sem)

    def start_cot(c):
        @pl.when(section == 1)
        def _():
            cot_load(c).start()

    first = state_loads(0)
    start_cot(0)
    for copy in (loads[1], first[0], loads[0], loads[2], first[1], loads[3], first[2], first[4],
                 first[5], loads[4], first[3]):
        copy.start()

    small[...] = jnp.zeros_like(small)
    up_sums[...] = jnp.zeros_like(up_sums)
    low_lanes = lax.broadcasted_iota(jnp.int32, (1, 128), 1) < HD
    slots = probs.shape[0]
    pairs_total = clips * heads2

    def probs_load(step):
        slot = lax.rem(step, slots)
        return pltpu.make_async_copy(
            probs_h.at[step // heads2, pl.ds(lax.rem(step, heads2) * 2, 2)],
            probs.at[slot], probs_sem.at[slot])

    for step in range(slots):
        probs_load(step).start()

    def saves(c):
        rows = pl.ds(pl.multiple_of(c * length, length), length)
        pairs = [(d_qkv.at[:, pl.ds(b * width, width)], right_h.at[b, rows]) for b in range(3)]
        pairs += [(d_branch, right_h.at[3, rows])]
        pairs += [
            (d_hidden.at[:, pl.ds(b * width, width)], right_h.at[4 + b, rows])
            for b in range(blocks)
        ]
        pairs += [(g.at[c], right_h.at[4 + blocks, rows])]
        return [pltpu.make_async_copy(s, d, save_sem.at[i]) for i, (s, d) in enumerate(pairs)]

    def send_half(c, h):
        rows = pl.ds(h * half, half)
        return to_partner(
            d_low.at[c, rows], g.at[c, rows], send_sem.at[c, h], recv_sem.at[c, h])

    def dx_save(c):
        return pltpu.make_async_copy(d_low.at[c], dx_h.at[c], dx_sem.at[c])

    def norm_back(source, carried, which, shift_row, rows, take):
        gain = gains[which : which + 1, :]
        values = source[rows, :]
        values = values - row_mean(values)
        scale = lax.rsqrt(row_mean(values * values) + EPS)
        values = values * scale
        grad = wide_grad[rows, :]
        small[which : which + 1, :] += column_sum(grad * values)
        small[shift_row : shift_row + 1, :] += column_sum(grad)
        grad = grad * gain
        return carried + scale * (grad - row_mean(grad) - values * row_mean(grad * values))

    def turn_lefts():
        def block(b, carry):
            come = pltpu.make_async_copy(left_h.at[b], upright, turn_sem.at[0])
            come.start()
            come.wait()

            def piece(i, carry):
                at = tile_of(i, 128)
                turned[at, :] = upright[:, at].T
                return carry

            loop(width // 128, piece, 2)
            leave = pltpu.make_async_copy(turned, turned_h.at[b], turn_sem.at[1])
            leave.start()
            leave.wait()
            return carry

        lax.fori_loop(0, left_h.shape[0], block, 0)

    @pl.when(section == 0)
    def _():
        turn_lefts()

    def clip(c, carry):
        def after_first(lo, hi):
            @pl.when(c > 0)
            def _():
                for copy in saves(c - 1)[lo:hi]:
                    copy.wait()

        after_first(4, 5 + blocks)

        @pl.when(section == 1)
        def _():
            cot_load(c).wait()

        state = state_loads(c)
        own = saves(c)

        @pl.when(c == 0)
        def _():
            for copy in loads[:3]:
                copy.wait()

        state[0].wait()
        state[1].wait()
        for h in range(2):
            rows = pl.ds(h * half, half)

            @pl.when(section == 0)
            def _():
                send_half(c, h).wait_recv()

            if h == 1:
                own[-1].start()

            def feed_tile(j, carry):
                at = tile_of(j, 256)
                d_active = dot_nt(g[c, rows, :], wdown[at, :])
                grad = (slope[c, rows, at].astype(f32) * d_active).astype(low)
                d_hidden[rows, at] = grad
                up_sums[:, at] += column_sum(grad.astype(f32))
                return carry

            loop(feed // 256, feed_tile, 12)

            def in_tile(j, carry):
                at = tile_of(j, 256)
                wide_grad[rows, at] = dot_nt(d_hidden[rows, :], wup[at, :])
                return carry

            loop(width // 256, in_tile, 3)

        after_first(3, 4)
        for copy in own[4:-1]:
            copy.start()

        @pl.when(c + 1 < clips)
        def _():
            start_cot(c + 1)
            for copy in state_loads(c + 1):
                copy.start()

        def middle_tile(i, carry):
            rows = tile_of(i, 64)
            grad_in = g[c, rows, :].astype(f32)
            total = norm_back(middle.at[c], grad_in, 1, 6, rows, None)
            d_middle[rows, :] = total
            rounded = total.astype(low)
            d_branch[rows, :] = rounded
            small[5:6, :] += column_sum(rounded.astype(f32))
            small[7:8, :] += column_sum(grad_in)
            return carry

        loop(length // 64, middle_tile, 4)
        own[3].start()

        @pl.when(c == 0)
        def _():
            loads[3].wait()

        def context_tile(j, carry):
            at = tile_of(j, 256)
            d_context[:, at] = dot_nt(d_branch[...], wout[at, :]).astype(low)
            return carry

        loop(width // 256, context_tile, 3)
        state[2].wait()
        state[4].wait()
        state[5].wait()
        after_first(0, 3)

        def attend(pair, carry):
            step = c * heads2 + pair
            slot = lax.rem(step, slots)
            probs_load(step).wait()
            at, key_at = tile_of(pair, 128), tile_of(pair + heads2, 128)
            value_at = tile_of(pair + 2 * heads2, 128)
            queries, keys_in, values_in = qkv[c, :, at], qkv[c, :, key_at], qkv[c, :, value_at]
            grad_wide = d_context[:, at].astype(f32) * inverse[c, :, at]
            grad = grad_wide.astype(low)
            along = grad.astype(f32) * context[c, :, at]
            queries_t, grad_t = queries.T, grad.T
            d_queries, keys_t, values_t = [], [], []
            for h in range(2):
                mine = low_lanes == (h == 0)
                soft = probs[slot, h]
                delta = jnp.sum(jnp.where(mine, along, 0.0), axis=-1, keepdims=True)
                d_soft = dot_nt(jnp.where(mine, grad, jnp.zeros_like(grad)), values_in)
                d_scores = (soft.astype(f32) * (d_soft - delta)).astype(low)
                part = slice(h * HD, (h + 1) * HD)
                values_t.append(dot_nn(grad_t[part], soft))
                keys_t.append(dot_nn(queries_t[part], d_scores))
                d_queries.append(dot_nn(d_scores, keys_in))
            scale = HD**-0.5
            query_grad = (jnp.where(low_lanes, d_queries[0], d_queries[1]) * scale).astype(low)
            value_grad = jnp.concatenate(values_t, axis=0).T.astype(low)
            d_qkv[:, at] = query_grad
            d_qkv[:, key_at] = (jnp.concatenate(keys_t, axis=0) * scale).T.astype(low)
            d_qkv[:, value_at] = value_grad
            small[3:4, at] += column_sum(query_grad.astype(f32))
            small[4:5, at] += column_sum(value_grad.astype(f32))

            @pl.when(step + slots < pairs_total)
            def _():
                probs_load(step + slots).start()

            return carry

        lax.fori_loop(0, heads2, attend, 0)
        for copy in own[:3]:
            copy.start()

        @pl.when(c == 0)
        def _():
            loads[4].wait()

        state[3].wait()
        for h in range(2):
            rows = pl.ds(h * half, half)

            def in_tile(j, carry):
                at = tile_of(j, 256)
                wide_grad[rows, at] = dot_nt(d_qkv[rows, :], wqkv[at, :])
                return carry

            loop(width // 256, in_tile, 3)

            def last_tile(i, carry):
                part = tile_of(i, 64)
                total = norm_back(x.at[c], d_middle[part, :], 0, 2, part, None)
                d_low[c, part, :] = total.astype(low)
                return carry

            loop(half // 64, lambda i, carry: last_tile(h * (half // 64) + i, carry), 4)

            @pl.when(section == 1)
            def _():
                send_half(c, h).start()

        dx_save(c).start()
        return carry

    lax.fori_loop(0, clips, clip, 0)

    @pl.when(section == 1)
    def _():
        turn_lefts()

    for copy in saves(clips - 1):
        copy.wait()
    for c in range(clips):
        dx_save(c).wait()
        for h in range(2):
            @pl.when(section == 1)
            def _():
                send_half(c, h).wait_send()


def sums_kernel(
    members, kinds, turned_h, right_h, dx_h, feat_h, embw_h, cols, small_in, up_sums, stats,
    o_ref, t_ref, e_ref, h_ref,
    lefts, rights, chunk, part, ring, tails, tail_own, tail_part, tail_ring,
    dx, feat, embw, feat_grad, embed, small, sems,
):
    (load_sem, embed_sem, part_send, part_recv, ring_send, ring_recv, gather_send, gather_recv,
     pair_send, pair_recv, keep_sem, cross_send, cross_recv, feat_sem) = sems
    low = jnp.bfloat16
    f32 = jnp.float32
    n = members // 2
    share, columns = chunk.shape[3:]
    width = 2 * columns
    tail = tails.shape[1]
    unit = unit_rows(members, width)
    per_block, per_member = width // unit, share // unit
    slots = chunk.shape[1]
    clips, length, feat_width = feat.shape
    me = lax.axis_index("wide")
    section = lax.axis_index("section")
    chip, core = me // 2, me % 2
    place = jnp.where(chip % 2 == 0, chip // 2, n - 1 - chip // 2)

    def member_at(position):
        position = lax.rem(position + 2 * n, n)
        return jnp.where(2 * position < n, 2 * position, 2 * (n - 1 - position) + 1) * 2 + core

    right, left = member_at(place + 1), member_at(place - 1)
    other = chip * 2 + 1 - core
    target = (right, left)

    barrier = pltpu.get_barrier_semaphore()
    for peer in (right, left, other):
        pl.semaphore_signal(barrier, inc=1, device_id={"wide": peer}, device_id_type=MESH)
    @pl.when(section == 1)
    def _():
        pl.semaphore_signal(barrier, inc=1, device_id={"section": 0}, device_id_type=MESH)

    pieces = ring_send.shape[1] - 1
    piece = -(-share // (16 * pieces)) * 16
    spans = [(q * piece, min(piece, share - q * piece)) for q in range(pieces)]
    mains = [(q, d) for q in range(pieces) for d in range(2)]
    streams = mains + [(pieces, 0), (pieces, 1)]

    def turn(position):
        return lax.rem(position + 2 * n, n)

    def reduce_at(d, step):
        return turn(place - step) if d == 0 else turn(place + step)

    def gather_at(d, index):
        return turn(place + 1 - index) if d == 0 else turn(place - 1 + index)

    def span(q):
        return pl.ds(*spans[q])

    def cols_of(d):
        return pl.ds(d * columns, columns)

    def remote(src, dst, send, recv, device):
        return pltpu.make_async_remote_copy(
            src_ref=src, dst_ref=dst, send_sem=send, recv_sem=recv,
            device_id=device, device_id_type=MESH)

    def block_of(spot):
        return spot // per_block

    def operand_copies(d, s):
        base = reduce_at(d, s) * 2 * per_member
        first, second = block_of(base), block_of(base + 2 * per_member - 1)
        copies = []
        for u in range(2 * per_member):
            block = block_of(base + u)
            source = jnp.where(
                block < 3, 0, jnp.where(block == 3, 1, jnp.where(block < 8, 2, block - 5)))
            row = pl.multiple_of(lax.rem(base + u, per_block) * unit, 16)
            copies.append(pltpu.make_async_copy(
                turned_h.at[source, pl.ds(row, unit)], lefts.at[d, u], load_sem.at[d, u]))
        for i, block in enumerate((first, second)):
            copies.append(pltpu.make_async_copy(
                right_h.at[jnp.minimum(block, 8), :, cols_of(d)], rights.at[d, i],
                load_sem.at[d, 2 * per_member + i]))
        return copies

    def load_operands(d, s):
        for copy in operand_copies(d, s):
            copy.start()

    def part_copy(d, s):
        return remote(
            chunk.at[d, lax.rem(s, slots), 1 - core], part.at[d, s], part_send.at[d, s], part_recv.at[d, s],
            {"wide": other})

    def ring_copy(q, d, s):
        if q == pieces:
            src, dst = tail_own.at[d, s], tail_ring.at[d, s]
        else:
            src, dst = chunk.at[d, lax.rem(s, slots), core, span(q)], ring.at[d, s, span(q)]
        return remote(src, dst, ring_send.at[d, q, s], ring_recv.at[d, q, s],
                      {"wide": target[d]})

    def products(d, s, prefetch):
        for copy in operand_copies(d, s):
            copy.wait()
        base = reduce_at(d, s) * 2 * per_member
        first = block_of(base)

        for u in range(0, 2 * per_member, 2):
            rows = lefts[d, u : u + 2].reshape(2 * unit, lefts.shape[3])
            tile = dot_nn(rows, rights[d, block_of(base + u) - first]).astype(low)
            for i in range(2):
                which, row = (u + i) // per_member, (u + i) % per_member * unit
                chunk[d, lax.rem(s, slots), which, pl.ds(row, unit), :] = (
                    tile[i * unit : (i + 1) * unit])
        part_copy(d, s).start()
        prefetch()

    def final_of(q, d):
        return tail_own.at[d, n - 1] if q == pieces else chunk.at[d, (n - 1) % slots, core, span(q)]

    def spot_of(q, d, index, which):
        member = gather_at(d, index) * 2 + which
        if q == pieces:
            return t_ref.at[member, :, cols_of(d)]
        return o_ref.at[member, span(q), cols_of(d)]

    def gather_copy(q, d, index, first=False):
        src = final_of(q, d) if first else spot_of(q, d, index, core)
        return remote(
            src, spot_of(q, d, index, core),
            gather_send.at[d, q, index], gather_recv.at[d, q, index], {"wide": target[d]})

    def gather_landed(q, d, index):
        return remote(
            final_of(q, d), spot_of(q, d, index + 1, core),
            gather_send.at[d, q, index], gather_recv.at[d, q, index], {"wide": target[d]})

    def pair_copy(q, d, index, first=False):
        src = final_of(q, d) if first else spot_of(q, d, index, core)
        return remote(
            src, spot_of(q, d, index, core),
            pair_send.at[d, q, index], pair_recv.at[d, q, index], {"wide": other})

    def pair_landed(q, d, index):
        return remote(
            final_of(q, d), spot_of(q, d, index, 1 - core),
            pair_send.at[d, q, index], pair_recv.at[d, q, index], {"wide": other})

    def keep_copy(q, d):
        return pltpu.make_async_copy(final_of(q, d), spot_of(q, d, 0, core), keep_sem.at[d, q])

    def cross_copy(d, index, mine, first=False):
        member = gather_at(d, index) * 2 + (core if mine else 1 - core)
        src = final_of(pieces, d) if first else t_ref.at[member, :, cols_of(d)]
        lane = 0 if mine else 1
        return remote(
            src, e_ref.at[member, :, cols_of(d)],
            cross_send.at[d, lane, index], cross_recv.at[d, lane, index],
            {"section": 1 - section})

    def hand_over(q, d):
        gather_copy(q, d, 0, True).start()
        pair_copy(q, d, 0, True).start()
        keep_copy(q, d).start()
        if q == pieces:
            @pl.when(section == 0)
            def _():
                cross_copy(d, 0, True, True).start()

    def reduce_main(q, d, s, begin=False, end=False):
        if not begin:
            ring_copy(q, d, s - 1).wait_recv()

        def add(tile, carry):
            at = pl.ds(pl.multiple_of(spans[q][0] + tile * 16, 16), 16)
            slot = lax.rem(s, slots)
            total = chunk[d, slot, core, at].astype(f32) + part[d, s, at].astype(f32)
            if not begin:
                total = total + ring[d, s - 1, at].astype(f32)
            chunk[d, slot, core, at] = total.astype(low)
            return carry

        loop(spans[q][1] // 16, add, 1)
        if end:
            hand_over(q, d)
        else:
            ring_copy(q, d, s).start()

    def tail_part_copy(d, s):
        return remote(
            tails.at[reduce_at(d, s) * 2 + 1 - core, :, cols_of(d)], tail_part.at[d, s],
            part_send.at[d, n + s], part_recv.at[d, n + s], {"wide": other})

    def reduce_tail(d, s, begin=False, end=False):
        tail_part_copy(d, s).wait_recv()
        total = tails[reduce_at(d, s) * 2 + core, :, cols_of(d)].astype(f32)
        total = total + tail_part[d, s].astype(f32)
        if not begin:
            ring_copy(pieces, d, s - 1).wait_recv()
            total = total + tail_ring[d, s - 1].astype(f32)
        tail_own[d, s] = total.astype(low)
        if end:
            hand_over(pieces, d)
        else:
            ring_copy(pieces, d, s).start()

    feat_half = h_ref.shape[2]
    feat_keep = pltpu.make_async_copy(
        feat_grad.at[:, :, pl.ds(0, feat_half)], h_ref, feat_sem.at[0])
    feat_send = remote(
        feat_grad.at[:, :, pl.ds(feat_half, feat_half)], h_ref, feat_sem.at[1], feat_sem.at[2],
        {"section": 1 - section})

    def embed_back():
        first = (1 - section).astype(f32)
        small[...] = jnp.zeros_like(small)
        small[0:8, :] = small_in[...]
        for i in range(up_sums.shape[1] // width):
            small[8 + i : 9 + i, :] = up_sums[:, i * width : (i + 1) * width]
        lane = lax.broadcasted_iota(jnp.int32, (1, width), 1)
        row = jnp.zeros((1, width), f32)
        for i in range(3):
            row = jnp.where(lane == i, jnp.sum(stats[i : i + 1, :], axis=1, keepdims=True), row)
        count = jnp.zeros((1, 1), f32)
        for c in range(clips):
            count = count + jnp.sum(cols[c][:, 1:2], axis=0, keepdims=True)
        small[15:16, :] = jnp.where(lane == 3, count, row)
        embed[...] = jnp.zeros_like(embed)

        @pl.when(section == 0)
        def _():
            weight_sum = [jnp.zeros((feat_width, width), f32)] * 2
            place_sum = jnp.zeros((length, width), f32)
            for c in range(clips):
                grad = dx[c]
                kept = jnp.where(cols[c][:, 0:1] > 0.0, jnp.zeros_like(grad), grad)
                chosen = pick_kind(kinds[c], embw[0], embw[1]).astype(low)
                feat_grad[c] = dot_nt(kept, chosen).astype(low)
                second = kinds[c].astype(f32)
                flags = (1.0 - second, second)
                wide = dot_nn(feat[c].T, kept)
                sums = column_sum(kept.astype(f32))
                for kind in range(2):
                    weight_sum[kind] = weight_sum[kind] + flags[kind] * wide
                    small[12 + kind : 13 + kind, :] += flags[kind] * sums
                small[14:15, :] += column_sum(grad.astype(f32)) - sums
                place_sum = place_sum + grad.astype(f32)
            embed[0:feat_width, :] = weight_sum[0].astype(low)
            embed[feat_width : 2 * feat_width, :] = weight_sum[1].astype(low)
            embed[2 * feat_width :, :] = place_sum.astype(low)
            feat_keep.start()
            feat_send.start()

        embed_share = tail - SMALL
        for w in range(members):
            tails[w, 0:embed_share, :] = embed[w * embed_share : (w + 1) * embed_share, :]
            if w == 0:
                tails[w, embed_share:, :] = small[...].astype(low)
            else:
                tails[w, embed_share:, :] = jnp.zeros((SMALL, width), low)

    embed_loads = [
        pltpu.make_async_copy(src, dst, embed_sem.at[i])
        for i, (src, dst) in enumerate(((dx_h, dx), (feat_h, feat), (embw_h, embw)))
    ]

    for d in range(2):
        load_operands(d, 0)
    pl.semaphore_wait(barrier, jnp.where(section == 0, 4, 3))
    for d in range(2):
        products(d, 0, functools.partial(load_operands, d, 1))
    for copy in embed_loads:
        copy.start()
    for d in range(2):
        part_copy(d, 0).wait_recv()
        for q in range(pieces):
            reduce_main(q, d, 0, begin=True)

    def prefetch_after(d, s):
        @pl.when(s < n)
        def _():
            load_operands(d, s)

    for d in range(2):
        products(d, 1, functools.partial(prefetch_after, d, 2))
    for copy in embed_loads:
        copy.wait()
    embed_back()

    def send_tails(s, carry):
        for d in range(2):
            tail_part_copy(d, s).start()
        return carry

    lax.fori_loop(0, n, send_tails, 0)

    def scatter_step(s, carry):
        for q in range(pieces):
            for d in range(2):
                if q == 0:
                    part_copy(d, s).wait_recv()
                reduce_main(q, d, s)

        for d in range(2):
            @pl.when(s > 1)
            def _():
                part_copy(d, s - 2).wait_send()
                for q in range(pieces):
                    ring_copy(q, d, s - 2).wait_send()

            products(d, s + 1, functools.partial(prefetch_after, d, s + 2))

        for d in range(2):
            @pl.when(s == 1)
            def _():
                reduce_tail(d, 0, begin=True)

            @pl.when(s > 1)
            def _():
                reduce_tail(d, s - 1)
        return carry

    lax.fori_loop(1, n - 1, scatter_step, 0)
    for q in range(pieces):
        for d in range(2):
            if q == 0:
                part_copy(d, n - 1).wait_recv()
            reduce_main(q, d, n - 1, end=True)
    for d in range(2):
        reduce_tail(d, n - 2, begin=n == 2)

    def gather_step(q, d, t):
        gather_landed(q, d, t).wait_recv()

        @pl.when(t < n - 2)
        def _():
            gather_copy(q, d, t + 1).start()

        pair_copy(q, d, t + 1).start()
        if q == pieces:
            @pl.when(section == 0)
            def _():
                cross_copy(d, t + 1, True).start()

    def pass_pair(d, t):
        pair_landed(pieces, d, t).wait_recv()

        @pl.when(section == 0)
        def _():
            cross_copy(d, t, False).start()

    for q, d in mains:
        gather_step(q, d, 0)
    for d in range(2):
        reduce_tail(d, n - 1, end=True)

    def spread(t, carry):
        for q, d in mains:
            gather_step(q, d, t)
        for d in range(2):
            gather_step(pieces, d, t - 1)
            pass_pair(d, t - 1)
        return carry

    lax.fori_loop(1, n - 1, spread, 0)
    for d in range(2):
        gather_step(pieces, d, n - 2)
        pass_pair(d, n - 2)
    for d in range(2):
        pass_pair(d, n - 1)

    @pl.when(section == 0)
    def _():
        feat_keep.wait()
        feat_send.wait_send()

    @pl.when(section == 1)
    def _():
        feat_send.wait_recv()

    for q, d in streams:
        keep_copy(q, d).wait()
    for d in range(2):
        for s in range(max(n - 3, 0), n):
            part_copy(d, s).wait_send()
        for s in range(max(n - 3, 0), n - 1):
            for q in range(pieces):
                ring_copy(q, d, s).wait_send()

    def finish(s, carry):
        for d in range(2):
            tail_part_copy(d, s).wait_send()
            for q in range(pieces + 1):
                pair_copy(q, d, s).wait_send()
                if q < pieces:
                    pair_landed(q, d, s).wait_recv()

            @pl.when(s < n - 1)
            def _():
                ring_copy(pieces, d, s).wait_send()
                for q in range(pieces + 1):
                    gather_copy(q, d, s).wait_send()

            for mine in (True, False):
                @pl.when(section == 0)
                def _():
                    cross_copy(d, s, mine).wait_send()

                @pl.when(section == 1)
                def _():
                    cross_copy(d, s, mine).wait_recv()
        return carry

    lax.fori_loop(0, n, finish, 0)


def finish_kernel(
    blocks, total, tails, cross, out_in, feat_in,
    out, feat, embed, places, attend, project, up, down, embed_vectors, gains, vectors, up_bias, rms,
    coming, going, ends, wide_ends, out_hold, feat_hold, in_sem, out_sem, ends_sem, plain_sem,
    embed_sem,
):
    members, share, width = total.shape
    section = lax.axis_index("section")
    tail = tails.shape[1]
    embed_share = tail - SMALL
    held = [(out_in, out_hold, out), (feat_in, feat_hold, feat)]
    plain_in = [
        pltpu.make_async_copy(src, hold, plain_sem.at[i]) for i, (src, hold, _) in enumerate(held)
    ]
    plain_out = [
        pltpu.make_async_copy(hold, dst, plain_sem.at[2 + i])
        for i, (_, hold, dst) in enumerate(held)
    ]
    slots, unit = coming.shape[:2]
    per_block, per_member = width // unit, share // unit
    count = members * per_member

    def in_copy(u):
        slot = lax.rem(u, slots)
        row = pl.multiple_of(lax.rem(u, per_member) * unit, 16)
        return pltpu.make_async_copy(
            total.at[u // per_member, pl.ds(row, unit)], coming.at[slot], in_sem.at[slot])

    def out_copy(u, dst, row, column):
        slot = lax.rem(u, slots)
        return pltpu.make_async_copy(
            going.at[slot],
            dst.at[pl.ds(pl.multiple_of(row, 16), unit), pl.ds(pl.multiple_of(column, 128), width)],
            out_sem.at[slot])

    own_ends = pltpu.make_async_copy(tails, ends.at[0], ends_sem.at[0])
    far_ends = pltpu.make_async_copy(cross, ends.at[1], ends_sem.at[1])
    for u in range(slots):
        in_copy(u).start()
    own_ends.start()
    far_ends.start()
    for copy in plain_in:
        copy.start()

    def step(u, carry):
        slot = lax.rem(u, slots)
        in_copy(u).wait()

        @pl.when(u >= slots)
        def _():
            out_copy(u, project, 0, 0).wait()

        going[slot] = coming[slot].astype(jnp.float32)
        block, row = u // per_block, lax.rem(u, per_block) * unit

        @pl.when(block < 3)
        def _():
            out_copy(u, attend, row, block * width).start()

        @pl.when(block == 3)
        def _():
            out_copy(u, project, row, 0).start()

        @pl.when((block > 3) & (block < 4 + blocks))
        def _():
            out_copy(u, up, row, (block - 4) * width).start()

        @pl.when(block > 3 + blocks)
        def _():
            out_copy(u, down, (u - (4 + blocks) * per_block) * unit, 0).start()

        @pl.when(u + slots < count)
        def _():
            in_copy(u + slots).start()

        return carry

    lax.fori_loop(0, count, step, 0)
    for copy in plain_in:
        copy.wait()
    for copy in plain_out:
        copy.start()
    own_ends.wait()
    far_ends.wait()
    small = ends[0, 0, embed_share:, :].astype(jnp.float32)
    gains[...] = small[0:2, :]
    for i in range(6):
        vectors[i] = small[2 + i : 3 + i, :]
    for i in range(blocks):
        up_bias[:, i * width : (i + 1) * width] = small[8 + i : 9 + i, :]
    stat = small[15:16, :]
    rms[...] = jnp.sqrt(stat[:, 0:3] / (stat[:, 3:4] * width))
    embed_vectors[...] = ends[section, 0, embed_share:, :].astype(jnp.float32)[12:15, :]

    def widen(w, carry):
        wide_ends[w] = ends[section, w, 0:embed_share, :].astype(jnp.float32)
        return carry

    lax.fori_loop(0, members, widen, 0)
    per_weight = embed.shape[0] // embed_share
    leave = []
    for w in range(members):
        at = w if w < per_weight else w - per_weight
        dst = embed if w < per_weight else places
        leave.append(pltpu.make_async_copy(
            wide_ends.at[w], dst.at[pl.ds(at * embed_share, embed_share)], embed_sem.at[w]))
    for copy in leave:
        copy.start()
    for copy in leave + plain_out:
        copy.wait()
    for u in range(count - slots, count):
        out_copy(u, project, 0, 0).wait()


ANY = pl.BlockSpec(memory_space=pl.ANY)
VMEM = pl.BlockSpec(memory_space=pltpu.VMEM)
SMEM = pl.BlockSpec(memory_space=pltpu.SMEM)
LOW = jnp.bfloat16
WIDE = jnp.float32
PIECES = 2


def shaped(kind, *dims):
    return jax.ShapeDtypeStruct(dims, kind)


def run_forward(features, masked, valid, kinds, embed_weight, embed_vectors, pos_embed, norm_gains,
                vectors, qkv_weight, out_weight, up_weight, up_bias, down_weight):
    clips, length, feat_width = features.shape
    width, feed = up_weight.shape[1:]
    blocks = feed // width
    dma = pltpu.SemaphoreType.DMA
    vm = pltpu.VMEM
    return pl.pallas_call(
        forward_kernel,
        out_shape=(
            shaped(LOW, 3 + blocks, clips * length, width),
            shaped(WIDE, clips, length, width),
            shaped(LOW, clips, length, 3 * width),
            shaped(LOW, clips, H, length, length),
            shaped(WIDE, clips, length, width),
            shaped(WIDE, clips, length, width),
            shaped(WIDE, clips, length, width),
            shaped(LOW, clips, length, feed),
            shaped(LOW, clips, length, width // 2),
            shaped(WIDE, clips, length, 128),
            shaped(WIDE, 8, width),
        ),
        in_specs=[SMEM] + [ANY] * 13,
        out_specs=(ANY,) * 9 + (VMEM,) * 2,
        scratch_shapes=[
            vm(features.shape, LOW), vm(masked.shape, jnp.int32), vm(valid.shape, jnp.int32),
            vm(embed_weight.shape, LOW), vm(embed_vectors.shape, WIDE), vm(pos_embed.shape, WIDE),
            vm(norm_gains.shape[1:], WIDE), vm(vectors.shape, WIDE),
            vm((width, 3 * width), LOW), vm((width, width), LOW), vm((width, feed), LOW),
            vm(up_bias.shape, WIDE), vm((feed, width), LOW),
            vm((feat_width, width), LOW), vm((length, 128), LOW), vm((length, width), WIDE),
            vm((length, width), WIDE),
            vm((length, width), WIDE), vm((length, width), LOW), vm((length, 3 * width), LOW),
            vm((2, 2, length, length), LOW), vm((length, width), LOW), vm((length, width), WIDE),
            vm((length, width), LOW), vm((length, feed), LOW), vm((length, feed), LOW),
            vm((clips, length, width), LOW), vm((clips, length, width), LOW),
            dma((13,)), dma((9 + blocks,)), dma((2,)), dma((clips, 2)), dma((clips, 2)),
            dma((clips, 2)), dma((clips, 2)), dma((clips, 2)),
        ],
        compiler_params=pltpu.CompilerParams(
            collective_id=1, has_side_effects=True, vmem_limit_bytes=56 * 2**20
        ),
    )(kinds, features, masked, valid, embed_weight, embed_vectors, pos_embed, norm_gains, vectors,
      qkv_weight, out_weight, up_weight, up_bias, down_weight)


def run_backward(cotangent, weights, x, qkv, probs, inverse, exact, middle, slope, left, gains):
    clips, length, width = cotangent.shape
    feed = weights[2].shape[2]
    blocks = feed // width
    dma = pltpu.SemaphoreType.DMA
    vm = pltpu.VMEM
    return pl.pallas_call(
        backward_kernel,
        out_shape=(
            shaped(LOW, 5 + blocks, clips * length, width),
            shaped(LOW, clips, length, width),
            shaped(LOW, left.shape[0], width, clips * length),
            shaped(WIDE, 8, width),
            shaped(WIDE, 1, feed),
        ),
        in_specs=[ANY] * 14,
        out_specs=(ANY, ANY, ANY, VMEM, VMEM),
        scratch_shapes=[
            vm((width, 3 * width), LOW), vm((width, width), LOW), vm((width, feed), LOW),
            vm((feed, width), LOW), vm(gains.shape[1:], WIDE),
            vm((clips, length, width), WIDE), vm((clips, length, 3 * width), LOW),
            vm((2, 2, length, length), LOW), vm((clips, length, width), WIDE),
            vm((clips, length, width), WIDE), vm((clips, length, width), WIDE),
            vm((clips, length, feed), LOW), vm((clips, length, width), LOW),
            vm((length, feed), LOW), vm((length, width), WIDE), vm((length, width), WIDE),
            vm((length, width), LOW), vm((length, width), LOW), vm((length, 3 * width), LOW),
            vm((clips, length, width), LOW),
            vm((clips * length, width), LOW), vm((width, clips * length), LOW),
            dma((2,)), dma((5,)), dma((clips, 7)), dma((3,)), dma((5 + blocks,)), dma((clips,)),
            dma((clips, 2)), dma((clips, 2)),
        ],
        compiler_params=pltpu.CompilerParams(
            collective_id=2, has_side_effects=True, vmem_limit_bytes=62 * 2**20
        ),
    )(cotangent, *weights, x, qkv, probs, inverse, exact, middle, slope, left, gains)


def run_sums(members, kinds, turned, right, dx, features, embed_weight, cols, small, up_sums, stats):
    width, rows = turned.shape[1:]
    clips, length, feat_width = features.shape
    n = members // 2
    share = 12 * width // members
    embed_rows = 2 * feat_width + length
    tail = embed_rows // members + SMALL
    unit = unit_rows(members, width)
    per_member = share // unit
    half = width // 2
    dma = pltpu.SemaphoreType.DMA
    vm = pltpu.VMEM
    sems = [dma((2, 2 * per_member + 2)), dma((3,)), dma((2, 2 * n)), dma((2, 2 * n))]
    sems += [dma((2, PIECES + 1, n)) for _ in range(6)]
    sems += [dma((2, PIECES + 1)), dma((2, 2, n)), dma((2, 2, n)), dma((3,))]
    return pl.pallas_call(
        functools.partial(sums_kernel, members),
        out_shape=(
            shaped(LOW, members, share, width),
            shaped(LOW, members, tail, width),
            shaped(LOW, members, tail, width),
            shaped(LOW, clips, length, feat_width // 2),
        ),
        in_specs=[SMEM] + [ANY] * 5 + [VMEM] * 4,
        out_specs=(ANY,) * 4,
        scratch_shapes=[
            vm((2, 2 * per_member, unit, rows), LOW), vm((2, 2, rows, half), LOW),
            vm((2, 3, 2, share, half), LOW),
            vm((2, n, share, half), LOW), vm((2, n - 1, share, half), LOW),
            vm((members, tail, width), LOW), vm((2, n, tail, half), LOW),
            vm((2, n, tail, half), LOW), vm((2, n - 1, tail, half), LOW),
            vm((clips, length, width), LOW), vm(features.shape, LOW), vm(embed_weight.shape, LOW),
            vm(features.shape, LOW), vm((embed_rows, width), LOW), vm((SMALL, width), WIDE),
            sems,
        ],
        compiler_params=pltpu.CompilerParams(
            collective_id=0, has_side_effects=True, vmem_limit_bytes=60 * 2**20
        ),
    )(kinds, turned, right, dx, features, embed_weight, cols, small, up_sums, stats)


def run_finish(total, tails, cross, output, feature_out, feed, feat_width):
    members, share, width = total.shape
    unit = unit_rows(members, width)
    blocks = feed // width
    embed_share = tails.shape[1] - SMALL
    places = members * embed_share - 2 * feat_width
    slots = 12
    dma = pltpu.SemaphoreType.DMA
    vm = pltpu.VMEM
    return pl.pallas_call(
        functools.partial(finish_kernel, blocks),
        out_shape=(
            shaped(LOW, *output.shape), shaped(LOW, *feature_out.shape),
            shaped(WIDE, 2 * feat_width, width), shaped(WIDE, places, width),
            shaped(WIDE, width, 3 * width), shaped(WIDE, width, width),
            shaped(WIDE, width, feed), shaped(WIDE, feed, width),
            shaped(WIDE, 3, width), shaped(WIDE, 2, width), shaped(WIDE, 6, 1, width),
            shaped(WIDE, 1, feed), shaped(WIDE, 1, 3),
        ),
        in_specs=[ANY] * 5,
        out_specs=(ANY,) * 8 + (VMEM,) * 5,
        scratch_shapes=[
            vm((slots, unit, width), LOW), vm((slots, unit, width), WIDE),
            vm((2, *tails.shape), LOW), vm((members, embed_share, width), WIDE),
            vm(output.shape, LOW), vm(feature_out.shape, LOW),
            dma((slots,)), dma((slots,)), dma((2,)), dma((4,)), dma((members,)),
        ],
        compiler_params=pltpu.CompilerParams(vmem_limit_bytes=56 * 2**20),
    )(total, tails, cross, output, feature_out)


def local(
    features,
    masked,
    valid,
    kinds,
    embed_weight,
    embed_vectors,
    pos_embed,
    norm_gains,
    vectors,
    qkv_weight,
    out_weight,
    up_weight,
    up_bias,
    down_weight,
    cotangent,
):
    members = lax.axis_size("wide")
    clips, length, feat_width = features.shape
    width = pos_embed.shape[1]
    feed = up_weight.shape[2]
    left, x, qkv, probs, inverse, exact, middle, slope, output, cols, stats = run_forward(
        features, masked, valid, kinds, embed_weight, embed_vectors, pos_embed, norm_gains,
        vectors.transpose(1, 0, 2), qkv_weight, out_weight, up_weight, up_bias, down_weight)
    weights = (qkv_weight, out_weight, up_weight, down_weight)
    right, dx, turned, small, up_sums = run_backward(
        cotangent, weights, x, qkv, probs, inverse, exact, middle, slope, left, norm_gains)
    total, tails, cross, feature_out = run_sums(
        members, kinds, turned, right, dx, features, embed_weight, cols, small, up_sums, stats)
    (output, feature_out, embed, places, attend, project, up, down, embed_rows, gain_rows,
     vector_rows, up_rows, rms) = run_finish(
        total, tails, cross, output, feature_out, feed, feat_width)
    return (
        output,
        feature_out,
        embed.reshape(2, feat_width, width),
        embed_rows,
        places,
        gain_rows[None],
        vector_rows.transpose(1, 0, 2),
        attend[None],
        project[None],
        up[None],
        up_rows,
        down[None],
        rms,
    )


def solution(mesh):
    return jax.shard_map(
        local,
        mesh=mesh,
        in_specs=(
            P("wide", None, None),
            P("wide", None),
            P("wide", None),
            P("wide"),
            P(),
            P(),
            P(),
            P("section", None, None),
            P("section", None, None),
            P("section", None, None),
            P("section", None, None),
            P("section", None, None),
            P("section", None),
            P("section", None, None),
            P("wide", None, None),
        ),
        out_specs=(
            P("wide", None, "section"),
            P("wide", None, "section"),
            P(),
            P(),
            P(),
            P("section", None, None),
            P("section", None, None),
            P("section", None, None),
            P("section", None, None),
            P("section", None, None),
            P("section", None),
            P("section", None, None),
            P("section", None),
        ),
        check_vma=False,
    )
```

```python
import functools
import math

import jax
import jax.numpy as jnp
from jax import lax
from jax.experimental import pallas as pl
from jax.experimental.pallas import tpu as pltpu
from jax.sharding import PartitionSpec as P

H = 12
HD = 64
EPS = 1e-06
NEG = -1000000000.0


MESH = pl.DeviceIdType.MESH
SMALL = 16


def unit_rows(members, width):
    return math.gcd(12 * width // members, width)


def dot_nn(left, right):
    return jnp.dot(left, right, preferred_element_type=jnp.float32)


def dot_nt(left, right):
    return lax.dot_general(
        left, right, (((1,), (1,)), ((), ())), preferred_element_type=jnp.float32
    )


def tile_of(index, size):
    if isinstance(index, int):
        return pl.ds(index * size, size)
    return pl.ds(pl.multiple_of(index * size, size), size)


def loop(count, body, unroll):
    if count == unroll:
        for i in range(count):
            body(i, 0)
        return

    def step(i, carry):
        for u in range(unroll):
            body(i * unroll + u, 0)
        return carry

    lax.fori_loop(0, count // unroll, step, 0)


def column_sum(values):
    return jnp.sum(values, axis=0, keepdims=True)


def row_mean(values):
    return jnp.mean(values, axis=-1, keepdims=True)


def pick_kind(kind, first, second):
    keep = (kind == 0).astype(jnp.float32)
    return first.astype(jnp.float32) * keep + second.astype(jnp.float32) * (1.0 - keep)


def gelu_pair(hidden):
    decay = jnp.exp(-0.5 * hidden * hidden)
    cdf = 0.5 + 0.5 * lax.erf(hidden * 0.5**0.5)
    return hidden * cdf, cdf + hidden * decay * 0.3989422804014327


def fetches(pairs, sems):
    return [pltpu.make_async_copy(src, dst, sems.at[i]) for i, (src, dst) in enumerate(pairs)]


def greet_partner():
    barrier = pltpu.get_barrier_semaphore()
    pl.semaphore_signal(
        barrier, inc=1, device_id={"section": 1 - lax.axis_index("section")}, device_id_type=MESH
    )
    pl.semaphore_wait(barrier, 1)


def to_partner(src, dst, send, recv):
    return pltpu.make_async_remote_copy(
        src_ref=src, dst_ref=dst, send_sem=send, recv_sem=recv,
        device_id={"section": 1 - lax.axis_index("section")}, device_id_type=MESH)


def forward_kernel(
    kinds, feat_h, masked_h, valid_h, embw_h, embv_h, pos_h, gains_h, vectors_h, wqkv_h, wout_h,
    wup_h, upb_h, wdown_h,
    left_h, x_h, qkv_h, probs_h, inverse_h, exact_h, middle_h, slope_h, out_h, cols, stats,
    feat, masked, valid, embw, embv, pos, gains, vectors, wqkv, wout, wup, up_bias, wdown,
    chosen, dead_keys, inverse, exact,
    x, normed, qkv, probs, context, middle, hidden_in, active, slope, y, landed,
    load_sem, save_sem, probs_sem, send_sem, recv_sem, back_send, back_recv, keep_sem,
):
    low = jnp.bfloat16
    section = lax.axis_index("section")
    clips, length, width = landed.shape
    half = length // 2
    feed = wup.shape[1]
    heads2 = width // 128
    blocks = feed // width
    loads = fetches(
        [(masked_h, masked), (valid_h, valid), (gains_h.at[0], gains),
         (vectors_h, vectors), (upb_h, up_bias),
         (feat_h, feat), (embw_h, embw), (embv_h, embv), (pos_h, pos),
         (wqkv_h.at[0], wqkv), (wout_h.at[0], wout), (wup_h.at[0], wup), (wdown_h.at[0], wdown)],
        load_sem)
    for copy in loads:
        copy.start()
    greet_partner()
    stats[...] = jnp.zeros_like(stats)
    for copy in loads[:9]:
        copy.wait()
    sublane = lax.broadcasted_iota(jnp.int32, (128, length), 0)
    for c in range(clips):
        flags = jnp.where(sublane == 0, masked[c : c + 1, :], 0)
        flags = jnp.where(sublane == 1, valid[c : c + 1, :], flags)
        cols[c] = flags.astype(jnp.float32).T
    low_lanes = lax.broadcasted_iota(jnp.int32, (1, 128), 1) < HD

    def save(index, src, dst):
        return pltpu.make_async_copy(src, dst, save_sem.at[index])

    def saves(c):
        rows = pl.ds(pl.multiple_of(c * length, length), length)
        pairs = [
            (x, x_h.at[c]), (normed, left_h.at[0, rows]), (qkv, qkv_h.at[c]),
            (context, left_h.at[1, rows]), (middle, middle_h.at[c]),
            (hidden_in, left_h.at[2, rows]), (slope, slope_h.at[c]),
        ] + [
            (active.at[:, pl.ds(b * width, width)], left_h.at[3 + b, rows]) for b in range(blocks)
        ] + [(inverse, inverse_h.at[c]), (exact, exact_h.at[c])]
        return [save(i, src, dst) for i, (src, dst) in enumerate(pairs)]

    def probs_save(c, pair):
        slot = lax.rem(pair, 2)
        return pltpu.make_async_copy(
            probs.at[slot], probs_h.at[c, pl.ds(pair * 2, 2)], probs_sem.at[slot])

    def send_half(c, h):
        rows = pl.ds(h * half, half)
        return to_partner(
            y.at[c, rows], landed.at[c, rows], send_sem.at[c, h], recv_sem.at[c, h])

    def back_half(c, h):
        rows = pl.ds(h * half, half)
        return to_partner(
            y.at[c, rows, pl.ds(0, width // 2)], out_h.at[c, rows],
            back_send.at[c, h], back_recv.at[c, h])

    def keep_half(c, h):
        rows = pl.ds(h * half, half)
        return pltpu.make_async_copy(
            y.at[c, rows, pl.ds(width // 2, width // 2)], out_h.at[c, rows], keep_sem.at[c, h])

    def clip(c, carry):
        def after_first(index):
            @pl.when(c > 0)
            def _():
                saves(c - 1)[index].wait()

        after_first(0)
        after_first(1)

        def norm_rows(source, target, which, shift, first, count):
            gain, offset = gains[which : which + 1, :], vectors[shift]

            def tile(i, carry):
                rows = tile_of(i, 64)
                values = source[rows, :]
                values = values - row_mean(values)
                scale = lax.rsqrt(row_mean(values * values) + EPS)
                target[rows, :] = (values * scale * gain + offset).astype(low)
                return carry

            loop(count, lambda i, carry: tile(first + i, carry), 4)

        @pl.when(section == 0)
        def _():
            chosen[...] = pick_kind(kinds[c], embw[0], embw[1]).astype(low)
            offset = pick_kind(kinds[c], embv[0:1, :], embv[1:2, :])

            def tile(i, carry):
                rows = tile_of(i, 128)
                lifted = dot_nn(feat[c, rows, :], chosen[...]) + offset
                hidden = cols[c, rows, :][:, 0:1]
                x[rows, :] = jnp.where(hidden > 0.0, embv[2:3, :], lifted) + pos[rows, :]
                return carry

            loop(length // 128, tile, 4)
            norm_rows(x, normed, 0, 0, 0, length // 64)

        @pl.when(section == 1)
        def _():
            def tile(i, carry):
                rows = tile_of(i, 64)
                x[rows, :] = landed[c, rows, :].astype(jnp.float32)
                return carry

            for h in range(2):
                send_half(c, h).wait_recv()
                first = h * (half // 64)
                loop(half // 64, lambda i, carry, first=first: tile(first + i, carry), 4)
                norm_rows(x, normed, 0, 0, first, half // 64)

        own = saves(c)
        own[0].start()

        own[1].start()
        after_first(2)

        @pl.when(c == 0)
        def _():
            loads[9].wait()

        def qkv_tile(j, carry):
            at = tile_of(j, 256)
            part = dot_nn(normed[...], wqkv[:, at])
            if j < width // 256:
                part = part + vectors[1, :, at]
            elif j >= 2 * width // 256:
                part = part + vectors[2, :, tile_of(j - 2 * width // 256, 256)]
            qkv[:, at] = part.astype(low)
            return carry

        loop(3 * width // 256, qkv_tile, 9)
        own[2].start()
        after_first(3)
        after_first(7 + blocks)
        after_first(8 + blocks)

        lane = lax.broadcasted_iota(jnp.int32, (1, 128), 1)
        scale, one, zero = (jnp.full((1, 128), v, low) for v in (HD**-0.5, 1.0, 0.0))
        dead_keys[...] = jnp.broadcast_to(
            jnp.where(cols[c][:, 1:2] > 0.0, 0.0, NEG), dead_keys.shape).astype(low)

        def attend(pair, carry):
            @pl.when((pair > 1) | (c > 0))
            def _():
                probs_save(c, pair).wait()

            at = tile_of(pair, 128)
            queries = qkv[:, at]
            keys_in = qkv[:, tile_of(pair + heads2, 128)]
            values_in = qkv[:, tile_of(pair + 2 * heads2, 128)]
            raw, softs = [], []
            for h in range(2):
                extra = lane == (64 if h == 0 else 0)
                scaled = jnp.where(
                    low_lanes == (h == 0), queries * scale, jnp.where(extra, one, zero))
                raw.append(dot_nt(scaled, jnp.where(extra, dead_keys[...], keys_in)))
            for h in range(2):
                top = jnp.max(raw[h], axis=-1, keepdims=True)
                soft = jnp.exp(raw[h] - top).astype(low)
                probs[lax.rem(pair, 2), h] = soft
                softs.append(soft)
            outs = [
                dot_nn(softs[h], jnp.where(low_lanes == (h == 0), values_in, one))
                for h in range(2)
            ]
            total = pltpu.roll(jnp.where(low_lanes, outs[1], outs[0]), 64, 1)
            scale_back = 1.0 / total
            inverse[:, at] = scale_back
            mixed = jnp.where(low_lanes, outs[0], outs[1]) * scale_back
            exact[:, at] = mixed
            context[:, at] = mixed.astype(low)
            probs_save(c, pair).start()
            return carry

        lax.fori_loop(0, heads2, attend, 0)
        own[3].start()
        own[7 + blocks].start()
        own[8 + blocks].start()
        after_first(4)

        @pl.when(c == 0)
        def _():
            loads[10].wait()

        live = cols[c][:, 1:2]

        def out_tile(j, carry):
            at = tile_of(j, 256)
            branch = dot_nn(context[...], wout[:, at]) + vectors[3, :, at]
            middle[:, at] = x[:, at] + branch
            stats[1:2, at] += column_sum(branch * branch * live)
            return carry

        loop(width // 256, out_tile, 3)
        own[4].start()
        for index in range(5, 7 + blocks):
            after_first(index)

        @pl.when(c == 0)
        def _():
            loads[11].wait()
            loads[12].wait()

        for h in range(2):
            rows = pl.ds(h * half, half)
            norm_rows(middle, hidden_in, 1, 4, h * (half // 64), half // 64)
            if h == 1:
                own[5].start()

            def up_tile(j, carry):
                at = tile_of(j, 256)
                hidden = dot_nn(hidden_in[rows, :], wup[:, at]) + up_bias[:, at]
                value, steep = gelu_pair(hidden)
                active[rows, at] = value.astype(low)
                slope[rows, at] = steep.astype(low)
                return carry

            loop(feed // 256, up_tile, 12)
            if h == 1:
                for copy in own[6 : 7 + blocks]:
                    copy.start()

            def down_tile(j, carry):
                at = tile_of(j, 256)
                mixer = dot_nn(active[rows, :], wdown[:, at]) + vectors[5, :, at]
                total = middle[rows, at] + mixer
                flags = cols[c, rows, :][:, 1:2]
                stats[0:1, at] += column_sum(total * total * flags)
                stats[2:3, at] += column_sum(mixer * mixer * flags)
                y[c, rows, at] = total.astype(low)
                return carry

            loop(width // 256, down_tile, 3)

            @pl.when(section == 0)
            def _():
                send_half(c, h).start()

            @pl.when(section == 1)
            def _():
                back_half(c, h).start()
                keep_half(c, h).start()
        return carry

    lax.fori_loop(0, clips, clip, 0)
    for pair in (heads2 - 2, heads2 - 1):
        probs_save(clips - 1, pair).wait()
    for copy in saves(clips - 1):
        copy.wait()
    for c in range(clips):
        for h in range(2):
            @pl.when(section == 0)
            def _():
                send_half(c, h).wait_send()
                back_half(c, h).wait_recv()

            @pl.when(section == 1)
            def _():
                back_half(c, h).wait_send()
                keep_half(c, h).wait()


def backward_kernel(
    cot_h, wqkv_h, wout_h, wup_h, wdown_h, x_h, qkv_h, probs_h, inverse_h, exact_h, middle_h, slope_h, left_h, gains_h,
    right_h, dx_h, turned_h, small, up_sums,
    wqkv, wout, wup, wdown, gains, x, qkv, probs, inverse, context, middle, slope, g,
    d_hidden, wide_grad, d_middle, d_branch, d_context, d_qkv, d_low, upright, turned,
    turn_sem, load_sem, state_sem, probs_sem, save_sem, dx_sem, send_sem, recv_sem,
):
    low = jnp.bfloat16
    f32 = jnp.float32
    section = lax.axis_index("section")
    clips, length, width = g.shape
    half = length // 2
    feed = wup.shape[1]
    heads2 = width // 128
    blocks = feed // width
    greet_partner()

    def cot_load(c):
        return pltpu.make_async_copy(cot_h.at[c], g.at[c], state_sem.at[c, 0])

    def state_loads(c):
        pairs = [(slope_h, slope), (middle_h, middle), (qkv_h, qkv), (x_h, x), (inverse_h, inverse),
                 (exact_h, context)]
        return [
            pltpu.make_async_copy(src.at[c], dst.at[c], state_sem.at[c, 1 + i])
            for i, (src, dst) in enumerate(pairs)
        ]

    loads = fetches(
        [(gains_h.at[0], gains), (wdown_h.at[0], wdown), (wup_h.at[0], wup), (wout_h.at[0], wout),
         (wqkv_h.at[0], wqkv)], load_sem)

    def start_cot(c):
        @pl.when(section == 1)
        def _():
            cot_load(c).start()

    first = state_loads(0)
    start_cot(0)
    for copy in (loads[1], first[0], loads[0], loads[2], first[1], loads[3], first[2], first[4],
                 first[5], loads[4], first[3]):
        copy.start()

    small[...] = jnp.zeros_like(small)
    up_sums[...] = jnp.zeros_like(up_sums)
    low_lanes = lax.broadcasted_iota(jnp.int32, (1, 128), 1) < HD
    slots = probs.shape[0]
    pairs_total = clips * heads2

    def probs_load(step):
        slot = lax.rem(step, slots)
        return pltpu.make_async_copy(
            probs_h.at[step // heads2, pl.ds(lax.rem(step, heads2) * 2, 2)],
            probs.at[slot], probs_sem.at[slot])

    for step in range(slots):
        probs_load(step).start()

    def saves(c):
        rows = pl.ds(pl.multiple_of(c * length, length), length)
        pairs = [(d_qkv.at[:, pl.ds(b * width, width)], right_h.at[b, rows]) for b in range(3)]
        pairs += [(d_branch, right_h.at[3, rows])]
        pairs += [
            (d_hidden.at[:, pl.ds(b * width, width)], right_h.at[4 + b, rows])
            for b in range(blocks)
        ]
        pairs += [(g.at[c], right_h.at[4 + blocks, rows])]
        return [pltpu.make_async_copy(s, d, save_sem.at[i]) for i, (s, d) in enumerate(pairs)]

    def send_half(c, h):
        rows = pl.ds(h * half, half)
        return to_partner(
            d_low.at[c, rows], g.at[c, rows], send_sem.at[c, h], recv_sem.at[c, h])

    def dx_save(c):
        return pltpu.make_async_copy(d_low.at[c], dx_h.at[c], dx_sem.at[c])

    def norm_back(source, carried, which, shift_row, rows, take):
        gain = gains[which : which + 1, :]
        values = source[rows, :]
        values = values - row_mean(values)
        scale = lax.rsqrt(row_mean(values * values) + EPS)
        values = values * scale
        grad = wide_grad[rows, :]
        small[which : which + 1, :] += column_sum(grad * values)
        small[shift_row : shift_row + 1, :] += column_sum(grad)
        grad = grad * gain
        return carried + scale * (grad - row_mean(grad) - values * row_mean(grad * values))

    def turn_lefts():
        def block(b, carry):
            come = pltpu.make_async_copy(left_h.at[b], upright, turn_sem.at[0])
            come.start()
            come.wait()

            def piece(i, carry):
                at = tile_of(i, 128)
                turned[at, :] = upright[:, at].T
                return carry

            loop(width // 128, piece, 2)
            leave = pltpu.make_async_copy(turned, turned_h.at[b], turn_sem.at[1])
            leave.start()
            leave.wait()
            return carry

        lax.fori_loop(0, left_h.shape[0], block, 0)

    @pl.when(section == 0)
    def _():
        turn_lefts()

    def clip(c, carry):
        def after_first(lo, hi):
            @pl.when(c > 0)
            def _():
                for copy in saves(c - 1)[lo:hi]:
                    copy.wait()

        after_first(4, 5 + blocks)

        @pl.when(section == 1)
        def _():
            cot_load(c).wait()

        state = state_loads(c)
        own = saves(c)

        @pl.when(c == 0)
        def _():
            for copy in loads[:3]:
                copy.wait()

        state[0].wait()
        state[1].wait()
        for h in range(2):
            rows = pl.ds(h * half, half)

            @pl.when(section == 0)
            def _():
                send_half(c, h).wait_recv()

            if h == 1:
                own[-1].start()

            def feed_tile(j, carry):
                at = tile_of(j, 256)
                d_active = dot_nt(g[c, rows, :], wdown[at, :])
                grad = (slope[c, rows, at].astype(f32) * d_active).astype(low)
                d_hidden[rows, at] = grad
                up_sums[:, at] += column_sum(grad.astype(f32))
                return carry

            loop(feed // 256, feed_tile, 12)

            def in_tile(j, carry):
                at = tile_of(j, 256)
                wide_grad[rows, at] = dot_nt(d_hidden[rows, :], wup[at, :])
                return carry

            loop(width // 256, in_tile, 3)

        after_first(3, 4)
        for copy in own[4:-1]:
            copy.start()

        @pl.when(c + 1 < clips)
        def _():
            start_cot(c + 1)
            for copy in state_loads(c + 1):
                copy.start()

        def middle_tile(i, carry):
            rows = tile_of(i, 64)
            grad_in = g[c, rows, :].astype(f32)
            total = norm_back(middle.at[c], grad_in, 1, 6, rows, None)
            d_middle[rows, :] = total
            rounded = total.astype(low)
            d_branch[rows, :] = rounded
            small[5:6, :] += column_sum(rounded.astype(f32))
            small[7:8, :] += column_sum(grad_in)
            return carry

        loop(length // 64, middle_tile, 8)
        own[3].start()

        @pl.when(c == 0)
        def _():
            loads[3].wait()

        def context_tile(j, carry):
            at = tile_of(j, 256)
            d_context[:, at] = dot_nt(d_branch[...], wout[at, :]).astype(low)
            return carry

        loop(width // 256, context_tile, 3)
        state[2].wait()
        state[4].wait()
        state[5].wait()
        after_first(0, 3)

        def attend(pair, carry):
            step = c * heads2 + pair
            slot = lax.rem(step, slots)
            probs_load(step).wait()
            at, key_at = tile_of(pair, 128), tile_of(pair + heads2, 128)
            value_at = tile_of(pair + 2 * heads2, 128)
            queries, keys_in, values_in = qkv[c, :, at], qkv[c, :, key_at], qkv[c, :, value_at]
            grad_wide = d_context[:, at].astype(f32) * inverse[c, :, at]
            grad = grad_wide.astype(low)
            along = grad.astype(f32) * context[c, :, at]
            queries_t, grad_t = queries.T, grad.T
            d_queries, keys_t, values_t = [], [], []
            for h in range(2):
                mine = low_lanes == (h == 0)
                soft = probs[slot, h]
                delta = jnp.sum(jnp.where(mine, along, 0.0), axis=-1, keepdims=True)
                d_soft = dot_nt(jnp.where(mine, grad, jnp.zeros_like(grad)), values_in)
                d_scores = (soft.astype(f32) * (d_soft - delta)).astype(low)
                part = slice(h * HD, (h + 1) * HD)
                values_t.append(dot_nn(grad_t[part], soft))
                keys_t.append(dot_nn(queries_t[part], d_scores))
                d_queries.append(dot_nn(d_scores, keys_in))
            scale = HD**-0.5
            query_grad = (jnp.where(low_lanes, d_queries[0], d_queries[1]) * scale).astype(low)
            value_grad = jnp.concatenate(values_t, axis=0).T.astype(low)
            d_qkv[:, at] = query_grad
            d_qkv[:, key_at] = (jnp.concatenate(keys_t, axis=0) * scale).T.astype(low)
            d_qkv[:, value_at] = value_grad
            small[3:4, at] += column_sum(query_grad.astype(f32))
            small[4:5, at] += column_sum(value_grad.astype(f32))

            @pl.when(step + slots < pairs_total)
            def _():
                probs_load(step + slots).start()

            return carry

        lax.fori_loop(0, heads2, attend, 0)
        for copy in own[:3]:
            copy.start()

        @pl.when(c == 0)
        def _():
            loads[4].wait()

        state[3].wait()
        for h in range(2):
            rows = pl.ds(h * half, half)

            def in_tile(j, carry):
                at = tile_of(j, 256)
                wide_grad[rows, at] = dot_nt(d_qkv[rows, :], wqkv[at, :])
                return carry

            loop(width // 256, in_tile, 3)

            def last_tile(i, carry):
                part = tile_of(i, 64)
                total = norm_back(x.at[c], d_middle[part, :], 0, 2, part, None)
                d_low[c, part, :] = total.astype(low)
                return carry

            loop(half // 64, lambda i, carry: last_tile(h * (half // 64) + i, carry), 4)

            @pl.when(section == 1)
            def _():
                send_half(c, h).start()

        dx_save(c).start()
        return carry

    lax.fori_loop(0, clips, clip, 0)

    @pl.when(section == 1)
    def _():
        turn_lefts()

    for copy in saves(clips - 1):
        copy.wait()
    for c in range(clips):
        dx_save(c).wait()
        for h in range(2):
            @pl.when(section == 1)
            def _():
                send_half(c, h).wait_send()


def sums_kernel(
    members, kinds, turned_h, right_h, dx_h, feat_h, embw_h, cols, small_in, up_sums, stats,
    o_ref, t_ref, e_ref, h_ref,
    lefts, rights, chunk, part, ring, tails, tail_own, tail_part, tail_ring,
    dx, feat, embw, feat_grad, embed, small, sems,
):
    (load_sem, embed_sem, part_send, part_recv, ring_send, ring_recv, gather_send, gather_recv,
     pair_send, pair_recv, keep_sem, cross_send, cross_recv, feat_sem) = sems
    low = jnp.bfloat16
    f32 = jnp.float32
    n = members // 2
    share, columns = chunk.shape[3:]
    width = 2 * columns
    tail = tails.shape[1]
    unit = unit_rows(members, width)
    per_block, per_member = width // unit, share // unit
    slots = chunk.shape[1]
    clips, length, feat_width = feat.shape
    me = lax.axis_index("wide")
    section = lax.axis_index("section")
    chip, core = me // 2, me % 2
    place = jnp.where(chip % 2 == 0, chip // 2, n - 1 - chip // 2)

    def member_at(position):
        position = lax.rem(position + 2 * n, n)
        return jnp.where(2 * position < n, 2 * position, 2 * (n - 1 - position) + 1) * 2 + core

    right, left = member_at(place + 1), member_at(place - 1)
    other = chip * 2 + 1 - core
    target = (right, left)

    barrier = pltpu.get_barrier_semaphore()
    for peer in (right, left, other):
        pl.semaphore_signal(barrier, inc=1, device_id={"wide": peer}, device_id_type=MESH)
    @pl.when(section == 1)
    def _():
        pl.semaphore_signal(barrier, inc=1, device_id={"section": 0}, device_id_type=MESH)

    pieces = ring_send.shape[1] - 1
    piece = -(-share // (16 * pieces)) * 16
    spans = [(q * piece, min(piece, share - q * piece)) for q in range(pieces)]
    mains = [(q, d) for q in range(pieces) for d in range(2)]
    streams = mains + [(pieces, 0), (pieces, 1)]

    def turn(position):
        return lax.rem(position + 2 * n, n)

    def reduce_at(d, step):
        return turn(place - step) if d == 0 else turn(place + step)

    def gather_at(d, index):
        return turn(place + 1 - index) if d == 0 else turn(place - 1 + index)

    def span(q):
        return pl.ds(*spans[q])

    def cols_of(d):
        return pl.ds(d * columns, columns)

    def remote(src, dst, send, recv, device):
        return pltpu.make_async_remote_copy(
            src_ref=src, dst_ref=dst, send_sem=send, recv_sem=recv,
            device_id=device, device_id_type=MESH)

    def block_of(spot):
        return spot // per_block

    def operand_copies(d, s):
        base = reduce_at(d, s) * 2 * per_member
        first, second = block_of(base), block_of(base + 2 * per_member - 1)
        copies = []
        for u in range(2 * per_member):
            block = block_of(base + u)
            source = jnp.where(
                block < 3, 0, jnp.where(block == 3, 1, jnp.where(block < 8, 2, block - 5)))
            row = pl.multiple_of(lax.rem(base + u, per_block) * unit, 16)
            copies.append(pltpu.make_async_copy(
                turned_h.at[source, pl.ds(row, unit)], lefts.at[d, u], load_sem.at[d, u]))
        for i, block in enumerate((first, second)):
            copies.append(pltpu.make_async_copy(
                right_h.at[jnp.minimum(block, 8), :, cols_of(d)], rights.at[d, i],
                load_sem.at[d, 2 * per_member + i]))
        return copies

    def load_operands(d, s):
        for copy in operand_copies(d, s):
            copy.start()

    def part_copy(d, s):
        return remote(
            chunk.at[d, lax.rem(s, slots), 1 - core], part.at[d, s], part_send.at[d, s], part_recv.at[d, s],
            {"wide": other})

    def ring_copy(q, d, s):
        if q == pieces:
            src, dst = tail_own.at[d, s], tail_ring.at[d, s]
        else:
            src, dst = chunk.at[d, lax.rem(s, slots), core, span(q)], ring.at[d, s, span(q)]
        return remote(src, dst, ring_send.at[d, q, s], ring_recv.at[d, q, s],
                      {"wide": target[d]})

    def products(d, s, prefetch):
        for copy in operand_copies(d, s):
            copy.wait()
        base = reduce_at(d, s) * 2 * per_member
        first = block_of(base)

        for u in range(0, 2 * per_member, 2):
            rows = lefts[d, u : u + 2].reshape(2 * unit, lefts.shape[3])
            tile = dot_nn(rows, rights[d, block_of(base + u) - first]).astype(low)
            for i in range(2):
                which, row = (u + i) // per_member, (u + i) % per_member * unit
                chunk[d, lax.rem(s, slots), which, pl.ds(row, unit), :] = (
                    tile[i * unit : (i + 1) * unit])
        part_copy(d, s).start()
        prefetch()

    def final_of(q, d):
        return tail_own.at[d, n - 1] if q == pieces else chunk.at[d, (n - 1) % slots, core, span(q)]

    def spot_of(q, d, index, which):
        member = gather_at(d, index) * 2 + which
        if q == pieces:
            return t_ref.at[member, :, cols_of(d)]
        return o_ref.at[member, span(q), cols_of(d)]

    def gather_copy(q, d, index, first=False):
        src = final_of(q, d) if first else spot_of(q, d, index, core)
        return remote(
            src, spot_of(q, d, index, core),
            gather_send.at[d, q, index], gather_recv.at[d, q, index], {"wide": target[d]})

    def gather_landed(q, d, index):
        return remote(
            final_of(q, d), spot_of(q, d, index + 1, core),
            gather_send.at[d, q, index], gather_recv.at[d, q, index], {"wide": target[d]})

    def pair_copy(q, d, index, first=False):
        src = final_of(q, d) if first else spot_of(q, d, index, core)
        return remote(
            src, spot_of(q, d, index, core),
            pair_send.at[d, q, index], pair_recv.at[d, q, index], {"wide": other})

    def pair_landed(q, d, index):
        return remote(
            final_of(q, d), spot_of(q, d, index, 1 - core),
            pair_send.at[d, q, index], pair_recv.at[d, q, index], {"wide": other})

    def keep_copy(q, d):
        return pltpu.make_async_copy(final_of(q, d), spot_of(q, d, 0, core), keep_sem.at[d, q])

    def cross_copy(d, index, mine, first=False):
        member = gather_at(d, index) * 2 + (core if mine else 1 - core)
        src = final_of(pieces, d) if first else t_ref.at[member, :, cols_of(d)]
        lane = 0 if mine else 1
        return remote(
            src, e_ref.at[member, :, cols_of(d)],
            cross_send.at[d, lane, index], cross_recv.at[d, lane, index],
            {"section": 1 - section})

    def hand_over(q, d):
        gather_copy(q, d, 0, True).start()
        pair_copy(q, d, 0, True).start()
        keep_copy(q, d).start()
        if q == pieces:
            @pl.when(section == 0)
            def _():
                cross_copy(d, 0, True, True).start()

    def reduce_main(q, d, s, begin=False, end=False):
        if not begin:
            ring_copy(q, d, s - 1).wait_recv()

        def add(tile, carry):
            at = pl.ds(pl.multiple_of(spans[q][0] + tile * 16, 16), 16)
            slot = lax.rem(s, slots)
            total = chunk[d, slot, core, at].astype(f32) + part[d, s, at].astype(f32)
            if not begin:
                total = total + ring[d, s - 1, at].astype(f32)
            chunk[d, slot, core, at] = total.astype(low)
            return carry

        loop(spans[q][1] // 16, add, 6 if spans[q][1] % 96 == 0 else 1)
        if end:
            hand_over(q, d)
        else:
            ring_copy(q, d, s).start()

    def tail_part_copy(d, s):
        return remote(
            tails.at[reduce_at(d, s) * 2 + 1 - core, :, cols_of(d)], tail_part.at[d, s],
            part_send.at[d, n + s], part_recv.at[d, n + s], {"wide": other})

    def reduce_tail(d, s, begin=False, end=False):
        tail_part_copy(d, s).wait_recv()
        total = tails[reduce_at(d, s) * 2 + core, :, cols_of(d)].astype(f32)
        total = total + tail_part[d, s].astype(f32)
        if not begin:
            ring_copy(pieces, d, s - 1).wait_recv()
            total = total + tail_ring[d, s - 1].astype(f32)
        tail_own[d, s] = total.astype(low)
        if end:
            hand_over(pieces, d)
        else:
            ring_copy(pieces, d, s).start()

    feat_half = h_ref.shape[2]
    feat_keep = pltpu.make_async_copy(
        feat_grad.at[:, :, pl.ds(0, feat_half)], h_ref, feat_sem.at[0])
    feat_send = remote(
        feat_grad.at[:, :, pl.ds(feat_half, feat_half)], h_ref, feat_sem.at[1], feat_sem.at[2],
        {"section": 1 - section})

    def embed_back():
        first = (1 - section).astype(f32)
        small[...] = jnp.zeros_like(small)
        small[0:8, :] = small_in[...]
        for i in range(up_sums.shape[1] // width):
            small[8 + i : 9 + i, :] = up_sums[:, i * width : (i + 1) * width]
        lane = lax.broadcasted_iota(jnp.int32, (1, width), 1)
        row = jnp.zeros((1, width), f32)
        for i in range(3):
            row = jnp.where(lane == i, jnp.sum(stats[i : i + 1, :], axis=1, keepdims=True), row)
        count = jnp.zeros((1, 1), f32)
        for c in range(clips):
            count = count + jnp.sum(cols[c][:, 1:2], axis=0, keepdims=True)
        small[15:16, :] = jnp.where(lane == 3, count, row)
        embed[...] = jnp.zeros_like(embed)

        @pl.when(section == 0)
        def _():
            weight_sum = [jnp.zeros((feat_width, width), f32)] * 2
            place_sum = jnp.zeros((length, width), f32)
            for c in range(clips):
                grad = dx[c]
                kept = jnp.where(cols[c][:, 0:1] > 0.0, jnp.zeros_like(grad), grad)
                chosen = pick_kind(kinds[c], embw[0], embw[1]).astype(low)
                feat_grad[c] = dot_nt(kept, chosen).astype(low)
                second = kinds[c].astype(f32)
                flags = (1.0 - second, second)
                wide = dot_nn(feat[c].T, kept)
                sums = column_sum(kept.astype(f32))
                for kind in range(2):
                    weight_sum[kind] = weight_sum[kind] + flags[kind] * wide
                    small[12 + kind : 13 + kind, :] += flags[kind] * sums
                small[14:15, :] += column_sum(grad.astype(f32)) - sums
                place_sum = place_sum + grad.astype(f32)
            embed[0:feat_width, :] = weight_sum[0].astype(low)
            embed[feat_width : 2 * feat_width, :] = weight_sum[1].astype(low)
            embed[2 * feat_width :, :] = place_sum.astype(low)
            feat_keep.start()
            feat_send.start()

        embed_share = tail - SMALL
        for w in range(members):
            tails[w, 0:embed_share, :] = embed[w * embed_share : (w + 1) * embed_share, :]
            if w == 0:
                tails[w, embed_share:, :] = small[...].astype(low)
            else:
                tails[w, embed_share:, :] = jnp.zeros((SMALL, width), low)

    embed_loads = [
        pltpu.make_async_copy(src, dst, embed_sem.at[i])
        for i, (src, dst) in enumerate(((dx_h, dx), (feat_h, feat), (embw_h, embw)))
    ]

    for d in range(2):
        load_operands(d, 0)
    pl.semaphore_wait(barrier, jnp.where(section == 0, 4, 3))
    for d in range(2):
        products(d, 0, functools.partial(load_operands, d, 1))
        part_copy(d, 0).wait_recv()
        for q in range(pieces):
            reduce_main(q, d, 0, begin=True)
    for copy in embed_loads:
        copy.start()

    def prefetch_after(d, s):
        @pl.when(s < n)
        def _():
            load_operands(d, s)

    for d in range(2):
        products(d, 1, functools.partial(prefetch_after, d, 2))
    for copy in embed_loads:
        copy.wait()
    embed_back()

    def send_tails(s, carry):
        for d in range(2):
            tail_part_copy(d, s).start()
        return carry

    lax.fori_loop(0, n, send_tails, 0)

    def scatter_step(s, carry):
        for q in range(pieces):
            for d in range(2):
                if q == 0:
                    part_copy(d, s).wait_recv()
                reduce_main(q, d, s)

        for d in range(2):
            @pl.when(s > 1)
            def _():
                part_copy(d, s - 2).wait_send()
                for q in range(pieces):
                    ring_copy(q, d, s - 2).wait_send()

            products(d, s + 1, functools.partial(prefetch_after, d, s + 2))

        for d in range(2):
            @pl.when(s == 1)
            def _():
                reduce_tail(d, 0, begin=True)

            @pl.when(s > 1)
            def _():
                reduce_tail(d, s - 1)
        return carry

    lax.fori_loop(1, n - 1, scatter_step, 0)
    for q in range(pieces):
        for d in range(2):
            if q == 0:
                part_copy(d, n - 1).wait_recv()
            reduce_main(q, d, n - 1, end=True)
    for d in range(2):
        reduce_tail(d, n - 2, begin=n == 2)

    def gather_step(q, d, t):
        gather_landed(q, d, t).wait_recv()

        @pl.when(t < n - 2)
        def _():
            gather_copy(q, d, t + 1).start()

        pair_copy(q, d, t + 1).start()
        if q == pieces:
            @pl.when(section == 0)
            def _():
                cross_copy(d, t + 1, True).start()

    def pass_pair(d, t):
        pair_landed(pieces, d, t).wait_recv()

        @pl.when(section == 0)
        def _():
            cross_copy(d, t, False).start()

    for q, d in mains:
        gather_step(q, d, 0)
    for d in range(2):
        reduce_tail(d, n - 1, end=True)

    def spread(t, carry):
        for q, d in mains:
            gather_step(q, d, t)
        for d in range(2):
            gather_step(pieces, d, t - 1)
            pass_pair(d, t - 1)
        return carry

    lax.fori_loop(1, n - 1, spread, 0)
    for d in range(2):
        gather_step(pieces, d, n - 2)
        pass_pair(d, n - 2)
    for d in range(2):
        pass_pair(d, n - 1)

    @pl.when(section == 0)
    def _():
        feat_keep.wait()
        feat_send.wait_send()

    @pl.when(section == 1)
    def _():
        feat_send.wait_recv()

    for q, d in streams:
        keep_copy(q, d).wait()
    for d in range(2):
        for s in range(max(n - 3, 0), n):
            part_copy(d, s).wait_send()
        for s in range(max(n - 3, 0), n - 1):
            for q in range(pieces):
                ring_copy(q, d, s).wait_send()

    def finish(s, carry):
        for d in range(2):
            tail_part_copy(d, s).wait_send()
            for q in range(pieces + 1):
                pair_copy(q, d, s).wait_send()
                if q < pieces:
                    pair_landed(q, d, s).wait_recv()

            @pl.when(s < n - 1)
            def _():
                ring_copy(pieces, d, s).wait_send()
                for q in range(pieces + 1):
                    gather_copy(q, d, s).wait_send()

            for mine in (True, False):
                @pl.when(section == 0)
                def _():
                    cross_copy(d, s, mine).wait_send()

                @pl.when(section == 1)
                def _():
                    cross_copy(d, s, mine).wait_recv()
        return carry

    lax.fori_loop(0, n, finish, 0)


def finish_kernel(
    blocks, total, tails, cross, out_in, feat_in,
    out, feat, embed, places, attend, project, up, down, embed_vectors, gains, vectors, up_bias, rms,
    coming, going, ends, wide_ends, out_hold, feat_hold, in_sem, out_sem, ends_sem, plain_sem,
    embed_sem,
):
    members, share, width = total.shape
    section = lax.axis_index("section")
    tail = tails.shape[1]
    embed_share = tail - SMALL
    held = [(out_in, out_hold, out), (feat_in, feat_hold, feat)]
    plain_in = [
        pltpu.make_async_copy(src, hold, plain_sem.at[i]) for i, (src, hold, _) in enumerate(held)
    ]
    plain_out = [
        pltpu.make_async_copy(hold, dst, plain_sem.at[2 + i])
        for i, (_, hold, dst) in enumerate(held)
    ]
    slots, unit = coming.shape[:2]
    per_block, per_member = width // unit, share // unit
    count = members * per_member

    def in_copy(u):
        slot = lax.rem(u, slots)
        row = pl.multiple_of(lax.rem(u, per_member) * unit, 16)
        return pltpu.make_async_copy(
            total.at[u // per_member, pl.ds(row, unit)], coming.at[slot], in_sem.at[slot])

    def out_copy(u, dst, row, column):
        slot = lax.rem(u, slots)
        return pltpu.make_async_copy(
            going.at[slot],
            dst.at[pl.ds(pl.multiple_of(row, 16), unit), pl.ds(pl.multiple_of(column, 128), width)],
            out_sem.at[slot])

    own_ends = pltpu.make_async_copy(tails, ends.at[0], ends_sem.at[0])
    far_ends = pltpu.make_async_copy(cross, ends.at[1], ends_sem.at[1])
    for u in range(slots):
        in_copy(u).start()
    own_ends.start()
    far_ends.start()
    for copy in plain_in:
        copy.start()

    def step(u, carry):
        slot = lax.rem(u, slots)
        in_copy(u).wait()

        @pl.when(u >= slots)
        def _():
            out_copy(u, project, 0, 0).wait()

        going[slot] = coming[slot].astype(jnp.float32)
        block, row = u // per_block, lax.rem(u, per_block) * unit

        @pl.when(block < 3)
        def _():
            out_copy(u, attend, row, block * width).start()

        @pl.when(block == 3)
        def _():
            out_copy(u, project, row, 0).start()

        @pl.when((block > 3) & (block < 4 + blocks))
        def _():
            out_copy(u, up, row, (block - 4) * width).start()

        @pl.when(block > 3 + blocks)
        def _():
            out_copy(u, down, (u - (4 + blocks) * per_block) * unit, 0).start()

        @pl.when(u + slots < count)
        def _():
            in_copy(u + slots).start()

        return carry

    lax.fori_loop(0, count, step, 0)
    for copy in plain_in:
        copy.wait()
    for copy in plain_out:
        copy.start()
    own_ends.wait()
    far_ends.wait()
    small = ends[0, 0, embed_share:, :].astype(jnp.float32)
    gains[...] = small[0:2, :]
    for i in range(6):
        vectors[i] = small[2 + i : 3 + i, :]
    for i in range(blocks):
        up_bias[:, i * width : (i + 1) * width] = small[8 + i : 9 + i, :]
    stat = small[15:16, :]
    rms[...] = jnp.sqrt(stat[:, 0:3] / (stat[:, 3:4] * width))
    embed_vectors[...] = ends[section, 0, embed_share:, :].astype(jnp.float32)[12:15, :]

    def widen(w, carry):
        wide_ends[w] = ends[section, w, 0:embed_share, :].astype(jnp.float32)
        return carry

    lax.fori_loop(0, members, widen, 0)
    per_weight = embed.shape[0] // embed_share
    leave = []
    for w in range(members):
        at = w if w < per_weight else w - per_weight
        dst = embed if w < per_weight else places
        leave.append(pltpu.make_async_copy(
            wide_ends.at[w], dst.at[pl.ds(at * embed_share, embed_share)], embed_sem.at[w]))
    for copy in leave:
        copy.start()
    for copy in leave + plain_out:
        copy.wait()
    for u in range(count - slots, count):
        out_copy(u, project, 0, 0).wait()


ANY = pl.BlockSpec(memory_space=pl.ANY)
VMEM = pl.BlockSpec(memory_space=pltpu.VMEM)
SMEM = pl.BlockSpec(memory_space=pltpu.SMEM)
LOW = jnp.bfloat16
WIDE = jnp.float32
PIECES = 2


def shaped(kind, *dims):
    return jax.ShapeDtypeStruct(dims, kind)


def run_forward(features, masked, valid, kinds, embed_weight, embed_vectors, pos_embed, norm_gains,
                vectors, qkv_weight, out_weight, up_weight, up_bias, down_weight):
    clips, length, feat_width = features.shape
    width, feed = up_weight.shape[1:]
    blocks = feed // width
    dma = pltpu.SemaphoreType.DMA
    vm = pltpu.VMEM
    return pl.pallas_call(
        forward_kernel,
        out_shape=(
            shaped(LOW, 3 + blocks, clips * length, width),
            shaped(WIDE, clips, length, width),
            shaped(LOW, clips, length, 3 * width),
            shaped(LOW, clips, H, length, length),
            shaped(WIDE, clips, length, width),
            shaped(WIDE, clips, length, width),
            shaped(WIDE, clips, length, width),
            shaped(LOW, clips, length, feed),
            shaped(LOW, clips, length, width // 2),
            shaped(WIDE, clips, length, 128),
            shaped(WIDE, 8, width),
        ),
        in_specs=[SMEM] + [ANY] * 13,
        out_specs=(ANY,) * 9 + (VMEM,) * 2,
        scratch_shapes=[
            vm(features.shape, LOW), vm(masked.shape, jnp.int32), vm(valid.shape, jnp.int32),
            vm(embed_weight.shape, LOW), vm(embed_vectors.shape, WIDE), vm(pos_embed.shape, WIDE),
            vm(norm_gains.shape[1:], WIDE), vm(vectors.shape, WIDE),
            vm((width, 3 * width), LOW), vm((width, width), LOW), vm((width, feed), LOW),
            vm(up_bias.shape, WIDE), vm((feed, width), LOW),
            vm((feat_width, width), LOW), vm((length, 128), LOW), vm((length, width), WIDE),
            vm((length, width), WIDE),
            vm((length, width), WIDE), vm((length, width), LOW), vm((length, 3 * width), LOW),
            vm((2, 2, length, length), LOW), vm((length, width), LOW), vm((length, width), WIDE),
            vm((length, width), LOW), vm((length, feed), LOW), vm((length, feed), LOW),
            vm((clips, length, width), LOW), vm((clips, length, width), LOW),
            dma((13,)), dma((9 + blocks,)), dma((2,)), dma((clips, 2)), dma((clips, 2)),
            dma((clips, 2)), dma((clips, 2)), dma((clips, 2)),
        ],
        compiler_params=pltpu.CompilerParams(
            collective_id=1, has_side_effects=True, vmem_limit_bytes=56 * 2**20
        ),
    )(kinds, features, masked, valid, embed_weight, embed_vectors, pos_embed, norm_gains, vectors,
      qkv_weight, out_weight, up_weight, up_bias, down_weight)


def run_backward(cotangent, weights, x, qkv, probs, inverse, exact, middle, slope, left, gains):
    clips, length, width = cotangent.shape
    feed = weights[2].shape[2]
    blocks = feed // width
    dma = pltpu.SemaphoreType.DMA
    vm = pltpu.VMEM
    return pl.pallas_call(
        backward_kernel,
        out_shape=(
            shaped(LOW, 5 + blocks, clips * length, width),
            shaped(LOW, clips, length, width),
            shaped(LOW, left.shape[0], width, clips * length),
            shaped(WIDE, 8, width),
            shaped(WIDE, 1, feed),
        ),
        in_specs=[ANY] * 14,
        out_specs=(ANY, ANY, ANY, VMEM, VMEM),
        scratch_shapes=[
            vm((width, 3 * width), LOW), vm((width, width), LOW), vm((width, feed), LOW),
            vm((feed, width), LOW), vm(gains.shape[1:], WIDE),
            vm((clips, length, width), WIDE), vm((clips, length, 3 * width), LOW),
            vm((2, 2, length, length), LOW), vm((clips, length, width), WIDE),
            vm((clips, length, width), WIDE), vm((clips, length, width), WIDE),
            vm((clips, length, feed), LOW), vm((clips, length, width), LOW),
            vm((length, feed), LOW), vm((length, width), WIDE), vm((length, width), WIDE),
            vm((length, width), LOW), vm((length, width), LOW), vm((length, 3 * width), LOW),
            vm((clips, length, width), LOW),
            vm((clips * length, width), LOW), vm((width, clips * length), LOW),
            dma((2,)), dma((5,)), dma((clips, 7)), dma((3,)), dma((5 + blocks,)), dma((clips,)),
            dma((clips, 2)), dma((clips, 2)),
        ],
        compiler_params=pltpu.CompilerParams(
            collective_id=2, has_side_effects=True, vmem_limit_bytes=62 * 2**20
        ),
    )(cotangent, *weights, x, qkv, probs, inverse, exact, middle, slope, left, gains)


def run_sums(members, kinds, turned, right, dx, features, embed_weight, cols, small, up_sums, stats):
    width, rows = turned.shape[1:]
    clips, length, feat_width = features.shape
    n = members // 2
    share = 12 * width // members
    embed_rows = 2 * feat_width + length
    tail = embed_rows // members + SMALL
    unit = unit_rows(members, width)
    per_member = share // unit
    half = width // 2
    dma = pltpu.SemaphoreType.DMA
    vm = pltpu.VMEM
    sems = [dma((2, 2 * per_member + 2)), dma((3,)), dma((2, 2 * n)), dma((2, 2 * n))]
    sems += [dma((2, PIECES + 1, n)) for _ in range(6)]
    sems += [dma((2, PIECES + 1)), dma((2, 2, n)), dma((2, 2, n)), dma((3,))]
    return pl.pallas_call(
        functools.partial(sums_kernel, members),
        out_shape=(
            shaped(LOW, members, share, width),
            shaped(LOW, members, tail, width),
            shaped(LOW, members, tail, width),
            shaped(LOW, clips, length, feat_width // 2),
        ),
        in_specs=[SMEM] + [ANY] * 5 + [VMEM] * 4,
        out_specs=(ANY,) * 4,
        scratch_shapes=[
            vm((2, 2 * per_member, unit, rows), LOW), vm((2, 2, rows, half), LOW),
            vm((2, 3, 2, share, half), LOW),
            vm((2, n, share, half), LOW), vm((2, n - 1, share, half), LOW),
            vm((members, tail, width), LOW), vm((2, n, tail, half), LOW),
            vm((2, n, tail, half), LOW), vm((2, n - 1, tail, half), LOW),
            vm((clips, length, width), LOW), vm(features.shape, LOW), vm(embed_weight.shape, LOW),
            vm(features.shape, LOW), vm((embed_rows, width), LOW), vm((SMALL, width), WIDE),
            sems,
        ],
        compiler_params=pltpu.CompilerParams(
            collective_id=0, has_side_effects=True, vmem_limit_bytes=60 * 2**20
        ),
    )(kinds, turned, right, dx, features, embed_weight, cols, small, up_sums, stats)


def run_finish(total, tails, cross, output, feature_out, feed, feat_width):
    members, share, width = total.shape
    unit = unit_rows(members, width)
    blocks = feed // width
    embed_share = tails.shape[1] - SMALL
    places = members * embed_share - 2 * feat_width
    slots = 12
    dma = pltpu.SemaphoreType.DMA
    vm = pltpu.VMEM
    return pl.pallas_call(
        functools.partial(finish_kernel, blocks),
        out_shape=(
            shaped(LOW, *output.shape), shaped(LOW, *feature_out.shape),
            shaped(WIDE, 2 * feat_width, width), shaped(WIDE, places, width),
            shaped(WIDE, width, 3 * width), shaped(WIDE, width, width),
            shaped(WIDE, width, feed), shaped(WIDE, feed, width),
            shaped(WIDE, 3, width), shaped(WIDE, 2, width), shaped(WIDE, 6, 1, width),
            shaped(WIDE, 1, feed), shaped(WIDE, 1, 3),
        ),
        in_specs=[ANY] * 5,
        out_specs=(ANY,) * 8 + (VMEM,) * 5,
        scratch_shapes=[
            vm((slots, unit, width), LOW), vm((slots, unit, width), WIDE),
            vm((2, *tails.shape), LOW), vm((members, embed_share, width), WIDE),
            vm(output.shape, LOW), vm(feature_out.shape, LOW),
            dma((slots,)), dma((slots,)), dma((2,)), dma((4,)), dma((members,)),
        ],
        compiler_params=pltpu.CompilerParams(vmem_limit_bytes=56 * 2**20),
    )(total, tails, cross, output, feature_out)


def local(
    features,
    masked,
    valid,
    kinds,
    embed_weight,
    embed_vectors,
    pos_embed,
    norm_gains,
    vectors,
    qkv_weight,
    out_weight,
    up_weight,
    up_bias,
    down_weight,
    cotangent,
):
    members = lax.axis_size("wide")
    clips, length, feat_width = features.shape
    width = pos_embed.shape[1]
    feed = up_weight.shape[2]
    left, x, qkv, probs, inverse, exact, middle, slope, output, cols, stats = run_forward(
        features, masked, valid, kinds, embed_weight, embed_vectors, pos_embed, norm_gains,
        vectors.transpose(1, 0, 2), qkv_weight, out_weight, up_weight, up_bias, down_weight)
    weights = (qkv_weight, out_weight, up_weight, down_weight)
    right, dx, turned, small, up_sums = run_backward(
        cotangent, weights, x, qkv, probs, inverse, exact, middle, slope, left, norm_gains)
    total, tails, cross, feature_out = run_sums(
        members, kinds, turned, right, dx, features, embed_weight, cols, small, up_sums, stats)
    (output, feature_out, embed, places, attend, project, up, down, embed_rows, gain_rows,
     vector_rows, up_rows, rms) = run_finish(
        total, tails, cross, output, feature_out, feed, feat_width)
    return (
        output,
        feature_out,
        embed.reshape(2, feat_width, width),
        embed_rows,
        places,
        gain_rows[None],
        vector_rows.transpose(1, 0, 2),
        attend[None],
        project[None],
        up[None],
        up_rows,
        down[None],
        rms,
    )


def solution(mesh):
    return jax.shard_map(
        local,
        mesh=mesh,
        in_specs=(
            P("wide", None, None),
            P("wide", None),
            P("wide", None),
            P("wide"),
            P(),
            P(),
            P(),
            P("section", None, None),
            P("section", None, None),
            P("section", None, None),
            P("section", None, None),
            P("section", None, None),
            P("section", None),
            P("section", None, None),
            P("wide", None, None),
        ),
        out_specs=(
            P("wide", None, "section"),
            P("wide", None, "section"),
            P(),
            P(),
            P(),
            P("section", None, None),
            P("section", None, None),
            P("section", None, None),
            P("section", None, None),
            P("section", None, None),
            P("section", None),
            P("section", None, None),
            P("section", None),
        ),
        check_vma=False,
    )
```
